32 devices in a mesh: req: 16 (over z, y, x), seq: 2 (over core).
Axes of the slice: x: 2, y: 2, z: 4, core: 2. Of those that a mesh axis runs over, the one named last changes fastest.
Arguments:
- tokens: bfloat16 [4096, 1536], P(('req', 'seq')), may hold values from -6 to 6
- attn_gain: float32 [1536], replicated, may hold values from 0.5 to 1.5
- w_qkv: bfloat16 [1536, 2560], replicated, may hold values from -80 to 80
- w_out: bfloat16 [1536, 1536], replicated, may hold values from -0.15625 to 0.15625
- k_cache: bfloat16 [16, 2048, 512], P('req', 'seq'), may hold values from -6 to 6
- v_cache: bfloat16 [16, 2048, 512], P('req', 'seq'), may hold values from -7.5 to 7.5
- cache_len: int32 [16], P('req'), may hold values from 1 to 2048, as said below
- ffn_gain: float32 [1536], replicated, may hold values from 0.5 to 1.5
- routes: int32 [4096, 8], P(('req', 'seq')), may hold values from 0 to 39, as said below
- route_scores: float32 [4096, 8], P(('req', 'seq')), may hold values from 0.05 to 1
- replica_slot: int32 [4096, 40], P(('req', 'seq')), may hold values from 0 to 63, as said below
- expert_up: bfloat16 [64, 1536, 1024], P(('req', 'seq')), may hold values from -2 to 2, as said below
- expert_down: bfloat16 [64, 512, 1536], P(('req', 'seq')), may hold values from -2 to 2, as said below
Outputs:
- attended: bfloat16 [4096, 1536], P(('req', 'seq'))
- stream: bfloat16 [4096, 1536], P(('req', 'seq'))
- expert_mix: bfloat16 [4096, 1536], P(('req', 'seq'))
- appended: bfloat16 [4096, 1024], P(('req', 'seq'))
The draws below stay inside these ranges and needn't reach their ends.
Inputs may be any that keep to these rules, and one draw needn't show every extreme that they name: `routes`: each token names 8 different experts. Each slot hosts one expert, every expert at least one slot; replica_slot[t, e] is a slot hosting expert e. The 128 rows of one device (rows d * 128 to (d + 1) * 128 - 1) send at most 32 of their routes to any one slot (slot replica_slot[t, routes[t, k]]), and each device sends exactly 32 to some slot. `expert_up`: slots hosting the same expert hold equal weights. `expert_down`: slots hosting the same expert hold equal weights. `cache_len`: at least one request has exactly 2048 cached positions.
All inputs are finite; a program needn't handle non-finite values.
Results may differ from the reference program's by a relative error of at most 0.01.
Values may be sent and summed in bfloat16 or wider, within the bound.
No kernel may reach another device: no remote copies, remote signals or barrier semaphores. Data moves between devices by JAX's collectives and lax.ppermute only.
A program may use at most 128 MiB of HBM per device.

```python
import math
import jax
import jax.numpy as jnp
from jax import lax

D = 1536
HEADS = 24
KV_HEADS = 8
HEAD = 64
EXPERTS = 40
FF = 512
TOP = 8
KEY_BLOCK = 128
SPAN_DEV = 128
SPAN = 256
CACHE = 2048
REQS = 16
TOKENS = 4096
SLOTS = 64
CAP = 32
N_REQ = 16
N_SEQ = 2


def slot_hosts(key):
    route_order = jax.random.permutation(jax.random.fold_in(key, 101), SLOTS).astype(jnp.int32)
    hosted = jnp.zeros((SLOTS,), jnp.int32).at[route_order].set(jnp.arange(SLOTS, dtype=jnp.int32) % EXPERTS)
    return (route_order, hosted)


def route_plan(key):
    route_order, hosted = slot_hosts(key)
    total = SPAN_DEV * TOP
    mean_load = (total + SLOTS - 1) // SLOTS
    sorted_slots = jnp.argsort(hosted * SLOTS + jnp.arange(SLOTS, dtype=jnp.int32)).astype(jnp.int32)

    def one_device(device):
        device_key = jax.random.fold_in(jax.random.fold_in(key, 141), device)
        visit = jax.random.permutation(jax.random.fold_in(device_key, 1), SLOTS).astype(jnp.int32)
        wanted = jax.random.randint(jax.random.fold_in(device_key, 2), (SLOTS,), mean_load, CAP + 1).astype(jnp.int32)
        wanted = wanted.at[0].set(CAP)
        before_load = jnp.cumsum(wanted).astype(jnp.int32) - wanted
        kept_load = jnp.clip(total - before_load, 0, wanted).astype(jnp.int32)
        load = jnp.zeros((SLOTS,), jnp.int32).at[visit].set(kept_load)
        ends = jnp.cumsum(load[sorted_slots]).astype(jnp.int32)
        entry = jnp.arange(total, dtype=jnp.int32)
        where_at = jnp.searchsorted(ends, entry, side='right').astype(jnp.int32)
        slot_rows = sorted_slots[where_at].reshape(TOP, SPAN_DEV).T
        shuffle = jax.random.permutation(jax.random.fold_in(device_key, 3), SPAN_DEV).astype(jnp.int32)
        return slot_rows[shuffle]
    chosen_slots = jax.vmap(one_device)(jnp.arange(N_REQ * N_SEQ, dtype=jnp.int32)).reshape(TOKENS, TOP)
    return (route_order, hosted, chosen_slots.astype(jnp.int32))


def draw_routes(key, part):
    route_order, hosted, chosen_slots = route_plan(key)
    return hosted[chosen_slots].astype(jnp.int32)


def draw_replica_slot(key, part):
    route_order, hosted, chosen_slots = route_plan(key)
    routes = hosted[chosen_slots].astype(jnp.int32)
    experts = jnp.arange(EXPERTS, dtype=jnp.int32)
    copies = (SLOTS - experts + EXPERTS - 1) // EXPERTS
    picked = jax.random.randint(jax.random.fold_in(key, 102), (TOKENS, EXPERTS), 0, 1 << 20) % copies[None, :]
    table = route_order[experts[None, :] + picked * EXPERTS].astype(jnp.int32)
    row_ids = jnp.arange(TOKENS, dtype=jnp.int32)[:, None]
    return table.at[row_ids, routes].set(chosen_slots).astype(jnp.int32)


def expert_table(key, salt_tag, row_count, col_count):
    route_order, hosted = slot_hosts(key)
    base_key = jax.random.fold_in(key, salt_tag)

    def draw_single(expert):
        expert_key = jax.random.fold_in(base_key, expert)
        return jnp.clip(jax.random.normal(expert_key, (row_count, col_count), jnp.float32), -6.0, 6.0)
    return jax.vmap(draw_single)(hosted) * row_count ** (-0.5)


def draw_expert_up(key, part):
    return expert_table(key, 103, D, 2 * FF).astype(jnp.bfloat16)


def draw_expert_down(key, part):
    return expert_table(key, 104, FF, D).astype(jnp.bfloat16)


def draw_w_qkv(key, part):
    col_count = (HEADS + 2 * KV_HEADS) * HEAD
    base_draw = jnp.clip(jax.random.normal(jax.random.fold_in(key, 111), (D, col_count), jnp.float32), -6.0, 6.0) * D ** (-0.5)
    return base_draw.astype(jnp.bfloat16)


def draw_cache_len(key, part):
    lengths = jax.random.randint(jax.random.fold_in(key, 121), (REQS,), 1, CACHE + 1)
    full_request = jax.random.randint(jax.random.fold_in(key, 122), (), 0, REQS)
    return jnp.where(jnp.arange(REQS) == full_request, CACHE, lengths).astype(jnp.int32)


def draw_v_cache(key, part):
    row_width = KV_HEADS * HEAD
    noise_part = jnp.clip(jax.random.normal(jax.random.fold_in(key, 131), (REQS, CACHE // 16, 16, row_width), jnp.float32), -6.0, 6.0)
    regions = jax.random.uniform(jax.random.fold_in(key, 132), (REQS, CACHE // 16, 1, row_width), jnp.float32, -1.5, 1.5)
    return (noise_part + regions).reshape(REQS, CACHE, row_width).astype(jnp.bfloat16)


def shard_levels(rng, dims, pieces, low, largest):
    loudness, own = 1.0, jax.random.fold_in(rng, 6)
    for axis_at, parts in pieces:
        steps = jnp.exp(jax.random.uniform(jax.random.fold_in(own, axis_at), (parts,), jnp.float32, low / len(pieces), largest / len(pieces)))
        loudness = loudness * jnp.repeat(steps, dims[axis_at] // parts).reshape([-1 if axis == axis_at else 1 for axis in range(len(dims))])
    return loudness


def centred(own_key, extent, scale, reach, split=(), held_as=jnp.bfloat16):
    entries = jax.random.normal(own_key, extent, jnp.float32) * scale
    if len(split) > 0:
        entries = shard_levels(own_key, extent, split, -0.22, 0.18) * entries
    return jnp.clip(entries, min=-reach, max=reach).astype(held_as)


def setup_inputs(seed: int = 0) -> dict:
    key_list = jax.random.split(jax.random.key(seed), 14)
    return {
        "tokens": centred(key_list[0], (TOKENS, D), 1.0, 6.0, ((0, 32),)),
        "attn_gain": jnp.clip(1.0 + 0.1 * jax.random.normal(key_list[1], (D,), jnp.float32), 0.5, 1.5),
        "w_qkv": draw_w_qkv(jax.random.fold_in(key_list[13], 71), 0),
        "w_out": centred(key_list[3], (HEADS * HEAD, D), (HEADS * HEAD) ** -0.5, 0.15625),
        "k_cache": centred(key_list[4], (REQS, CACHE, KV_HEADS * HEAD), 1.0, 6.0, ((0, 16), (1, 2))),
        "v_cache": draw_v_cache(jax.random.fold_in(key_list[13], 71), 0),
        "cache_len": draw_cache_len(jax.random.fold_in(key_list[13], 71), 0),
        "ffn_gain": jnp.clip(1.0 + 0.1 * jax.random.normal(key_list[7], (D,), jnp.float32), 0.5, 1.5),
        "routes": draw_routes(jax.random.fold_in(key_list[13], 71), 0),
        "route_scores": jnp.clip(jnp.exp(math.log(1.0) - 2.9957323 * jax.random.uniform(key_list[9], (TOKENS, TOP), jnp.float32) ** shard_levels(key_list[9], (TOKENS, TOP), ((0, 32),), -0.2, 0.2)), 0.05, 1.0),
        "replica_slot": draw_replica_slot(jax.random.fold_in(key_list[13], 71), 0),
        "expert_up": draw_expert_up(jax.random.fold_in(key_list[13], 71), 0),
        "expert_down": draw_expert_down(jax.random.fold_in(key_list[13], 71), 0),
    }


epsilon = 1e-06
residual_scale = 0.22
score_scale = 0.015625
rope_base = 10000.0
neg_big = -1e+30

def rms_scale(row_block, gain_vector):
    widened = row_block.astype(jnp.float32)
    mean_square = lax.optimization_barrier(jnp.mean(widened * widened, axis=-1, keepdims=True))
    return (widened * lax.rsqrt(mean_square + epsilon) * gain_vector).astype(jnp.bfloat16)

def rotate(head_values, positions):
    half_width = head_values.shape[-1] // 2
    frequency = rope_base ** (-jnp.arange(half_width, dtype=jnp.float32) / half_width)
    angles = positions.astype(jnp.float32)[:, None] * frequency[None, :]
    cosine = jnp.cos(angles)[:, None, :]
    sine_part = jnp.sin(angles)[:, None, :]
    lower_half = head_values[..., :half_width]
    upper_half = head_values[..., half_width:]
    return jnp.concatenate([lower_half * cosine - upper_half * sine_part, upper_half * cosine + lower_half * sine_part], axis=-1)

def project(row_block, gain_vector, w_qkv, positions):
    normed = rms_scale(row_block, gain_vector)
    projected = jnp.dot(normed, w_qkv, preferred_element_type=jnp.float32)
    query_width = HEADS * HEAD
    key_width = KV_HEADS * HEAD
    queries = rotate(projected[:, :query_width].reshape(-1, HEADS, HEAD), positions).astype(jnp.bfloat16)
    new_keys = rotate(projected[:, query_width:query_width + key_width].reshape(-1, KV_HEADS, HEAD), positions).astype(jnp.bfloat16)
    new_values = projected[:, query_width + key_width:].astype(jnp.bfloat16)
    return (queries, new_keys, new_values)

def request_attention(inputs):
    queries, new_keys, new_values, cache_keys, cache_values, length = inputs
    group_size = HEADS // KV_HEADS
    grouped = queries.reshape(SPAN, KV_HEADS, group_size, HEAD).astype(jnp.float32)
    all_keys = jnp.concatenate([cache_keys.reshape(CACHE, KV_HEADS, HEAD), new_keys], axis=0)
    all_values = jnp.concatenate([cache_values.reshape(CACHE, KV_HEADS, HEAD), new_values.reshape(SPAN, KV_HEADS, HEAD)], axis=0)
    query_index = jnp.arange(SPAN, dtype=jnp.int32)

    def fold_step(carried, block_index):
        best_score, running_total, running_sum = carried
        start = (block_index * KEY_BLOCK).astype(jnp.int32)
        key_part = lax.dynamic_slice_in_dim(all_keys, start, KEY_BLOCK, 0).astype(jnp.float32)
        value_part = lax.dynamic_slice_in_dim(all_values, start, KEY_BLOCK, 0).astype(jnp.float32)
        key_index = start + jnp.arange(KEY_BLOCK, dtype=jnp.int32)
        cached = (key_index < CACHE) & (key_index < length)
        in_span = (key_index >= CACHE)[None, :] & ((key_index - CACHE)[None, :] <= query_index[:, None])
        visible = (cached[None, :] | in_span)[:, None, None, :]
        scores = jnp.einsum('rkgh,bkh->rkgb', grouped, key_part) * score_scale
        block_max = lax.optimization_barrier(jnp.max(jnp.where(visible, scores, neg_big), axis=-1))
        weights = jnp.where(visible, jnp.exp(scores - block_max[..., None]), 0.0).astype(jnp.bfloat16)
        weights = lax.optimization_barrier(weights).astype(jnp.float32)
        block_total = lax.optimization_barrier(jnp.sum(weights, axis=-1))
        block_sum = jnp.einsum('rkgb,bkh->rkgh', weights, value_part)
        new_best = jnp.maximum(best_score, block_max)
        old_scale = jnp.exp(best_score - new_best)
        block_scale = jnp.exp(block_max - new_best)
        running_total = running_total * old_scale + block_total * block_scale
        running_sum = running_sum * old_scale[..., None] + block_sum * block_scale[..., None]
        return ((new_best, running_total, running_sum), None)
    initial = (jnp.full((SPAN, KV_HEADS, group_size), neg_big, jnp.float32), jnp.zeros((SPAN, KV_HEADS, group_size), jnp.float32), jnp.zeros((SPAN, KV_HEADS, group_size, HEAD), jnp.float32))
    block_count = (CACHE + SPAN) // KEY_BLOCK
    (best_score, running_total, running_sum), _ = lax.scan(fold_step, initial, jnp.arange(block_count, dtype=jnp.int32))
    return (running_sum / running_total[..., None]).astype(jnp.bfloat16).reshape(SPAN, HEADS * HEAD)

def mix_experts(expert_in, routes, route_scores, replica_slot, expert_up, expert_down):
    device_count = N_REQ * N_SEQ
    route_count = SPAN_DEV * TOP
    sentinel = TOKENS * TOP
    slot_of = jnp.take_along_axis(replica_slot, routes, axis=1).astype(jnp.int32)
    by_source = slot_of.reshape(device_count, route_count)
    onehot = (by_source[:, :, None] == jnp.arange(SLOTS, dtype=jnp.int32)[None, None, :]).astype(jnp.int32)
    slot_rank = lax.optimization_barrier(jnp.sum((jnp.cumsum(onehot, axis=1) - onehot) * onehot, axis=2)).astype(jnp.int32)
    route_ids = jnp.arange(sentinel, dtype=jnp.int32).reshape(device_count, route_count)
    device_ids = jnp.arange(device_count, dtype=jnp.int32)[:, None]
    slot_table = jnp.full((device_count, SLOTS, CAP), sentinel, jnp.int32).at[device_ids, by_source, slot_rank].set(route_ids)
    shares = (route_scores / lax.optimization_barrier(jnp.sum(route_scores, axis=1, keepdims=True))).reshape(-1)

    def slot_step(mixed_sum, slot_index):
        slot_routes = lax.dynamic_index_in_dim(slot_table, slot_index, 1, keepdims=False).reshape(-1)
        live_rows = slot_routes < sentinel
        token_index = jnp.where(live_rows, slot_routes // TOP, 0).astype(jnp.int32)
        gathered = expert_in[token_index].astype(jnp.float32) * live_rows[:, None].astype(jnp.float32)
        up_weight = lax.dynamic_index_in_dim(expert_up, slot_index, 0, keepdims=False).astype(jnp.float32)
        down_weight = lax.dynamic_index_in_dim(expert_down, slot_index, 0, keepdims=False).astype(jnp.float32)
        gate_up = jnp.dot(gathered, up_weight, precision=lax.Precision.HIGHEST)
        active = (jax.nn.silu(gate_up[:, :FF]) * gate_up[:, FF:]).astype(jnp.bfloat16)
        active = lax.optimization_barrier(active).astype(jnp.float32)
        outputs = jnp.dot(active, down_weight, precision=lax.Precision.HIGHEST).astype(jnp.bfloat16)
        outputs = lax.optimization_barrier(outputs).astype(jnp.float32)
        route_share = jnp.where(live_rows, shares[jnp.where(live_rows, slot_routes, 0)], 0.0)
        target = jnp.where(live_rows, token_index, TOKENS).astype(jnp.int32)
        mixed_sum = mixed_sum.at[target].add(outputs * route_share[:, None], mode='drop')
        return (mixed_sum, None)
    mixed_sum, _ = lax.scan(slot_step, jnp.zeros((TOKENS, D), jnp.float32), jnp.arange(SLOTS, dtype=jnp.int32))
    return mixed_sum.astype(jnp.bfloat16)

def reference(tokens, attn_gain, w_qkv, w_out, k_cache, v_cache, cache_len, ffn_gain, routes, route_scores, replica_slot, expert_up, expert_down):
    positions = (cache_len[:, None] + jnp.arange(SPAN, dtype=jnp.int32)[None, :]).reshape(-1).astype(jnp.int32)
    queries, new_keys, new_values = project(tokens, attn_gain, w_qkv, positions)
    appended = jnp.concatenate([new_keys.reshape(TOKENS, -1), new_values], axis=1)
    attended = lax.map(request_attention, (queries.reshape(REQS, SPAN, HEADS, HEAD), new_keys.reshape(REQS, SPAN, KV_HEADS, HEAD), new_values.reshape(REQS, SPAN, KV_HEADS * HEAD), k_cache, v_cache, cache_len)).reshape(TOKENS, HEADS * HEAD)
    stream = (tokens.astype(jnp.float32) + residual_scale * jnp.dot(attended, w_out, preferred_element_type=jnp.float32)).astype(jnp.bfloat16)
    expert_in = rms_scale(stream, ffn_gain)
    expert_mix = mix_experts(expert_in, routes, route_scores, replica_slot, expert_up, expert_down)
    return (attended, stream, expert_mix, appended)
```

```python
import jax
import jax.numpy as jnp
from jax import lax
from jax.sharding import PartitionSpec as P

HEADS = 24
KV_HEADS = 8
HEAD = 64
KEY_BLOCK = 128


epsilon = 1e-06
residual_scale = 0.22
score_scale = 0.015625
rope_base = 10000.0
neg_big = -1e30


def rms_scale(row_block, gain_vector):
    widened = row_block.astype(jnp.float32)
    mean_square = jnp.mean(widened * widened, axis=-1, keepdims=True)
    return (widened * lax.rsqrt(mean_square + epsilon) * gain_vector).astype(jnp.bfloat16)


def rotate(head_values, positions):
    half_width = head_values.shape[-1] // 2
    frequency = rope_base ** (-jnp.arange(half_width, dtype=jnp.float32) / half_width)
    angles = positions.astype(jnp.float32)[:, None] * frequency[None, :]
    cosine = jnp.cos(angles)[:, None, :]
    sine_part = jnp.sin(angles)[:, None, :]
    lower_half = head_values[..., :half_width]
    upper_half = head_values[..., half_width:]
    return jnp.concatenate(
        [
            lower_half * cosine - upper_half * sine_part,
            upper_half * cosine + lower_half * sine_part,
        ],
        axis=-1,
    )


def project(row_block, gain_vector, w_qkv, positions):
    normed = rms_scale(row_block, gain_vector)
    projected = jnp.dot(normed, w_qkv, preferred_element_type=jnp.float32)
    query_width = HEADS * HEAD
    key_width = KV_HEADS * HEAD
    queries = rotate(projected[:, :query_width].reshape(-1, HEADS, HEAD), positions).astype(
        jnp.bfloat16
    )
    new_keys = rotate(
        projected[:, query_width : query_width + key_width].reshape(-1, KV_HEADS, HEAD), positions
    ).astype(jnp.bfloat16)
    new_values = projected[:, query_width + key_width :].astype(jnp.bfloat16)
    return (queries, new_keys, new_values)


def fold_blocks(carried, queries, key_part, value_part, visible):
    scores = (
        jnp.einsum("rkgh,nbkh->rkgnb", queries, key_part, preferred_element_type=jnp.float32)
        * score_scale
    )
    visible_mask = visible[:, None, None, :, :]
    block_max = jnp.max(jnp.where(visible_mask, scores, neg_big), axis=-1)
    weights = jnp.where(visible_mask, jnp.exp(scores - block_max[..., None]), 0.0).astype(
        jnp.bfloat16
    )
    totals = jnp.sum(weights, axis=-1, dtype=jnp.float32)
    block_sums = jnp.einsum(
        "rkgnb,nbkh->rkgnh", weights, value_part, preferred_element_type=jnp.float32
    )
    best_score, running_total, running_sum = carried
    new_best = jnp.maximum(best_score, jnp.max(block_max, axis=-1))
    old_scale = jnp.exp(best_score - new_best)
    block_scale = jnp.exp(block_max - new_best[..., None])
    running_total = running_total * old_scale + jnp.sum(totals * block_scale, axis=-1)
    running_sum = running_sum * old_scale[..., None] + jnp.sum(
        block_sums * block_scale[..., None], axis=-2
    )
    return (new_best, running_total, running_sum)


def attend_keys(carried, queries, key_rows, value_rows, visible_of):
    block_count = key_rows.shape[0] // KEY_BLOCK
    group_size = 1
    while group_size * 2 * queries.shape[0] <= 1024 and block_count % (group_size * 2) == 0:
        group_size = group_size * 2
    turn_count = block_count // group_size
    shaped_keys = key_rows.reshape(turn_count, group_size, KEY_BLOCK, KV_HEADS, HEAD)
    shaped_values = value_rows.reshape(turn_count, group_size, KEY_BLOCK, KV_HEADS, HEAD)

    def fold_step(running, inputs):
        turn_index, key_part, value_part = inputs
        visible = visible_of(turn_index * group_size * KEY_BLOCK, group_size * KEY_BLOCK)
        visible = visible.reshape(-1, group_size, KEY_BLOCK)
        return (fold_blocks(running, queries, key_part, value_part, visible), None)

    carried, _ = lax.scan(
        fold_step, carried, (jnp.arange(turn_count, dtype=jnp.int32), shaped_keys, shaped_values)
    )
    return carried


def empty_state(row_count):
    group_size = HEADS // KV_HEADS
    return (
        jnp.full((row_count, KV_HEADS, group_size), neg_big, jnp.float32),
        jnp.zeros((row_count, KV_HEADS, group_size), jnp.float32),
        jnp.zeros((row_count, KV_HEADS, group_size, HEAD), jnp.float32),
    )


def flatten_state(carried):
    best_score, running_total, running_sum = carried
    row_count = best_score.shape[0]
    return (
        best_score.reshape(row_count, HEADS),
        running_total.reshape(row_count, HEADS),
        running_sum.reshape(row_count, HEADS * HEAD),
    )


def finish_state(flat_state):
    best_score, running_total, running_sum = flat_state
    row_count = best_score.shape[0]
    shaped = running_sum.reshape(row_count, HEADS, HEAD) / running_total[..., None]
    return shaped.astype(jnp.bfloat16).reshape(row_count, HEADS * HEAD)


def route_tables(routes, route_scores, replica_slot, slot_total):
    row_count = routes.shape[0]
    experts = jnp.arange(replica_slot.shape[1], dtype=jnp.int32)
    slot_ids = jnp.sum(
        jnp.where(routes[:, :, None] == experts, replica_slot[:, None, :], 0), axis=2
    )
    shares = route_scores / jnp.sum(route_scores, axis=1, keepdims=True)
    slots = jnp.arange(slot_total, dtype=jnp.int32)[:, None, None]
    hot = slot_ids[None] == slots
    share_of = jnp.sum(jnp.where(hot, shares[None], 0.0), axis=2)
    here = jnp.any(hot, axis=2).astype(jnp.bfloat16)
    order = jnp.arange(row_count, dtype=jnp.int32)
    earlier = (order[:, None] < order[None, :]).astype(jnp.bfloat16)
    rank = jnp.dot(here, earlier, preferred_element_type=jnp.float32)
    rank = jnp.where(here > 0, rank, -1.0)
    return rank, share_of


def shards(
    tokens,
    attn_gain,
    w_qkv,
    w_out,
    k_cache,
    v_cache,
    cache_len,
    ffn_gain,
    routes,
    route_scores,
    replica_slot,
    expert_up,
    expert_down,
):
    row_count = tokens.shape[0]
    seq_count = lax.axis_size("seq")
    seq_index = lax.axis_index("seq")
    length = cache_len[0]
    slots_dev = expert_up.shape[0]
    req_count = lax.axis_size("req")
    slot_total = req_count * seq_count * slots_dev
    swap = [(i, seq_count - 1 - i) for i in range(seq_count)]
    up_other = lax.ppermute(expert_up, "seq", swap)
    down_other = lax.ppermute(expert_down, "seq", swap)
    tables = jnp.stack(route_tables(routes, route_scores, replica_slot, slot_total))
    tables = lax.all_gather(tables, "req", axis=0).reshape(
        req_count, 2, req_count, seq_count, slots_dev, row_count
    )
    tables = lax.dynamic_index_in_dim(tables, lax.axis_index("req"), 2, keepdims=False)
    own = lax.dynamic_index_in_dim(tables, seq_index, 2, keepdims=False)
    other = lax.dynamic_index_in_dim(tables, seq_count - 1 - seq_index, 2, keepdims=False)
    tables = jnp.concatenate([own, other], axis=2)
    rank_here, share_here = tables[:, 0], tables[:, 1]
    group_size = HEADS // KV_HEADS
    key_width = KV_HEADS * HEAD
    query_index = seq_index * row_count + jnp.arange(row_count, dtype=jnp.int32)
    positions = length + query_index
    queries, new_keys, new_values = project(tokens, attn_gain, w_qkv, positions)
    appended = jnp.concatenate([new_keys.reshape(row_count, -1), new_values], axis=1)
    own_queries = queries.reshape(row_count, KV_HEADS, group_size, HEAD)
    cache_k, cache_v, span_all = (
        lax.all_gather(k_cache, "seq", axis=1, tiled=True),
        lax.all_gather(v_cache, "seq", axis=1, tiled=True),
        lax.all_gather(appended[None], "seq", axis=1, tiled=True),
    )

    def cache_visible(first_key, key_count):
        key_index = first_key + jnp.arange(key_count, dtype=jnp.int32)
        return jnp.broadcast_to((key_index < length)[None, :], (row_count, key_count))

    def span_visible(first_key, key_count):
        key_index = first_key + jnp.arange(key_count, dtype=jnp.int32)
        return key_index[None, :] <= query_index[:, None]

    carried = attend_keys(
        empty_state(row_count),
        own_queries,
        cache_k[0].reshape(-1, KV_HEADS, HEAD),
        cache_v[0].reshape(-1, KV_HEADS, HEAD),
        cache_visible,
    )
    carried = attend_keys(
        carried,
        own_queries,
        span_all[0][:, :key_width].reshape(-1, KV_HEADS, HEAD),
        span_all[0][:, key_width:].reshape(-1, KV_HEADS, HEAD),
        span_visible,
    )
    attended = finish_state(flatten_state(carried))
    stream = (
        tokens.astype(jnp.float32)
        + residual_scale * jnp.dot(attended, w_out, preferred_element_type=jnp.float32)
    ).astype(jnp.bfloat16)
    expert_in = rms_scale(stream, ffn_gain)
    slots_dev = expert_up.shape[0]
    req_count = lax.axis_size("req")
    slot_total = req_count * seq_count * slots_dev
    capacity = 2 * ((row_count * routes.shape[1] + slot_total - 1) // slot_total)
    up_all = jnp.concatenate([expert_up, up_other], axis=0)
    down_all = jnp.concatenate([expert_down, down_other], axis=0)
    rows_in = lax.all_gather(expert_in, "req", axis=0)
    pick = (rank_here[:, :, None, :] == jnp.arange(capacity, dtype=jnp.float32)[:, None]).astype(
        jnp.bfloat16
    )
    share_rows = jnp.sum(pick.astype(jnp.float32) * share_here[:, :, None, :], axis=-1)
    share_rows = jnp.swapaxes(share_rows, 0, 1)
    gathered = jnp.einsum(
        "ijct,itd->jicd", pick, rows_in, preferred_element_type=jnp.float32
    ).astype(jnp.bfloat16)
    gate_up = jnp.einsum("jicd,jdf->jicf", gathered, up_all, preferred_element_type=jnp.float32)
    hidden_width = expert_down.shape[1]
    active = (
        jax.nn.silu(gate_up[..., :hidden_width])
        * gate_up[..., hidden_width:]
        * share_rows[..., None]
    ).astype(jnp.bfloat16)
    outputs = jnp.einsum(
        "jicf,jfd->jicd", active, down_all, preferred_element_type=jnp.float32
    ).astype(jnp.bfloat16)
    partial = jnp.einsum(
        "ijct,jicd->itd", pick, outputs, preferred_element_type=jnp.float32
    ).astype(jnp.bfloat16)
    expert_mix = lax.psum_scatter(partial, "req", scatter_dimension=0)
    return (attended, stream, expert_mix, appended)


def solution(mesh):
    return jax.shard_map(
        shards,
        mesh=mesh,
        in_specs=(
            P(("req", "seq"), None),
            P(),
            P(),
            P(),
            P("req", "seq", None),
            P("req", "seq", None),
            P("req"),
            P(),
            P(("req", "seq"), None),
            P(("req", "seq"), None),
            P(("req", "seq"), None),
            P(("req", "seq"), None, None),
            P(("req", "seq"), None, None),
        ),
        out_specs=(
            P(("req", "seq"), None),
            P(("req", "seq"), None),
            P(("req", "seq"), None),
            P(("req", "seq"), None),
        ),
        check_vma=False,
    )
```

```python
import functools
import math

import jax
import jax.numpy as jnp
from jax import lax
from jax.experimental import pallas as pl
from jax.experimental.pallas import tpu as pltpu
from jax.sharding import PartitionSpec as P

HEADS = 24
KV_HEADS = 8
HEAD = 64
GROUP = HEADS // KV_HEADS
LANES = 128
PAIR = 2 * GROUP * HEAD

epsilon = 1e-06
residual_scale = 0.22
score_scale = 0.015625
rope_base = 10000.0
neg_big = -1e30

BOTH = ("req", "seq")


def vmem_spec():
    return pl.BlockSpec(memory_space=pltpu.VMEM)


def params(mebibytes):
    return pltpu.CompilerParams(vmem_limit_bytes=mebibytes * 2**20)


def qkv_kernel(own_ref, other_ref, gain_ref, cos_ref, sin_ref, w_ref, q_ref, kv_ref, kvo_ref, normed):
    step = pl.program_id(0)
    rows = own_ref.shape[0]
    width = w_ref.shape[1]

    @pl.when(step == 0)
    def _():
        for index, ref in enumerate((own_ref, other_ref)):
            wide = ref[...].astype(jnp.float32)
            mean_square = jnp.mean(wide * wide, axis=-1, keepdims=True)
            normed[index * rows : (index + 1) * rows] = (
                wide * lax.rsqrt(mean_square + epsilon) * gain_ref[...]
            ).astype(jnp.bfloat16)

    def rotated(x, row_slice):
        lane = lax.broadcasted_iota(jnp.int32, x.shape, 1)
        low = (lane & (HEAD - 1)) < HEAD // 2
        swapped = jnp.where(
            low, pltpu.roll(x, width - HEAD // 2, 1), pltpu.roll(x, HEAD // 2, 1)
        )
        times = width // LANES
        cosine = jnp.concatenate([cos_ref[row_slice]] * times, axis=1)
        sine = jnp.concatenate([sin_ref[row_slice]] * times, axis=1)
        return x * cosine + swapped * sine

    @pl.when(step < 3)
    def _():
        x = jnp.dot(normed[:rows], w_ref[...], preferred_element_type=jnp.float32)
        q_ref[...] = (rotated(x, slice(0, rows)) * score_scale).astype(jnp.bfloat16)

    @pl.when(step == 3)
    def _():
        x = jnp.dot(normed[...], w_ref[...], preferred_element_type=jnp.float32)
        x = rotated(x, slice(0, 2 * rows)).astype(jnp.bfloat16)
        kv_ref[...] = x[:rows]
        kvo_ref[...] = x[rows:]

    @pl.when(step == 4)
    def _():
        x = jnp.dot(normed[...], w_ref[...], preferred_element_type=jnp.float32)
        x = x.astype(jnp.bfloat16)
        kv_ref[...] = x[:rows]
        kvo_ref[...] = x[rows:]


def project(own, other, gain, cosine, sine, w_qkv):
    rows, width = own.shape
    tile = KV_HEADS * HEAD
    return pl.pallas_call(
        qkv_kernel,
        grid=(5,),
        in_specs=[vmem_spec()] * 5 + [pl.BlockSpec((width, tile), lambda i: (0, i))],
        out_specs=[
            pl.BlockSpec((rows, tile), lambda i: (0, jnp.minimum(i, 2))),
            pl.BlockSpec((rows, tile), lambda i: (0, jnp.maximum(i - 3, 0))),
            pl.BlockSpec((rows, tile), lambda i: (0, jnp.maximum(i - 3, 0))),
        ],
        out_shape=[
            jax.ShapeDtypeStruct((rows, HEADS * HEAD), jnp.bfloat16),
            jax.ShapeDtypeStruct((rows, 2 * tile), jnp.bfloat16),
            jax.ShapeDtypeStruct((rows, 2 * tile), jnp.bfloat16),
        ],
        scratch_shapes=[pltpu.VMEM((2 * rows, width), jnp.bfloat16)],
        compiler_params=params(24),
        cost_estimate=pl.CostEstimate(
            flops=2 * rows * width * 3584, bytes_accessed=9_500_000, transcendentals=0
        ),
        name="project_rows",
    )(own, other, gain[None], cosine, sine, w_qkv)


def attend_kernel(
    first_row,
    place_ref,
    q_ref,
    kc_ref,
    kco_ref,
    vc_ref,
    vco_ref,
    ks_ref,
    kso_ref,
    vs_ref,
    vso_ref,
    w_out_ref,
    tokens_ref,
    gain_ref,
    attended_ref,
    stream_ref,
    expert_in_ref,
    keys,
    values,
    wide_q,
    total,
):
    step = pl.program_id(0)
    rows = q_ref.shape[0]
    cached = kc_ref.shape[1]
    span = ks_ref.shape[0]
    seq_index = place_ref[0]
    length = place_ref[1]

    @pl.when(step == 0)
    def _():
        position = lax.broadcasted_iota(jnp.int32, (cached, LANES), 0)
        for index, half in enumerate((seq_index, 1 - seq_index)):
            visible = position + half * cached < length
            keys[index * cached : (index + 1) * cached, LANES:] = jnp.where(
                visible, 0.0, neg_big
            ).astype(jnp.bfloat16)
        key = lax.broadcasted_iota(jnp.int32, (span, LANES), 0)
        row = lax.broadcasted_iota(jnp.int32, (span, LANES), 1)
        keys[2 * cached : 2 * cached + span, LANES:] = jnp.where(key <= row, 0.0, neg_big).astype(
            jnp.bfloat16
        )
        keys[2 * cached + span :, LANES:] = jnp.where(
            jnp.zeros((span, LANES), jnp.int32) < seq_index, 0.0, neg_big
        ).astype(jnp.bfloat16)
        values[:, LANES:] = jnp.ones((values.shape[0], LANES), jnp.bfloat16)
        row = lax.broadcasted_iota(jnp.int32, (rows, LANES), 0) + first_row
        lane = lax.broadcasted_iota(jnp.int32, (rows, LANES), 1)
        chosen = jnp.where(row == lane, 1.0, 0.0).astype(jnp.bfloat16)
        for head in range(2 * GROUP):
            wide_q[head * rows : (head + 1) * rows, LANES:] = chosen

    for ref, parts in ((keys, (kc_ref, kco_ref)), (values, (vc_ref, vco_ref))):
        for index, part in enumerate(parts):
            ref[index * cached : (index + 1) * cached, :LANES] = part[0]
    for ref, parts in ((keys, (ks_ref, kso_ref)), (values, (vs_ref, vso_ref))):
        for index, part in enumerate(parts):
            start = 2 * cached + index * span
            ref[start : start + span, :LANES] = part[...]

    low = lax.broadcasted_iota(jnp.int32, (rows, LANES), 1) < HEAD
    tiles = [q_ref[:, i * LANES : (i + 1) * LANES].astype(jnp.float32) for i in range(3)]
    parts = [
        jnp.where(low, tiles[0], 0.0),
        jnp.where(low, pltpu.roll(tiles[0], HEAD, 1), 0.0),
        jnp.where(low, tiles[1], 0.0),
        jnp.where(low, 0.0, tiles[1]),
        jnp.where(low, 0.0, pltpu.roll(tiles[2], HEAD, 1)),
        jnp.where(low, 0.0, tiles[2]),
    ]
    for head, part in enumerate(parts):
        wide_q[head * rows : (head + 1) * rows, :LANES] = part.astype(jnp.bfloat16)

    heads = []
    for head in range(2 * GROUP):
        scores = lax.dot_general(
            wide_q[head * rows : (head + 1) * rows],
            keys[...],
            (((1,), (1,)), ((), ())),
            preferred_element_type=jnp.float32,
        )
        best = jnp.max(scores, axis=-1, keepdims=True)
        weights = jnp.exp(scores - best).astype(jnp.bfloat16)
        sums = jnp.dot(weights, values[...], preferred_element_type=jnp.float32)
        heads.append(sums[:, :LANES] / sums[:, LANES:])
    merged = jnp.concatenate(
        [
            jnp.where(low, heads[0], pltpu.roll(heads[1], HEAD, 1)),
            jnp.where(low, heads[2], heads[3]),
            jnp.where(low, pltpu.roll(heads[4], HEAD, 1), heads[5]),
        ],
        axis=1,
    ).astype(jnp.bfloat16)
    attended_ref[...] = merged
    product = jnp.dot(merged, w_out_ref[...], preferred_element_type=jnp.float32)

    @pl.when(step == 0)
    def _():
        total[...] = product

    @pl.when(step > 0)
    def _():
        total[...] += product

    @pl.when(step == pl.num_programs(0) - 1)
    def _():
        stream = (tokens_ref[...].astype(jnp.float32) + residual_scale * total[...]).astype(
            jnp.bfloat16
        )
        stream_ref[...] = stream
        wide = stream.astype(jnp.float32)
        mean_square = jnp.mean(wide * wide, axis=-1, keepdims=True)
        expert_in_ref[...] = (wide * lax.rsqrt(mean_square + epsilon) * gain_ref[...]).astype(
            jnp.bfloat16
        )


def attend(place, queries, caches, spans, w_out, tokens, gain, first_row, rows):
    k_cache, k_other, v_cache, v_other = caches
    own_span, other_span = spans
    cached = k_cache.shape[1]
    span = own_span.shape[0]
    width = tokens.shape[1]
    pairs = KV_HEADS // 2
    part = first_row // rows
    key_count = 2 * cached + 2 * span
    cache_spec = pl.BlockSpec((1, cached, LANES), lambda j: (0, 0, j))
    key_spec = pl.BlockSpec((span, LANES), lambda j: (0, j))
    value_spec = pl.BlockSpec((span, LANES), lambda j: (0, pairs + j))
    return pl.pallas_call(
        functools.partial(attend_kernel, first_row),
        grid=(pairs,),
        in_specs=[
            pl.BlockSpec(memory_space=pltpu.SMEM),
            pl.BlockSpec((rows, PAIR), lambda j: (part, j)),
            cache_spec,
            cache_spec,
            cache_spec,
            cache_spec,
            key_spec,
            key_spec,
            value_spec,
            value_spec,
            pl.BlockSpec((PAIR, width), lambda j: (j, 0)),
            pl.BlockSpec((rows, width), lambda j: (part, 0)),
            vmem_spec(),
        ],
        out_specs=[
            pl.BlockSpec((rows, PAIR), lambda j: (0, j)),
            pl.BlockSpec((rows, width), lambda j: (0, 0)),
            pl.BlockSpec((rows, width), lambda j: (0, 0)),
        ],
        out_shape=[
            jax.ShapeDtypeStruct((rows, HEADS * HEAD), jnp.bfloat16),
            jax.ShapeDtypeStruct((rows, width), jnp.bfloat16),
            jax.ShapeDtypeStruct((rows, width), jnp.bfloat16),
        ],
        scratch_shapes=[
            pltpu.VMEM((key_count, 2 * LANES), jnp.bfloat16),
            pltpu.VMEM((key_count, 2 * LANES), jnp.bfloat16),
            pltpu.VMEM((2 * GROUP * rows, 2 * LANES), jnp.bfloat16),
            pltpu.VMEM((rows, width), jnp.float32),
        ],
        compiler_params=params(40),
        cost_estimate=pl.CostEstimate(
            flops=8 * HEADS * rows * key_count * LANES,
            bytes_accessed=10_000_000,
            transcendentals=HEADS * rows * key_count,
        ),
        name="attend_rows",
    )(
        place,
        queries,
        k_cache,
        k_other,
        v_cache,
        v_other,
        own_span,
        other_span,
        own_span,
        other_span,
        w_out,
        tokens,
        gain[None],
    )


def expert_kernel(sources, capacity, slot_ref, *refs):
    row_refs = refs[:sources]
    table_ref, up_ref, up_other_ref, down_ref, down_other_ref = refs[sources : sources + 5]
    out_refs = refs[sources + 5 : 2 * sources + 5]
    held, pick, share_rows = refs[2 * sources + 5 :]
    step = pl.program_id(0)
    slots = held.shape[0]
    own_slots = slots // 2
    tokens = row_refs[0].shape[0]
    hidden = down_ref.shape[1]
    top = table_ref.shape[1] // 2

    @pl.when(step == 0)
    def _():
        hot_rows, share_lines = [], []
        for source in range(sources):
            ids = table_ref[source, :top]
            shares = table_ref[source, top:]
            for slot in range(slots):
                match = ids == slot_ref[slot].astype(jnp.float32)
                hot_rows.append(
                    jnp.max(jnp.where(match, 1.0, 0.0), axis=0, keepdims=True)
                )
                share_lines.append(
                    jnp.sum(jnp.where(match, shares, 0.0), axis=0, keepdims=True)
                )
        hot = jnp.concatenate(hot_rows, axis=0)
        earlier = jnp.where(
            lax.broadcasted_iota(jnp.int32, (tokens, tokens), 0)
            < lax.broadcasted_iota(jnp.int32, (tokens, tokens), 1),
            1.0,
            0.0,
        ).astype(jnp.bfloat16)
        rank = jnp.dot(hot.astype(jnp.bfloat16), earlier, preferred_element_type=jnp.float32)
        rank = jnp.where(hot > 0.0, rank, -1.0)
        place = lax.broadcasted_iota(jnp.int32, (capacity, tokens), 0).astype(jnp.float32)
        for source in range(sources):
            picks = []
            for slot in range(slots):
                line = source * slots + slot
                chosen = jnp.where(place == rank[line : line + 1], 1.0, 0.0)
                share_rows[slot, source * capacity : (source + 1) * capacity] = jnp.sum(
                    chosen * share_lines[line], axis=1, keepdims=True
                )
                picks.append(chosen)
            picked = jnp.concatenate(picks, axis=0)
            pick[source] = jnp.transpose(picked).astype(jnp.bfloat16)
            rows = jnp.dot(
                picked.astype(jnp.bfloat16),
                row_refs[source][...],
                preferred_element_type=jnp.float32,
            ).astype(jnp.bfloat16)
            for slot in range(slots):
                held[slot, source * capacity : (source + 1) * capacity] = rows[
                    slot * capacity : (slot + 1) * capacity
                ]

    def run(up, down):
        gate_up = jnp.dot(held[step], up[0], preferred_element_type=jnp.float32)
        active = (
            jax.nn.silu(gate_up[:, :hidden]) * gate_up[:, hidden:] * share_rows[step]
        ).astype(jnp.bfloat16)
        held[step] = jnp.dot(active, down[0], preferred_element_type=jnp.float32).astype(
            jnp.bfloat16
        )

    @pl.when(step < own_slots)
    def _():
        run(up_ref, down_ref)

    @pl.when(step >= own_slots)
    def _():
        run(up_other_ref, down_other_ref)

    @pl.when(step == slots - 1)
    def _():
        for source in range(sources):
            rows = jnp.concatenate(
                [
                    held[slot, source * capacity : (source + 1) * capacity]
                    for slot in range(slots)
                ],
                axis=0,
            )
            out_refs[source][...] = jnp.dot(
                pick[source], rows, preferred_element_type=jnp.float32
            ).astype(jnp.bfloat16)


def run_experts(slot_ids, rows, tables, ups, downs, capacity):
    sources = len(rows)
    tokens, width = rows[0].shape
    own_slots, _, double = ups[0].shape
    hidden = double // 2
    slots = 2 * own_slots

    def own(j):
        return (jnp.minimum(j, own_slots - 1), 0, 0)

    def other(j):
        return (jnp.maximum(j - own_slots, 0), 0, 0)

    return pl.pallas_call(
        functools.partial(expert_kernel, sources, capacity),
        grid=(slots,),
        in_specs=[pl.BlockSpec(memory_space=pltpu.SMEM)]
        + [vmem_spec()] * (sources + 1)
        + [
            pl.BlockSpec((1, width, double), own),
            pl.BlockSpec((1, width, double), other),
            pl.BlockSpec((1, hidden, width), own),
            pl.BlockSpec((1, hidden, width), other),
        ],
        out_specs=[vmem_spec()] * sources,
        out_shape=[jax.ShapeDtypeStruct((tokens, width), jnp.bfloat16)] * sources,
        scratch_shapes=[
            pltpu.VMEM((slots, sources * capacity, width), jnp.bfloat16),
            pltpu.VMEM((sources, tokens, slots * capacity), jnp.bfloat16),
            pltpu.VMEM((slots, sources * capacity, 1), jnp.float32),
        ],
        compiler_params=params(48),
        cost_estimate=pl.CostEstimate(
            flops=6 * slots * sources * capacity * width * hidden,
            bytes_accessed=26_000_000,
            transcendentals=slots * sources * capacity * hidden,
        ),
        name="run_experts",
    )(slot_ids, *rows, tables, ups[0], ups[1], downs[0], downs[1])


def chip_shape(chips):
    depth = 4 if chips % 4 == 0 else 1
    plane = chips // depth
    side = math.isqrt(plane)
    while plane % side:
        side -= 1
    return depth, plane // side, side


def make_shift(chips, cores):
    depth, tall, wide = chip_shape(chips)
    swap = tall == wide
    sizes = {"z": depth, "a": tall, "b": wide}

    def pairs(role, offset):
        out = []
        for z in range(depth):
            for y in range(tall):
                for x in range(wide):
                    for core in range(cores):
                        axis = role
                        if swap and core % 2 == 1:
                            axis = {"z": "z", "a": "b", "b": "a"}[role]
                        to_z, to_y, to_x = z, y, x
                        if axis == "z":
                            to_z = (z + offset) % depth
                        elif axis == "a":
                            to_y = (y + offset) % tall
                        else:
                            to_x = (x + offset) % wide
                        source = ((z * tall + y) * wide + x) * cores + core
                        target = ((to_z * tall + to_y) * wide + to_x) * cores + core
                        out.append((source, target))
        return out

    def shift(value, role, offset):
        return lax.ppermute(value, BOTH, pairs(role, offset % sizes[role]))

    return shift, sizes


def gather_blocks(value, shift, sizes):
    line = [value] + [shift(value, "z", k) for k in range(1, sizes["z"])]
    plane = [line] + [[shift(v, "a", j) for v in line] for j in range(1, sizes["a"])]
    return [plane] + [
        [[shift(v, "b", k) for v in row] for row in plane] for k in range(1, sizes["b"])
    ]


def gather_stacked(value, shift, sizes):
    stacked = value[None]
    for role in ("z", "a", "b"):
        stacked = jnp.concatenate(
            [stacked] + [shift(stacked, role, k) for k in range(1, sizes[role])], axis=0
        )
    return stacked


def add_all(terms):
    total = terms[0].astype(jnp.float32)
    for term in terms[1:]:
        total = total + term.astype(jnp.float32)
    return total.astype(terms[0].dtype)


def scatter_blocks(blocks, shift, sizes):
    plane = [
        [
            add_all(
                [blocks[0][j][i]]
                + [shift(blocks[k][j][i], "b", -k) for k in range(1, sizes["b"])]
            )
            for i in range(sizes["z"])
        ]
        for j in range(sizes["a"])
    ]
    line = [
        add_all([plane[0][i]] + [shift(plane[j][i], "a", -j) for j in range(1, sizes["a"])])
        for i in range(sizes["z"])
    ]
    return add_all([line[0]] + [shift(line[i], "z", -i) for i in range(1, sizes["z"])])


def rope_tables(positions):
    half = HEAD // 2
    frequency = rope_base ** (-jnp.arange(half, dtype=jnp.float32) / half)
    angles = positions.astype(jnp.float32)[:, None] * frequency[None, :]
    cosine, sine = jnp.cos(angles), jnp.sin(angles)
    return (
        jnp.concatenate([cosine] * 4, axis=1),
        jnp.concatenate([-sine, sine, -sine, sine], axis=1),
    )


def shards(
    tokens,
    attn_gain,
    w_qkv,
    w_out,
    k_cache,
    v_cache,
    cache_len,
    ffn_gain,
    routes,
    route_scores,
    replica_slot,
    expert_up,
    expert_down,
):
    row_count, top_count = routes.shape
    chips, cores = lax.axis_size("req"), lax.axis_size("seq")
    seq_index = lax.axis_index("seq")
    length = cache_len[0]
    slots_dev = expert_up.shape[0]
    slot_total = chips * cores * slots_dev
    capacity = 2 * ((row_count * top_count + slot_total - 1) // slot_total)
    shift, sizes = make_shift(chips, cores)

    def swap(value):
        return lax.ppermute(value, "seq", [(0, 1), (1, 0)])

    other_tokens = swap(tokens)
    k_other, v_other = swap(k_cache), swap(v_cache)

    experts = jnp.arange(replica_slot.shape[1], dtype=jnp.int32)
    slot_of = jnp.sum(
        jnp.where(routes[:, :, None] == experts, replica_slot[:, None, :], 0), axis=2
    )
    shares = route_scores / jnp.sum(route_scores, axis=1, keepdims=True)
    table = jnp.concatenate([slot_of.astype(jnp.float32), shares], axis=1).T
    tables = gather_stacked(table, shift, sizes)

    row_index = jnp.arange(row_count, dtype=jnp.int32)
    cosine, sine = rope_tables(
        length
        + jnp.concatenate(
            [seq_index * row_count + row_index, (1 - seq_index) * row_count + row_index]
        )
    )
    queries, appended, other_span = project(tokens, other_tokens, attn_gain, cosine, sine, w_qkv)
    place = jnp.stack([seq_index, length]).astype(jnp.int32)
    attended, stream, expert_in = attend(
        place,
        queries,
        (k_cache, k_other, v_cache, v_other),
        (appended, other_span),
        w_out,
        tokens,
        ffn_gain,
        0,
        row_count,
    )
    up_other, down_other = swap(expert_up), swap(expert_down)
    chip_slots = jnp.arange(slots_dev, dtype=jnp.int32)
    core_base = lax.axis_index("req") * cores
    slot_ids = jnp.concatenate(
        [
            (core_base + seq_index) * slots_dev + chip_slots,
            (core_base + 1 - seq_index) * slots_dev + chip_slots,
        ]
    ).astype(jnp.int32)
    blocks = gather_blocks(expert_in, shift, sizes)
    in_group = sizes["a"] * sizes["z"]
    results = []
    for index, plane in enumerate(blocks):
        flat = run_experts(
            slot_ids,
            [value for line in plane for value in line],
            tables[index * in_group : (index + 1) * in_group],
            (expert_up, up_other),
            (expert_down, down_other),
            capacity,
        )
        results.append(
            [flat[j * sizes["z"] : (j + 1) * sizes["z"]] for j in range(sizes["a"])]
        )
    expert_mix = scatter_blocks(results, shift, sizes)
    return (attended, stream, expert_mix, appended)


def solution(mesh):
    return jax.shard_map(
        shards,
        mesh=mesh,
        in_specs=(
            P(("req", "seq"), None),
            P(),
            P(),
            P(),
            P("req", "seq", None),
            P("req", "seq", None),
            P("req"),
            P(),
            P(("req", "seq"), None),
            P(("req", "seq"), None),
            P(("req", "seq"), None),
            P(("req", "seq"), None, None),
            P(("req", "seq"), None, None),
        ),
        out_specs=(
            P(("req", "seq"), None),
            P(("req", "seq"), None),
            P(("req", "seq"), None),
            P(("req", "seq"), None),
        ),
        check_vma=False,
    )
```

```python
import functools
import math

import jax
import jax.numpy as jnp
from jax import lax
from jax.experimental import pallas as pl
from jax.experimental.pallas import tpu as pltpu
from jax.sharding import PartitionSpec as P

HEADS = 24
KV_HEADS = 8
HEAD = 64
GROUP = HEADS // KV_HEADS
LANES = 128
PAIR = 2 * GROUP * HEAD

epsilon = 1e-06
residual_scale = 0.22
score_scale = 0.015625
rope_base = 10000.0
neg_big = -1e30

BOTH = ("req", "seq")


def vmem_spec():
    return pl.BlockSpec(memory_space=pltpu.VMEM)


def params(mebibytes):
    return pltpu.CompilerParams(vmem_limit_bytes=mebibytes * 2**20)


def qkv_kernel(own_ref, other_ref, gain_ref, cos_ref, sin_ref, w_ref, q_ref, kv_ref, kvo_ref, normed):
    step = pl.program_id(0)
    rows = own_ref.shape[0]
    width = w_ref.shape[1]

    @pl.when(step == 0)
    def _():
        for index, ref in enumerate((own_ref, other_ref)):
            wide = ref[...].astype(jnp.float32)
            mean_square = jnp.mean(wide * wide, axis=-1, keepdims=True)
            normed[index * rows : (index + 1) * rows] = (
                wide * lax.rsqrt(mean_square + epsilon) * gain_ref[...]
            ).astype(jnp.bfloat16)

    def rotated(x, row_slice):
        lane = lax.broadcasted_iota(jnp.int32, x.shape, 1)
        low = (lane & (HEAD - 1)) < HEAD // 2
        swapped = jnp.where(
            low, pltpu.roll(x, width - HEAD // 2, 1), pltpu.roll(x, HEAD // 2, 1)
        )
        times = width // LANES
        cosine = jnp.concatenate([cos_ref[row_slice]] * times, axis=1)
        sine = jnp.concatenate([sin_ref[row_slice]] * times, axis=1)
        return x * cosine + swapped * sine

    @pl.when(step < 3)
    def _():
        x = jnp.dot(normed[:rows], w_ref[...], preferred_element_type=jnp.float32)
        q_ref[...] = (rotated(x, slice(0, rows)) * score_scale).astype(jnp.bfloat16)

    @pl.when(step == 3)
    def _():
        x = jnp.dot(normed[...], w_ref[...], preferred_element_type=jnp.float32)
        x = rotated(x, slice(0, 2 * rows)).astype(jnp.bfloat16)
        kv_ref[...] = x[:rows]
        kvo_ref[...] = x[rows:]

    @pl.when(step == 4)
    def _():
        x = jnp.dot(normed[...], w_ref[...], preferred_element_type=jnp.float32)
        x = x.astype(jnp.bfloat16)
        kv_ref[...] = x[:rows]
        kvo_ref[...] = x[rows:]


def project(own, other, gain, cosine, sine, w_qkv):
    rows, width = own.shape
    tile = KV_HEADS * HEAD
    return pl.pallas_call(
        qkv_kernel,
        grid=(5,),
        in_specs=[vmem_spec()] * 5 + [pl.BlockSpec((width, tile), lambda i: (0, i))],
        out_specs=[
            pl.BlockSpec((rows, tile), lambda i: (0, jnp.minimum(i, 2))),
            pl.BlockSpec((rows, tile), lambda i: (0, jnp.maximum(i - 3, 0))),
            pl.BlockSpec((rows, tile), lambda i: (0, jnp.maximum(i - 3, 0))),
        ],
        out_shape=[
            jax.ShapeDtypeStruct((rows, HEADS * HEAD), jnp.bfloat16),
            jax.ShapeDtypeStruct((rows, 2 * tile), jnp.bfloat16),
            jax.ShapeDtypeStruct((rows, 2 * tile), jnp.bfloat16),
        ],
        scratch_shapes=[pltpu.VMEM((2 * rows, width), jnp.bfloat16)],
        compiler_params=params(56),
        cost_estimate=pl.CostEstimate(
            flops=2 * rows * width * 3584, bytes_accessed=9_500_000, transcendentals=0
        ),
        name="project_rows",
    )(own, other, gain[None], cosine, sine, w_qkv)


def attend_kernel(first_row, extra, place_ref, q_ref, kc_ref, kco_ref, vc_ref, vco_ref, ks_ref, kso_ref, vs_ref, vso_ref, w_out_ref, tokens_ref, gain_ref, *refs):
    attended_ref, stream_ref, expert_in_ref, keys, values, wide_q, total = refs[extra:]
    step = pl.program_id(0)
    rows = q_ref.shape[0]
    cached = kc_ref.shape[1]
    span = ks_ref.shape[0]
    seq_index = place_ref[0]
    length = place_ref[1]

    @pl.when(step == 0)
    def _():
        position = lax.broadcasted_iota(jnp.int32, (cached, LANES), 0)
        for index, half in enumerate((seq_index, 1 - seq_index)):
            visible = position + half * cached < length
            keys[index * cached : (index + 1) * cached, LANES:] = jnp.where(
                visible, 0.0, neg_big
            ).astype(jnp.bfloat16)
        key = lax.broadcasted_iota(jnp.int32, (span, LANES), 0)
        row = lax.broadcasted_iota(jnp.int32, (span, LANES), 1)
        keys[2 * cached : 2 * cached + span, LANES:] = jnp.where(key <= row, 0.0, neg_big).astype(
            jnp.bfloat16
        )
        keys[2 * cached + span :, LANES:] = jnp.where(
            jnp.zeros((span, LANES), jnp.int32) < seq_index, 0.0, neg_big
        ).astype(jnp.bfloat16)
        values[:, LANES:] = jnp.ones((values.shape[0], LANES), jnp.bfloat16)
        row = lax.broadcasted_iota(jnp.int32, (rows, LANES), 0) + first_row
        lane = lax.broadcasted_iota(jnp.int32, (rows, LANES), 1)
        chosen = jnp.where(row == lane, 1.0, 0.0).astype(jnp.bfloat16)
        for head in range(2 * GROUP):
            wide_q[head * rows : (head + 1) * rows, LANES:] = chosen

    for ref, parts in ((keys, (kc_ref, kco_ref)), (values, (vc_ref, vco_ref))):
        for index, part in enumerate(parts):
            ref[index * cached : (index + 1) * cached, :LANES] = part[0]
    for ref, parts in ((keys, (ks_ref, kso_ref)), (values, (vs_ref, vso_ref))):
        for index, part in enumerate(parts):
            start = 2 * cached + index * span
            ref[start : start + span, :LANES] = part[...]

    low = lax.broadcasted_iota(jnp.int32, (rows, LANES), 1) < HEAD
    tiles = [q_ref[:, i * LANES : (i + 1) * LANES].astype(jnp.float32) for i in range(3)]
    parts = [
        jnp.where(low, tiles[0], 0.0),
        jnp.where(low, pltpu.roll(tiles[0], HEAD, 1), 0.0),
        jnp.where(low, tiles[1], 0.0),
        jnp.where(low, 0.0, tiles[1]),
        jnp.where(low, 0.0, pltpu.roll(tiles[2], HEAD, 1)),
        jnp.where(low, 0.0, tiles[2]),
    ]
    for head, part in enumerate(parts):
        wide_q[head * rows : (head + 1) * rows, :LANES] = part.astype(jnp.bfloat16)

    heads = []
    batch = GROUP * rows
    for first in range(0, 2 * GROUP * rows, batch):
        scores = lax.dot_general(
            wide_q[first : first + batch],
            keys[...],
            (((1,), (1,)), ((), ())),
            preferred_element_type=jnp.float32,
        )
        best = jnp.max(scores, axis=-1, keepdims=True)
        weights = jnp.exp(scores - best).astype(jnp.bfloat16)
        sums = jnp.dot(weights, values[...], preferred_element_type=jnp.float32)
        mean = sums[:, :LANES] / sums[:, LANES:]
        heads += [mean[i : i + rows] for i in range(0, batch, rows)]
    merged = jnp.concatenate(
        [
            jnp.where(low, heads[0], pltpu.roll(heads[1], HEAD, 1)),
            jnp.where(low, heads[2], heads[3]),
            jnp.where(low, pltpu.roll(heads[4], HEAD, 1), heads[5]),
        ],
        axis=1,
    ).astype(jnp.bfloat16)
    attended_ref[...] = merged
    product = jnp.dot(merged, w_out_ref[...], preferred_element_type=jnp.float32)

    @pl.when(step == 0)
    def _():
        total[...] = product

    @pl.when(step > 0)
    def _():
        total[...] += product

    @pl.when(step == pl.num_programs(0) - 1)
    def _():
        stream = (tokens_ref[...].astype(jnp.float32) + residual_scale * total[...]).astype(
            jnp.bfloat16
        )
        stream_ref[...] = stream
        wide = stream.astype(jnp.float32)
        mean_square = jnp.mean(wide * wide, axis=-1, keepdims=True)
        expert_in_ref[...] = (wide * lax.rsqrt(mean_square + epsilon) * gain_ref[...]).astype(
            jnp.bfloat16
        )


def attend(place, queries, caches, spans, w_out, tokens, gain, first_row, rows, filled, after):
    k_cache, k_other, v_cache, v_other = caches
    own_span, other_span = spans
    cached = k_cache.shape[1]
    span, width = tokens.shape
    pairs = KV_HEADS // 2
    part = first_row // rows
    key_count = 2 * cached + 2 * span
    cache_spec = pl.BlockSpec((1, cached, LANES), lambda j: (0, 0, j))
    key_spec = pl.BlockSpec((span, LANES), lambda j: (0, j))
    value_spec = pl.BlockSpec((span, LANES), lambda j: (0, pairs + j))
    extra = [*filled, *after]
    return pl.pallas_call(
        functools.partial(attend_kernel, first_row, len(extra)),
        grid=(pairs,),
        in_specs=[
            pl.BlockSpec(memory_space=pltpu.SMEM),
            pl.BlockSpec((rows, PAIR), lambda j: (part, j)),
            cache_spec,
            cache_spec,
            cache_spec,
            cache_spec,
            key_spec,
            key_spec,
            value_spec,
            value_spec,
            pl.BlockSpec((PAIR, width), lambda j: (j, 0)),
            pl.BlockSpec((rows, width), lambda j: (part, 0)),
            vmem_spec(),
        ]
        + [pl.BlockSpec(memory_space=pl.ANY)] * len(extra),
        out_specs=[
            pl.BlockSpec((rows, PAIR), lambda j: (part, j)),
            pl.BlockSpec((rows, width), lambda j: (part, 0)),
            pl.BlockSpec((rows, width), lambda j: (0, 0)),
        ],
        out_shape=[
            jax.ShapeDtypeStruct((span, HEADS * HEAD), jnp.bfloat16),
            jax.ShapeDtypeStruct((span, width), jnp.bfloat16),
            jax.ShapeDtypeStruct((rows, width), jnp.bfloat16),
        ],
        input_output_aliases={13 + i: i for i in range(len(filled))},
        scratch_shapes=[
            pltpu.VMEM((key_count, 2 * LANES), jnp.bfloat16),
            pltpu.VMEM((key_count, 2 * LANES), jnp.bfloat16),
            pltpu.VMEM((2 * GROUP * rows, 2 * LANES), jnp.bfloat16),
            pltpu.VMEM((rows, width), jnp.float32),
        ],
        compiler_params=params(36),
        cost_estimate=pl.CostEstimate(
            flops=16 * HEADS * rows * key_count * LANES,
            bytes_accessed=10_000_000,
            transcendentals=HEADS * rows * key_count,
        ),
        name="attend_rows",
    )(
        place,
        queries,
        k_cache,
        k_other,
        v_cache,
        v_other,
        own_span,
        other_span,
        own_span,
        other_span,
        w_out,
        tokens,
        gain[None],
        *extra,
    )


def plan_kernel(groups, capacity, slot_ref, chip_ref, table_ref, *out_refs):
    slots = slot_ref.shape[0]
    chips, height, tokens = table_ref.shape
    top = height // 2
    in_group = chips // groups
    earlier = jnp.where(
        lax.broadcasted_iota(jnp.int32, (tokens, tokens), 0)
        < lax.broadcasted_iota(jnp.int32, (tokens, tokens), 1),
        1.0,
        0.0,
    ).astype(jnp.bfloat16)
    place = lax.broadcasted_iota(jnp.int32, (capacity, tokens), 0).astype(jnp.float32)
    for group in range(groups):
        pick_ref, back_ref, share_ref = out_refs[3 * group : 3 * group + 3]
        hot_rows, share_lines = [], []
        for source in range(in_group):
            entry = table_ref[chip_ref[group * in_group + source]]
            for slot in range(slots):
                match = entry[:top] == slot_ref[slot].astype(jnp.float32)
                hot_rows.append(jnp.max(jnp.where(match, 1.0, 0.0), axis=0, keepdims=True))
                share_lines.append(
                    jnp.sum(jnp.where(match, entry[top:], 0.0), axis=0, keepdims=True)
                )
        hot = jnp.concatenate(hot_rows, axis=0)
        rank = jnp.dot(hot.astype(jnp.bfloat16), earlier, preferred_element_type=jnp.float32)
        rank = jnp.where(hot > 0.0, rank, -1.0)
        for source in range(in_group):
            picks = []
            for slot in range(slots):
                line = source * slots + slot
                chosen = jnp.where(place == rank[line : line + 1], 1.0, 0.0)
                share_ref[slot, source * capacity : (source + 1) * capacity] = jnp.sum(
                    chosen * share_lines[line], axis=1, keepdims=True
                )
                picks.append(chosen)
            picked = jnp.concatenate(picks, axis=0)
            pick_ref[source] = picked.astype(jnp.bfloat16)
            back_ref[source] = jnp.transpose(picked).astype(jnp.bfloat16)


def plan_routes(slot_ids, chip_ids, tables, groups, capacity):
    chips, _, tokens = tables.shape
    slots = slot_ids.shape[0]
    in_group = chips // groups
    flat = pl.pallas_call(
        functools.partial(plan_kernel, groups, capacity),
        in_specs=[pl.BlockSpec(memory_space=pltpu.SMEM)] * 2 + [vmem_spec()],
        out_specs=[vmem_spec()] * (3 * groups),
        out_shape=[
            jax.ShapeDtypeStruct((in_group, slots * capacity, tokens), jnp.bfloat16),
            jax.ShapeDtypeStruct((in_group, tokens, slots * capacity), jnp.bfloat16),
            jax.ShapeDtypeStruct((slots, in_group * capacity, 1), jnp.float32),
        ]
        * groups,
        compiler_params=params(24),
        cost_estimate=pl.CostEstimate(
            flops=5_000_000_000, bytes_accessed=2_000_000, transcendentals=0
        ),
        name="plan_routes",
    )(slot_ids, chip_ids, tables)
    return [flat[3 * i : 3 * i + 3] for i in range(groups)]


def expert_kernel(in_cuts, out_cuts, extra, *refs):
    row_refs = refs[: len(in_cuts)]
    rest = refs[len(in_cuts) :]
    pick_ref, back_ref, share_ref, up_ref, up_other_ref, down_ref, down_other_ref = rest[:7]
    out_refs = rest[7 + extra : 7 + extra + len(out_cuts)]
    held = rest[-1]
    step = pl.program_id(0)
    slots = held.shape[0]
    own_slots = slots // 2
    sources = pick_ref.shape[0]
    capacity = held.shape[1] // sources
    hidden = down_ref.shape[1]

    @pl.when(step == 0)
    def _():
        for source in range(sources):
            rows = jnp.concatenate([ref[source] for ref in row_refs], axis=0)
            rows = jnp.dot(
                pick_ref[source], rows, preferred_element_type=jnp.float32
            ).astype(jnp.bfloat16)
            for slot in range(slots):
                held[slot, source * capacity : (source + 1) * capacity] = rows[
                    slot * capacity : (slot + 1) * capacity
                ]

    def run(up, down):
        gate_up = jnp.dot(held[step], up[0], preferred_element_type=jnp.float32)
        active = (
            jax.nn.silu(gate_up[:, :hidden]) * gate_up[:, hidden:] * share_ref[step]
        ).astype(jnp.bfloat16)
        held[step] = jnp.dot(active, down[0], preferred_element_type=jnp.float32).astype(
            jnp.bfloat16
        )

    @pl.when(step < own_slots)
    def _():
        run(up_ref, down_ref)

    @pl.when(step >= own_slots)
    def _():
        run(up_other_ref, down_other_ref)

    @pl.when(step == slots - 1)
    def _():
        for source in range(sources):
            rows = jnp.concatenate(
                [
                    held[slot, source * capacity : (source + 1) * capacity]
                    for slot in range(slots)
                ],
                axis=0,
            )
            mixed = jnp.dot(back_ref[source], rows, preferred_element_type=jnp.float32)
            start = 0
            for ref, count in zip(out_refs, out_cuts):
                ref[source] = mixed[start : start + count].astype(jnp.bfloat16)
                start += count


def run_experts(rows, plan, ups, downs, out_cuts, after):
    sources, _, width = rows[0].shape
    own_slots, _, double = ups[0].shape
    hidden = double // 2
    slots = 2 * own_slots
    places = plan[2].shape[1]

    def own(j):
        return (jnp.minimum(j, own_slots - 1), 0, 0)

    def other(j):
        return (jnp.maximum(j - own_slots, 0), 0, 0)

    return pl.pallas_call(
        functools.partial(
            expert_kernel, tuple(r.shape[1] for r in rows), tuple(out_cuts), len(after)
        ),
        grid=(slots,),
        in_specs=[vmem_spec()] * (len(rows) + 3)
        + [
            pl.BlockSpec((1, width, double), own),
            pl.BlockSpec((1, width, double), other),
            pl.BlockSpec((1, hidden, width), own),
            pl.BlockSpec((1, hidden, width), other),
        ]
        + [pl.BlockSpec(memory_space=pl.ANY)] * len(after),
        out_specs=[vmem_spec()] * len(out_cuts),
        out_shape=[jax.ShapeDtypeStruct((sources, c, width), jnp.bfloat16) for c in out_cuts],
        scratch_shapes=[pltpu.VMEM((slots, places, width), jnp.bfloat16)],
        compiler_params=params(44),
        cost_estimate=pl.CostEstimate(
            flops=6 * slots * places * width * hidden,
            bytes_accessed=26_000_000,
            transcendentals=slots * places * hidden,
        ),
        name="run_experts",
    )(*rows, *plan, ups[0], ups[1], downs[0], downs[1], *after)


def chip_shape(chips):
    depth = 4 if chips % 4 == 0 else 1
    plane = chips // depth
    side = math.isqrt(plane)
    while plane % side:
        side -= 1
    return depth, plane // side, side


def make_shift(chips, cores):
    depth, tall, wide = chip_shape(chips)
    swap = tall == wide
    sizes = {"z": depth, "a": tall, "b": wide}

    def pairs(role, offset):
        out = []
        for z in range(depth):
            for y in range(tall):
                for x in range(wide):
                    for core in range(cores):
                        axis = role
                        if swap and core % 2 == 1:
                            axis = {"z": "z", "a": "b", "b": "a"}[role]
                        to_z, to_y, to_x = z, y, x
                        if axis == "z":
                            to_z = (z + offset) % depth
                        elif axis == "a":
                            to_y = (y + offset) % tall
                        else:
                            to_x = (x + offset) % wide
                        source = ((z * tall + y) * wide + x) * cores + core
                        target = ((to_z * tall + to_y) * wide + to_x) * cores + core
                        out.append((source, target))
        return out

    def shift(value, role, offset):
        return lax.ppermute(value, BOTH, pairs(role, offset % sizes[role]))

    return shift, sizes


def gather_planes(value, shift, sizes):
    stacked = value[None]
    for role in ("z", "a"):
        stacked = jnp.concatenate(
            [stacked] + [shift(stacked, role, k) for k in range(1, sizes[role])], axis=0
        )
    return [stacked] + [shift(stacked, "b", k) for k in range(1, sizes["b"])]


def add_all(terms):
    total = terms[0].astype(jnp.float32)
    for term in terms[1:]:
        total = total + term.astype(jnp.float32)
    return total.astype(terms[0].dtype)


def scatter_planes(planes, shift, sizes):
    deep = sizes["z"]
    terms = [planes[0]] + [shift(planes[k], "b", -k) for k in range(1, sizes["b"])]

    def part(j):
        return [term[j * deep : (j + 1) * deep] for term in terms]

    arrived = [shift(add_all(part(j)), "a", -j) for j in range(1, sizes["a"])]
    line = part(0) + arrived
    moved = [shift(add_all([t[i] for t in line]), "z", -i) for i in range(1, deep)]
    return add_all([add_all([t[0] for t in line])] + moved)


def source_chips(chip, core, chips):
    depth, tall, wide = chip_shape(chips)
    index = jnp.arange(chips, dtype=jnp.int32)
    back_z, back_a, back_b = index % depth, index // depth % tall, index // (depth * tall)
    back_y, back_x = back_a, back_b
    if tall == wide:
        back_y = jnp.where(core == 0, back_a, back_b)
        back_x = jnp.where(core == 0, back_b, back_a)
    z, y, x = chip // (tall * wide), chip // wide % tall, chip % wide
    z, y, x = (z - back_z) % depth, (y - back_y) % tall, (x - back_x) % wide
    return ((z * tall + y) * wide + x).astype(jnp.int32)


def rope_tables(positions):
    half = HEAD // 2
    frequency = rope_base ** (-jnp.arange(half, dtype=jnp.float32) / half)
    angles = positions.astype(jnp.float32)[:, None] * frequency[None, :]
    cosine, sine = jnp.cos(angles), jnp.sin(angles)
    return (
        jnp.concatenate([cosine] * 4, axis=1),
        jnp.concatenate([-sine, sine, -sine, sine], axis=1),
    )


def shards(
    tokens,
    attn_gain,
    w_qkv,
    w_out,
    k_cache,
    v_cache,
    cache_len,
    ffn_gain,
    routes,
    route_scores,
    replica_slot,
    expert_up,
    expert_down,
):
    row_count, top_count = routes.shape
    chips, cores = lax.axis_size("req"), lax.axis_size("seq")
    seq_index = lax.axis_index("seq")
    length = cache_len[0]
    slots_dev = expert_up.shape[0]
    slot_total = chips * cores * slots_dev
    capacity = 2 * ((row_count * top_count + slot_total - 1) // slot_total)
    shift, sizes = make_shift(chips, cores)

    def swap(value):
        return lax.ppermute(value, "seq", [(0, 1), (1, 0)])

    other_tokens = swap(tokens)
    k_other, v_other = swap(k_cache), swap(v_cache)

    up_other, down_other = swap(expert_up), swap(expert_down)
    experts = jnp.arange(replica_slot.shape[1], dtype=jnp.int32)
    slot_of = jnp.sum(
        jnp.where(routes[:, :, None] == experts, replica_slot[:, None, :], 0), axis=2
    )
    shares = route_scores / jnp.sum(route_scores, axis=1, keepdims=True)
    table = jnp.concatenate([slot_of.astype(jnp.float32), shares], axis=1).T
    tables = lax.all_gather(table, "req", axis=0)
    chip = lax.axis_index("req")
    chip_slots = jnp.arange(slots_dev, dtype=jnp.int32)
    slot_ids = jnp.concatenate(
        [
            (chip * cores + seq_index) * slots_dev + chip_slots,
            (chip * cores + 1 - seq_index) * slots_dev + chip_slots,
        ]
    ).astype(jnp.int32)
    plans = plan_routes(slot_ids, source_chips(chip, seq_index, chips), tables, sizes["b"], capacity)

    row_index = jnp.arange(row_count, dtype=jnp.int32)
    cosine, sine = rope_tables(
        length
        + jnp.concatenate(
            [seq_index * row_count + row_index, (1 - seq_index) * row_count + row_index]
        )
    )
    queries, appended, other_span = project(tokens, other_tokens, attn_gain, cosine, sine, w_qkv)
    place = jnp.stack([seq_index, length]).astype(jnp.int32)
    half = row_count // 2
    filled, halves = [], []
    for index in range(2):
        attended, stream, expert_in = attend(
            place,
            queries,
            (k_cache, k_other, v_cache, v_other),
            (appended, other_span),
            w_out,
            tokens,
            ffn_gain,
            index * half,
            half,
            filled,
            [up_other, down_other] if index else [],
        )
        filled = [attended, stream]
        halves.append(gather_planes(expert_in, shift, sizes))
    results = []
    for index in range(sizes["b"]):
        results.append(
            run_experts(
                [planes[index] for planes in halves],
                plans[index],
                (expert_up, up_other),
                (expert_down, down_other),
                (half, row_count - half),
                results[-1][:1] if results else [],
            )
        )
    expert_mix = jnp.concatenate(
        [scatter_planes([r[i] for r in results], shift, sizes) for i in range(2)], axis=0
    )
    return (attended, stream, expert_mix, appended)


def solution(mesh):
    return jax.shard_map(
        shards,
        mesh=mesh,
        in_specs=(
            P(("req", "seq"), None),
            P(),
            P(),
            P(),
            P("req", "seq", None),
            P("req", "seq", None),
            P("req"),
            P(),
            P(("req", "seq"), None),
            P(("req", "seq"), None),
            P(("req", "seq"), None),
            P(("req", "seq"), None, None),
            P(("req", "seq"), None, None),
        ),
        out_specs=(
            P(("req", "seq"), None),
            P(("req", "seq"), None),
            P(("req", "seq"), None),
            P(("req", "seq"), None),
        ),
        check_vma=False,
    )
```

```python
import functools
import math

import jax
import jax.numpy as jnp
from jax import lax
from jax.experimental import pallas as pl
from jax.experimental.pallas import tpu as pltpu
from jax.sharding import PartitionSpec as P

HEADS = 24
KV_HEADS = 8
HEAD = 64
GROUP = HEADS // KV_HEADS
LANES = 128
PAIR = 2 * GROUP * HEAD

epsilon = 1e-06
residual_scale = 0.22
score_scale = 0.015625
rope_base = 10000.0
neg_big = -1e30

BOTH = ("req", "seq")


def vmem_spec():
    return pl.BlockSpec(memory_space=pltpu.VMEM)


def params(mebibytes):
    return pltpu.CompilerParams(vmem_limit_bytes=mebibytes * 2**20)


def qkv_kernel(own_ref, other_ref, gain_ref, cos_ref, sin_ref, w_ref, *refs):
    q_ref, kv_ref, kvo_ref, normed = refs[-4:]
    step = pl.program_id(0)
    rows = own_ref.shape[0]
    width = w_ref.shape[1]

    @pl.when(step == 0)
    def _():
        for index, ref in enumerate((own_ref, other_ref)):
            wide = ref[...].astype(jnp.float32)
            mean_square = jnp.mean(wide * wide, axis=-1, keepdims=True)
            normed[index * rows : (index + 1) * rows] = (
                wide * lax.rsqrt(mean_square + epsilon) * gain_ref[...][None, :]
            ).astype(jnp.bfloat16)

    def rotated(x, row_slice):
        lane = lax.broadcasted_iota(jnp.int32, x.shape, 1)
        low = (lane & (HEAD - 1)) < HEAD // 2
        swapped = jnp.where(
            low, pltpu.roll(x, width - HEAD // 2, 1), pltpu.roll(x, HEAD // 2, 1)
        )
        times = width // LANES
        cosine = jnp.concatenate([cos_ref[row_slice]] * times, axis=1)
        sine = jnp.concatenate([sin_ref[row_slice]] * times, axis=1)
        return x * cosine + swapped * sine

    @pl.when(step < 3)
    def _():
        x = jnp.dot(normed[:rows], w_ref[...], preferred_element_type=jnp.float32)
        q_ref[...] = (rotated(x, slice(0, rows)) * score_scale).astype(jnp.bfloat16)

    @pl.when(step == 3)
    def _():
        x = jnp.dot(normed[...], w_ref[...], preferred_element_type=jnp.float32)
        x = rotated(x, slice(0, 2 * rows)).astype(jnp.bfloat16)
        kv_ref[...] = x[:rows]
        kvo_ref[...] = x[rows:]

    @pl.when(step == 4)
    def _():
        x = jnp.dot(normed[...], w_ref[...], preferred_element_type=jnp.float32)
        x = x.astype(jnp.bfloat16)
        kv_ref[...] = x[:rows]
        kvo_ref[...] = x[rows:]


def project(own, other, gain, cosine, sine, w_qkv, after):
    rows, width = own.shape
    tile = KV_HEADS * HEAD
    return pl.pallas_call(
        qkv_kernel,
        grid=(5,),
        in_specs=[vmem_spec()] * 5
        + [pl.BlockSpec((width, tile), lambda i: (0, i))]
        + [pl.BlockSpec(memory_space=pl.ANY)] * len(after),
        out_specs=[
            pl.BlockSpec((rows, tile), lambda i: (0, jnp.minimum(i, 2))),
            pl.BlockSpec((rows, tile), lambda i: (0, jnp.maximum(i - 3, 0))),
            pl.BlockSpec((rows, tile), lambda i: (0, jnp.maximum(i - 3, 0))),
        ],
        out_shape=[
            jax.ShapeDtypeStruct((rows, HEADS * HEAD), jnp.bfloat16),
            jax.ShapeDtypeStruct((rows, 2 * tile), jnp.bfloat16),
            jax.ShapeDtypeStruct((rows, 2 * tile), jnp.bfloat16),
        ],
        scratch_shapes=[pltpu.VMEM((2 * rows, width), jnp.bfloat16)],
        compiler_params=params(24),
        cost_estimate=pl.CostEstimate(
            flops=2 * rows * width * 3584, bytes_accessed=9_500_000, transcendentals=0
        ),
        name="project_rows",
    )(own, other, gain, cosine, sine, w_qkv, *after)


def attend_kernel(first_row, extra, place_ref, q_ref, kc_ref, kco_ref, vc_ref, vco_ref, ks_ref, kso_ref, vs_ref, vso_ref, w_out_ref, tokens_ref, gain_ref, *refs):
    attended_ref, stream_ref, expert_in_ref, keys, values, wide_q, total = refs[extra:]
    step = pl.program_id(0)
    rows = q_ref.shape[0]
    cached = kc_ref.shape[1]
    span = ks_ref.shape[0]
    seq_index = place_ref[0]
    length = place_ref[1]

    @pl.when(step == 0)
    def _():
        position = lax.broadcasted_iota(jnp.int32, (cached, LANES), 0)
        for index, half in enumerate((seq_index, 1 - seq_index)):
            visible = position + half * cached < length
            keys[index * cached : (index + 1) * cached, LANES:] = jnp.where(
                visible, 0.0, neg_big
            ).astype(jnp.bfloat16)
        key = lax.broadcasted_iota(jnp.int32, (span, LANES), 0)
        row = lax.broadcasted_iota(jnp.int32, (span, LANES), 1)
        keys[2 * cached : 2 * cached + span, LANES:] = jnp.where(key <= row, 0.0, neg_big).astype(
            jnp.bfloat16
        )
        keys[2 * cached + span :, LANES:] = jnp.where(
            jnp.zeros((span, LANES), jnp.int32) < seq_index, 0.0, neg_big
        ).astype(jnp.bfloat16)
        values[:, LANES:] = jnp.ones((values.shape[0], LANES), jnp.bfloat16)
        row = lax.broadcasted_iota(jnp.int32, (rows, LANES), 0) + first_row
        lane = lax.broadcasted_iota(jnp.int32, (rows, LANES), 1)
        chosen = jnp.where(row == lane, 1.0, 0.0).astype(jnp.bfloat16)
        for head in range(2 * GROUP):
            wide_q[head * rows : (head + 1) * rows, LANES:] = chosen

    for ref, parts in ((keys, (kc_ref, kco_ref)), (values, (vc_ref, vco_ref))):
        for index, part in enumerate(parts):
            ref[index * cached : (index + 1) * cached, :LANES] = part[0]
    for ref, parts in ((keys, (ks_ref, kso_ref)), (values, (vs_ref, vso_ref))):
        for index, part in enumerate(parts):
            start = 2 * cached + index * span
            ref[start : start + span, :LANES] = part[...]

    low = lax.broadcasted_iota(jnp.int32, (rows, LANES), 1) < HEAD
    tiles = [q_ref[:, i * LANES : (i + 1) * LANES].astype(jnp.float32) for i in range(3)]
    parts = [
        jnp.where(low, tiles[0], 0.0),
        jnp.where(low, pltpu.roll(tiles[0], HEAD, 1), 0.0),
        jnp.where(low, tiles[1], 0.0),
        jnp.where(low, 0.0, tiles[1]),
        jnp.where(low, 0.0, pltpu.roll(tiles[2], HEAD, 1)),
        jnp.where(low, 0.0, tiles[2]),
    ]
    for head, part in enumerate(parts):
        wide_q[head * rows : (head + 1) * rows, :LANES] = part.astype(jnp.bfloat16)

    heads = []
    batch = GROUP * rows
    for first in range(0, 2 * GROUP * rows, batch):
        scores = lax.dot_general(
            wide_q[first : first + batch],
            keys[...],
            (((1,), (1,)), ((), ())),
            preferred_element_type=jnp.float32,
        )
        best = jnp.max(scores, axis=-1, keepdims=True)
        weights = jnp.exp(scores - best).astype(jnp.bfloat16)
        sums = jnp.dot(weights, values[...], preferred_element_type=jnp.float32)
        mean = sums[:, :LANES] / sums[:, LANES:]
        heads += [mean[i : i + rows] for i in range(0, batch, rows)]
    merged = jnp.concatenate(
        [
            jnp.where(low, heads[0], pltpu.roll(heads[1], HEAD, 1)),
            jnp.where(low, heads[2], heads[3]),
            jnp.where(low, pltpu.roll(heads[4], HEAD, 1), heads[5]),
        ],
        axis=1,
    ).astype(jnp.bfloat16)
    attended_ref[...] = merged
    product = jnp.dot(merged, w_out_ref[...], preferred_element_type=jnp.float32)

    @pl.when(step == 0)
    def _():
        total[...] = product

    @pl.when(step > 0)
    def _():
        total[...] += product

    @pl.when(step == pl.num_programs(0) - 1)
    def _():
        stream = (tokens_ref[...].astype(jnp.float32) + residual_scale * total[...]).astype(
            jnp.bfloat16
        )
        stream_ref[...] = stream
        wide = stream.astype(jnp.float32)
        mean_square = jnp.mean(wide * wide, axis=-1, keepdims=True)
        expert_in_ref[...] = (wide * lax.rsqrt(mean_square + epsilon) * gain_ref[...][None, :]).astype(
            jnp.bfloat16
        )


def attend(place, queries, caches, spans, w_out, tokens, gain, first_row, rows, filled, after):
    k_cache, k_other, v_cache, v_other = caches
    own_span, other_span = spans
    cached = k_cache.shape[1]
    span, width = tokens.shape
    pairs = KV_HEADS // 2
    part = first_row // rows
    key_count = 2 * cached + 2 * span
    cache_spec = pl.BlockSpec((1, cached, LANES), lambda j: (0, 0, j))
    key_spec = pl.BlockSpec((span, LANES), lambda j: (0, j))
    value_spec = pl.BlockSpec((span, LANES), lambda j: (0, pairs + j))
    extra = [*filled, *after]
    return pl.pallas_call(
        functools.partial(attend_kernel, first_row, len(extra)),
        grid=(pairs,),
        in_specs=[
            pl.BlockSpec(memory_space=pltpu.SMEM),
            pl.BlockSpec((rows, PAIR), lambda j: (part, j)),
            cache_spec,
            cache_spec,
            cache_spec,
            cache_spec,
            key_spec,
            key_spec,
            value_spec,
            value_spec,
            pl.BlockSpec((PAIR, width), lambda j: (j, 0)),
            pl.BlockSpec((rows, width), lambda j: (part, 0)),
            vmem_spec(),
        ]
        + [pl.BlockSpec(memory_space=pl.ANY)] * len(extra),
        out_specs=[
            pl.BlockSpec((rows, PAIR), lambda j: (part, j)),
            pl.BlockSpec((rows, width), lambda j: (part, 0)),
            pl.BlockSpec((rows, width), lambda j: (0, 0)),
        ],
        out_shape=[
            jax.ShapeDtypeStruct((span, HEADS * HEAD), jnp.bfloat16),
            jax.ShapeDtypeStruct((span, width), jnp.bfloat16),
            jax.ShapeDtypeStruct((rows, width), jnp.bfloat16),
        ],
        input_output_aliases={13 + i: i for i in range(len(filled))},
        scratch_shapes=[
            pltpu.VMEM((key_count, 2 * LANES), jnp.bfloat16),
            pltpu.VMEM((key_count, 2 * LANES), jnp.bfloat16),
            pltpu.VMEM((2 * GROUP * rows, 2 * LANES), jnp.bfloat16),
            pltpu.VMEM((rows, width), jnp.float32),
        ],
        compiler_params=params(40),
        cost_estimate=pl.CostEstimate(
            flops=16 * HEADS * rows * key_count * LANES,
            bytes_accessed=10_000_000,
            transcendentals=HEADS * rows * key_count,
        ),
        name="attend_rows",
    )(
        place,
        queries,
        k_cache,
        k_other,
        v_cache,
        v_other,
        own_span,
        other_span,
        own_span,
        other_span,
        w_out,
        tokens,
        gain,
        *extra,
    )


def plan_kernel(groups, capacity, top, slot_ref, chip_ref, table_ref, *out_refs):
    slots = slot_ref.shape[0]
    chips, _, tokens = table_ref.shape
    in_group = chips // groups
    earlier = jnp.where(
        lax.broadcasted_iota(jnp.int32, (tokens, tokens), 0)
        < lax.broadcasted_iota(jnp.int32, (tokens, tokens), 1),
        1.0,
        0.0,
    ).astype(jnp.bfloat16)
    place = lax.broadcasted_iota(jnp.int32, (capacity, tokens), 0).astype(jnp.float32)
    for group in range(groups):
        pick_ref, back_ref, share_ref = out_refs[3 * group : 3 * group + 3]
        hot_rows, share_lines = [], []
        for source in range(in_group):
            entry = table_ref[chip_ref[group * in_group + source]]
            for slot in range(slots):
                match = entry[:top] == slot_ref[slot].astype(jnp.float32)
                hot_rows.append(jnp.max(jnp.where(match, 1.0, 0.0), axis=0, keepdims=True))
                share_lines.append(
                    jnp.sum(jnp.where(match, entry[top : 2 * top], 0.0), axis=0, keepdims=True)
                )
        hot = jnp.concatenate(hot_rows, axis=0)
        rank = jnp.dot(hot.astype(jnp.bfloat16), earlier, preferred_element_type=jnp.float32)
        rank = jnp.where(hot > 0.0, rank, -1.0)
        for source in range(in_group):
            picks = []
            for slot in range(slots):
                line = source * slots + slot
                chosen = jnp.where(place == rank[line : line + 1], 1.0, 0.0)
                share_ref[slot, source * capacity : (source + 1) * capacity] = jnp.sum(
                    chosen * share_lines[line], axis=1, keepdims=True
                )
                picks.append(chosen)
            picked = jnp.concatenate(picks, axis=0)
            pick_ref[source] = picked.astype(jnp.bfloat16)
            back_ref[source] = jnp.transpose(picked).astype(jnp.bfloat16)


def plan_routes(slot_ids, chip_ids, tables, groups, capacity, top):
    chips, _, tokens = tables.shape
    slots = slot_ids.shape[0]
    in_group = chips // groups
    flat = pl.pallas_call(
        functools.partial(plan_kernel, groups, capacity, top),
        in_specs=[pl.BlockSpec(memory_space=pltpu.SMEM)] * 2 + [vmem_spec()],
        out_specs=[vmem_spec()] * (3 * groups),
        out_shape=[
            jax.ShapeDtypeStruct((in_group, slots * capacity, tokens), jnp.bfloat16),
            jax.ShapeDtypeStruct((in_group, tokens, slots * capacity), jnp.bfloat16),
            jax.ShapeDtypeStruct((slots, in_group * capacity, 1), jnp.float32),
        ]
        * groups,
        compiler_params=params(24),
        cost_estimate=pl.CostEstimate(
            flops=5_000_000_000, bytes_accessed=2_000_000, transcendentals=0
        ),
        name="plan_routes",
    )(slot_ids, chip_ids, tables)
    return [flat[3 * i : 3 * i + 3] for i in range(groups)]


def expert_kernel(pieces, halves, out_cuts, extra, *refs):
    row_refs = refs[: pieces * halves]
    rest = refs[pieces * halves :]
    pick_ref, back_ref, share_ref, up_ref, up_other_ref, down_ref, down_other_ref = rest[:7]
    out_refs = rest[7 + extra : 7 + extra + pieces * len(out_cuts)]
    held = rest[-1]
    step = pl.program_id(0)
    slots = held.shape[0]
    own_slots = slots // 2
    sources = pick_ref.shape[0]
    deep = sources // pieces
    capacity = held.shape[1] // sources
    hidden = down_ref.shape[1]

    @pl.when(step == 0)
    def _():
        for source in range(sources):
            piece = source // deep
            rows = jnp.concatenate(
                [ref[source % deep] for ref in row_refs[piece * halves : (piece + 1) * halves]],
                axis=0,
            )
            rows = jnp.dot(
                pick_ref[source], rows, preferred_element_type=jnp.float32
            ).astype(jnp.bfloat16)
            for slot in range(slots):
                held[slot, source * capacity : (source + 1) * capacity] = rows[
                    slot * capacity : (slot + 1) * capacity
                ]

    def run(up, down):
        gate_up = jnp.dot(held[step], up[0], preferred_element_type=jnp.float32)
        active = (
            jax.nn.silu(gate_up[:, :hidden]) * gate_up[:, hidden:] * share_ref[step]
        ).astype(jnp.bfloat16)
        held[step] = jnp.dot(active, down[0], preferred_element_type=jnp.float32).astype(
            jnp.bfloat16
        )

    @pl.when(step < own_slots)
    def _():
        run(up_ref, down_ref)

    @pl.when(step >= own_slots)
    def _():
        run(up_other_ref, down_other_ref)

    @pl.when(step == slots - 1)
    def _():
        for source in range(sources):
            rows = jnp.concatenate(
                [
                    held[slot, source * capacity : (source + 1) * capacity]
                    for slot in range(slots)
                ],
                axis=0,
            )
            mixed = jnp.dot(back_ref[source], rows, preferred_element_type=jnp.float32)
            start = 0
            for index, count in enumerate(out_cuts):
                ref = out_refs[source // deep * len(out_cuts) + index]
                ref[source % deep] = mixed[start : start + count].astype(jnp.bfloat16)
                start += count


def run_experts(rows, plan, ups, downs, out_cuts, after):
    pieces, halves = len(rows), len(rows[0])
    deep, _, width = rows[0][0].shape
    own_slots, _, double = ups[0].shape
    hidden = double // 2
    slots = 2 * own_slots
    places = plan[2].shape[1]

    def own(j):
        return (jnp.minimum(j, own_slots - 1), 0, 0)

    def other(j):
        return (jnp.maximum(j - own_slots, 0), 0, 0)

    flat = pl.pallas_call(
        functools.partial(expert_kernel, pieces, halves, tuple(out_cuts), len(after)),
        grid=(slots,),
        in_specs=[vmem_spec()] * (pieces * halves + 3)
        + [
            pl.BlockSpec((1, width, double), own),
            pl.BlockSpec((1, width, double), other),
            pl.BlockSpec((1, hidden, width), own),
            pl.BlockSpec((1, hidden, width), other),
        ]
        + [pl.BlockSpec(memory_space=pl.ANY)] * len(after),
        out_specs=[vmem_spec()] * (pieces * len(out_cuts)),
        out_shape=[jax.ShapeDtypeStruct((deep, c, width), jnp.bfloat16) for c in out_cuts]
        * pieces,
        scratch_shapes=[pltpu.VMEM((slots, places, width), jnp.bfloat16)],
        compiler_params=params(44),
        cost_estimate=pl.CostEstimate(
            flops=10 * slots * places * width * hidden,
            bytes_accessed=26_000_000,
            transcendentals=slots * places * hidden,
        ),
        name="run_experts",
    )(*[r for piece in rows for r in piece], *plan, ups[0], ups[1], downs[0], downs[1], *after)
    count = len(out_cuts)
    return [flat[i * count : (i + 1) * count] for i in range(pieces)]


def stack_kernel(count, *refs):
    out_ref = refs[-1]
    for index in range(count):
        out_ref[index] = refs[index][...]


def stack_rows(parts, after):
    return pl.pallas_call(
        functools.partial(stack_kernel, len(parts)),
        in_specs=[vmem_spec()] * len(parts) + [pl.BlockSpec(memory_space=pl.ANY)] * len(after),
        out_specs=vmem_spec(),
        out_shape=jax.ShapeDtypeStruct((len(parts), *parts[0].shape), parts[0].dtype),
        compiler_params=params(16),
        name="stack_rows",
    )(*parts, *after)


def chip_shape(chips):
    depth = 4 if chips % 4 == 0 else 1
    plane = chips // depth
    side = math.isqrt(plane)
    while plane % side:
        side -= 1
    return depth, plane // side, side


def make_shift(chips, cores):
    depth, tall, wide = chip_shape(chips)
    swap = tall == wide
    sizes = {"z": depth, "a": tall, "b": wide}

    def pairs(role, offset):
        out = []
        for z in range(depth):
            for y in range(tall):
                for x in range(wide):
                    for core in range(cores):
                        axis = role
                        if swap and core % 2 == 1:
                            axis = {"z": "z", "a": "b", "b": "a"}[role]
                        to_z, to_y, to_x = z, y, x
                        if axis == "z":
                            to_z = (z + offset) % depth
                        elif axis == "a":
                            to_y = (y + offset) % tall
                        else:
                            to_x = (x + offset) % wide
                        source = ((z * tall + y) * wide + x) * cores + core
                        target = ((to_z * tall + to_y) * wide + to_x) * cores + core
                        out.append((source, target))
        return out

    def shift(value, role, offset):
        return lax.ppermute(value, BOTH, pairs(role, offset % sizes[role]))

    return shift, sizes


def gather_line(value, shift, sizes):
    return [value] + [shift(value, "z", k) for k in range(1, sizes["z"])]


def gather_planes(line, shift, sizes):
    plane = [line] + [shift(line, "a", j) for j in range(1, sizes["a"])]
    return [plane] + [[shift(v, "b", k) for v in plane] for k in range(1, sizes["b"])]


def add_all(terms):
    total = terms[0].astype(jnp.float32)
    for term in terms[1:]:
        total = total + term.astype(jnp.float32)
    return total.astype(terms[0].dtype)


def scatter_planes(planes, shift, sizes):
    tall = sizes["a"]
    arrived = {}
    for j in range(tall - 1, -1, -1):
        arrived[j] = [planes[0][j]] + [shift(planes[k][j], "b", -k) for k in range(1, sizes["b"])]
    line = [shift(add_all(arrived[j]), "a", -j) for j in range(1, tall)] + arrived[0]
    moved = [
        shift(add_all([t[i] for t in line]), "z", -i) for i in range(1, sizes["z"])
    ]
    return add_all([t[0] for t in line] + moved)


def source_chips(chip, core, chips):
    depth, tall, wide = chip_shape(chips)
    index = jnp.arange(chips, dtype=jnp.int32)
    back_z, back_a, back_b = index % depth, index // depth % tall, index // (depth * tall)
    back_y, back_x = back_a, back_b
    if tall == wide:
        back_y = jnp.where(core == 0, back_a, back_b)
        back_x = jnp.where(core == 0, back_b, back_a)
    z, y, x = chip // (tall * wide), chip // wide % tall, chip % wide
    z, y, x = (z - back_z) % depth, (y - back_y) % tall, (x - back_x) % wide
    return ((z * tall + y) * wide + x).astype(jnp.int32)


def rope_tables(positions):
    half = HEAD // 2
    frequency = rope_base ** (-jnp.arange(half, dtype=jnp.float32) / half)
    angles = positions.astype(jnp.float32)[:, None] * frequency[None, :]
    cosine, sine = jnp.cos(angles), jnp.sin(angles)
    return (
        jnp.concatenate([cosine] * 4, axis=1),
        jnp.concatenate([-sine, sine, -sine, sine], axis=1),
    )


def shards(
    tokens,
    attn_gain,
    w_qkv,
    w_out,
    k_cache,
    v_cache,
    cache_len,
    ffn_gain,
    routes,
    route_scores,
    replica_slot,
    expert_up,
    expert_down,
):
    row_count, top_count = routes.shape
    chips, cores = lax.axis_size("req"), lax.axis_size("seq")
    seq_index = lax.axis_index("seq")
    length = cache_len[0]
    slots_dev = expert_up.shape[0]
    slot_total = chips * cores * slots_dev
    capacity = 2 * ((row_count * top_count + slot_total - 1) // slot_total)
    shift, sizes = make_shift(chips, cores)

    def swap(value):
        return lax.ppermute(value, "seq", [(0, 1), (1, 0)])

    other_tokens = swap(tokens)
    k_other, v_other = swap(k_cache), swap(v_cache)
    experts = jnp.arange(replica_slot.shape[1], dtype=jnp.int32)
    slot_of = jnp.sum(
        jnp.where(routes[:, :, None] == experts, replica_slot[:, None, :], 0), axis=2
    )
    shares = route_scores / jnp.sum(route_scores, axis=1, keepdims=True)
    table = jnp.concatenate([slot_of.astype(jnp.float32), shares], axis=1).T
    table = jnp.pad(table, ((0, row_count - table.shape[0]), (0, 0)))
    tables = lax.all_gather(table, "req", axis=0)
    chip = lax.axis_index("req")
    chip_slots = jnp.arange(slots_dev, dtype=jnp.int32)
    slot_ids = jnp.concatenate(
        [
            (chip * cores + seq_index) * slots_dev + chip_slots,
            (chip * cores + 1 - seq_index) * slots_dev + chip_slots,
        ]
    ).astype(jnp.int32)
    plans = plan_routes(slot_ids, source_chips(chip, seq_index, chips), tables, sizes["b"], capacity, top_count)

    row_index = jnp.arange(row_count, dtype=jnp.int32)
    cosine, sine = rope_tables(
        length
        + jnp.concatenate(
            [seq_index * row_count + row_index, (1 - seq_index) * row_count + row_index]
        )
    )
    queries, appended, other_span = project(
        tokens, other_tokens, attn_gain, cosine, sine, w_qkv, [k_other, v_other]
    )
    place = jnp.stack([seq_index, length]).astype(jnp.int32)
    later_up, later_down, _ = lax.optimization_barrier((expert_up, expert_down, appended))
    up_other, down_other = swap(later_up), swap(later_down)
    half = row_count // 2
    filled, lines = [], []
    for index in range(2):
        attended, stream, expert_in = attend(
            place,
            queries,
            (k_cache, k_other, v_cache, v_other),
            (appended, other_span),
            w_out,
            tokens,
            ffn_gain,
            index * half,
            half,
            filled,
            [up_other, down_other] if index else [],
        )
        filled = [attended, stream]
        lines.append(gather_line(expert_in, shift, sizes))
    halves = [gather_planes(stack_rows(line, [expert_in]), shift, sizes) for line in lines]
    cut = row_count // 2
    results = []
    for index in range(sizes["b"]):
        results.append(
            run_experts(
                [[planes[index][j] for planes in halves] for j in range(sizes["a"])],
                plans[index],
                (expert_up, up_other),
                (expert_down, down_other),
                (cut, row_count - cut),
                results[-1][0][:1] if results else [],
            )
        )
    expert_mix = jnp.concatenate(
        [
            scatter_planes([[piece[i] for piece in r] for r in results], shift, sizes)
            for i in range(2)
        ],
        axis=0,
    )
    return (attended, stream, expert_mix, appended)


def solution(mesh):
    return jax.shard_map(
        shards,
        mesh=mesh,
        in_specs=(
            P(("req", "seq"), None),
            P(),
            P(),
            P(),
            P("req", "seq", None),
            P("req", "seq", None),
            P("req"),
            P(),
            P(("req", "seq"), None),
            P(("req", "seq"), None),
            P(("req", "seq"), None),
            P(("req", "seq"), None, None),
            P(("req", "seq"), None, None),
        ),
        out_specs=(
            P(("req", "seq"), None),
            P(("req", "seq"), None),
            P(("req", "seq"), None),
            P(("req", "seq"), None),
        ),
        check_vma=False,
    )
```

```python
import functools
import math

import jax
import jax.numpy as jnp
from jax import lax
from jax.experimental import pallas as pl
from jax.experimental.pallas import tpu as pltpu
from jax.sharding import PartitionSpec as P

HEADS = 24
KV_HEADS = 8
HEAD = 64
GROUP = HEADS // KV_HEADS
LANES = 128
PAIR = 2 * GROUP * HEAD

epsilon = 1e-06
residual_scale = 0.22
score_scale = 0.015625
rope_base = 10000.0
neg_big = -1e30

BOTH = ("req", "seq")


def vmem_spec():
    return pl.BlockSpec(memory_space=pltpu.VMEM)


def params(mebibytes):
    return pltpu.CompilerParams(vmem_limit_bytes=mebibytes * 2**20)


def qkv_kernel(own_ref, other_ref, gain_ref, cos_ref, sin_ref, w_ref, *refs):
    q_ref, kv_ref, kvo_ref, normed = refs[-4:]
    step = pl.program_id(0)
    rows = own_ref.shape[0]
    width = w_ref.shape[1]

    @pl.when(step == 0)
    def _():
        for index, ref in enumerate((own_ref, other_ref)):
            wide = ref[...].astype(jnp.float32)
            mean_square = jnp.mean(wide * wide, axis=-1, keepdims=True)
            normed[index * rows : (index + 1) * rows] = (
                wide * lax.rsqrt(mean_square + epsilon) * gain_ref[...][None, :]
            ).astype(jnp.bfloat16)

    def rotated(x, row_slice):
        lane = lax.broadcasted_iota(jnp.int32, x.shape, 1)
        low = (lane & (HEAD - 1)) < HEAD // 2
        swapped = jnp.where(
            low, pltpu.roll(x, width - HEAD // 2, 1), pltpu.roll(x, HEAD // 2, 1)
        )
        times = width // LANES
        cosine = jnp.concatenate([cos_ref[row_slice]] * times, axis=1)
        sine = jnp.concatenate([sin_ref[row_slice]] * times, axis=1)
        return x * cosine + swapped * sine

    @pl.when(step < 3)
    def _():
        x = jnp.dot(normed[:rows], w_ref[...], preferred_element_type=jnp.float32)
        q_ref[...] = (rotated(x, slice(0, rows)) * score_scale).astype(jnp.bfloat16)

    @pl.when(step == 3)
    def _():
        x = jnp.dot(normed[...], w_ref[...], preferred_element_type=jnp.float32)
        x = rotated(x, slice(0, 2 * rows)).astype(jnp.bfloat16)
        kv_ref[...] = x[:rows]
        kvo_ref[...] = x[rows:]

    @pl.when(step == 4)
    def _():
        x = jnp.dot(normed[...], w_ref[...], preferred_element_type=jnp.float32)
        x = x.astype(jnp.bfloat16)
        kv_ref[...] = x[:rows]
        kvo_ref[...] = x[rows:]


def project(own, other, gain, cosine, sine, w_qkv, after):
    rows, width = own.shape
    tile = KV_HEADS * HEAD
    return pl.pallas_call(
        qkv_kernel,
        grid=(5,),
        in_specs=[vmem_spec()] * 5
        + [pl.BlockSpec((width, tile), lambda i: (0, i))]
        + [pl.BlockSpec(memory_space=pl.ANY)] * len(after),
        out_specs=[
            pl.BlockSpec((rows, tile), lambda i: (0, jnp.minimum(i, 2))),
            pl.BlockSpec((rows, tile), lambda i: (0, jnp.maximum(i - 3, 0))),
            pl.BlockSpec((rows, tile), lambda i: (0, jnp.maximum(i - 3, 0))),
        ],
        out_shape=[
            jax.ShapeDtypeStruct((rows, HEADS * HEAD), jnp.bfloat16),
            jax.ShapeDtypeStruct((rows, 2 * tile), jnp.bfloat16),
            jax.ShapeDtypeStruct((rows, 2 * tile), jnp.bfloat16),
        ],
        scratch_shapes=[pltpu.VMEM((2 * rows, width), jnp.bfloat16)],
        compiler_params=params(58),
        cost_estimate=pl.CostEstimate(
            flops=2 * rows * width * 3584, bytes_accessed=9_500_000, transcendentals=0
        ),
        name="project_rows",
    )(own, other, gain, cosine, sine, w_qkv, *after)


def attend_kernel(first_row, riders, extra, place_ref, q_ref, kc_ref, kco_ref, vc_ref, vco_ref, ks_ref, kso_ref, vs_ref, vso_ref, w_out_ref, tokens_ref, gain_ref, *refs):
    attended_ref, stream_ref, expert_in_ref, keys, values, wide_q, total = refs[riders + extra :]
    step = pl.program_id(0)
    rows = q_ref.shape[0]
    cached = kc_ref.shape[1]
    span = ks_ref.shape[0]
    seq_index = place_ref[0]
    length = place_ref[1]

    @pl.when(step == 0)
    def _():
        position = lax.broadcasted_iota(jnp.int32, (cached, LANES), 0)
        for index, half in enumerate((seq_index, 1 - seq_index)):
            visible = position + half * cached < length
            keys[index * cached : (index + 1) * cached, LANES:] = jnp.where(
                visible, 0.0, neg_big
            ).astype(jnp.bfloat16)
        key = lax.broadcasted_iota(jnp.int32, (span, LANES), 0)
        row = lax.broadcasted_iota(jnp.int32, (span, LANES), 1)
        keys[2 * cached : 2 * cached + span, LANES:] = jnp.where(key <= row, 0.0, neg_big).astype(
            jnp.bfloat16
        )
        keys[2 * cached + span :, LANES:] = jnp.where(
            jnp.zeros((span, LANES), jnp.int32) < seq_index, 0.0, neg_big
        ).astype(jnp.bfloat16)
        values[:, LANES:] = jnp.ones((values.shape[0], LANES), jnp.bfloat16)
        row = lax.broadcasted_iota(jnp.int32, (rows, LANES), 0) + first_row
        lane = lax.broadcasted_iota(jnp.int32, (rows, LANES), 1)
        chosen = jnp.where(row == lane, 1.0, 0.0).astype(jnp.bfloat16)
        for head in range(2 * GROUP):
            wide_q[head * rows : (head + 1) * rows, LANES:] = chosen

    for ref, parts in ((keys, (kc_ref, kco_ref)), (values, (vc_ref, vco_ref))):
        for index, part in enumerate(parts):
            ref[index * cached : (index + 1) * cached, :LANES] = part[0]
    for ref, parts in ((keys, (ks_ref, kso_ref)), (values, (vs_ref, vso_ref))):
        for index, part in enumerate(parts):
            start = 2 * cached + index * span
            ref[start : start + span, :LANES] = part[...]

    low = lax.broadcasted_iota(jnp.int32, (rows, LANES), 1) < HEAD
    tiles = [q_ref[:, i * LANES : (i + 1) * LANES].astype(jnp.float32) for i in range(3)]
    parts = [
        jnp.where(low, tiles[0], 0.0),
        jnp.where(low, pltpu.roll(tiles[0], HEAD, 1), 0.0),
        jnp.where(low, tiles[1], 0.0),
        jnp.where(low, 0.0, tiles[1]),
        jnp.where(low, 0.0, pltpu.roll(tiles[2], HEAD, 1)),
        jnp.where(low, 0.0, tiles[2]),
    ]
    for head, part in enumerate(parts):
        wide_q[head * rows : (head + 1) * rows, :LANES] = part.astype(jnp.bfloat16)

    heads = []
    batch = GROUP * rows
    for first in range(0, 2 * GROUP * rows, batch):
        scores = lax.dot_general(
            wide_q[first : first + batch],
            keys[...],
            (((1,), (1,)), ((), ())),
            preferred_element_type=jnp.float32,
        )
        best = jnp.max(scores, axis=-1, keepdims=True)
        weights = jnp.exp(scores - best).astype(jnp.bfloat16)
        sums = jnp.dot(weights, values[...], preferred_element_type=jnp.float32)
        mean = sums[:, :LANES] / sums[:, LANES:]
        heads += [mean[i : i + rows] for i in range(0, batch, rows)]
    merged = jnp.concatenate(
        [
            jnp.where(low, heads[0], pltpu.roll(heads[1], HEAD, 1)),
            jnp.where(low, heads[2], heads[3]),
            jnp.where(low, pltpu.roll(heads[4], HEAD, 1), heads[5]),
        ],
        axis=1,
    ).astype(jnp.bfloat16)
    attended_ref[...] = merged
    product = jnp.dot(merged, w_out_ref[...], preferred_element_type=jnp.float32)

    @pl.when(step == 0)
    def _():
        total[...] = product

    @pl.when(step > 0)
    def _():
        total[...] += product

    @pl.when(step == pl.num_programs(0) - 1)
    def _():
        stream = (tokens_ref[...].astype(jnp.float32) + residual_scale * total[...]).astype(
            jnp.bfloat16
        )
        stream_ref[...] = stream
        wide = stream.astype(jnp.float32)
        mean_square = jnp.mean(wide * wide, axis=-1, keepdims=True)
        expert_in_ref[:rows] = (
            wide * lax.rsqrt(mean_square + epsilon) * gain_ref[...][None, :]
        ).astype(jnp.bfloat16)
        if riders:
            expert_in_ref[rows:] = refs[0][...]


def attend(place, queries, caches, spans, w_out, tokens, gain, first_row, rows, riders, filled, after):
    k_cache, k_other, v_cache, v_other = caches
    own_span, other_span = spans
    cached = k_cache.shape[1]
    span, width = tokens.shape
    pairs = KV_HEADS // 2
    part = first_row // rows
    key_count = 2 * cached + 2 * span
    cache_spec = pl.BlockSpec((1, cached, LANES), lambda j: (0, 0, j))
    key_spec = pl.BlockSpec((span, LANES), lambda j: (0, j))
    value_spec = pl.BlockSpec((span, LANES), lambda j: (0, pairs + j))
    extra = [*filled, *after]
    sent = rows + sum(r.shape[0] for r in riders)
    return pl.pallas_call(
        functools.partial(attend_kernel, first_row, len(riders), len(extra)),
        grid=(pairs,),
        in_specs=[
            pl.BlockSpec(memory_space=pltpu.SMEM),
            pl.BlockSpec((rows, PAIR), lambda j: (part, j)),
            cache_spec,
            cache_spec,
            cache_spec,
            cache_spec,
            key_spec,
            key_spec,
            value_spec,
            value_spec,
            pl.BlockSpec((PAIR, width), lambda j: (j, 0)),
            pl.BlockSpec((rows, width), lambda j: (part, 0)),
            vmem_spec(),
        ]
        + [vmem_spec()] * len(riders)
        + [pl.BlockSpec(memory_space=pl.ANY)] * len(extra),
        out_specs=[
            pl.BlockSpec((rows, PAIR), lambda j: (part, j)),
            pl.BlockSpec((rows, width), lambda j: (part, 0)),
            pl.BlockSpec((sent, width), lambda j: (0, 0)),
        ],
        out_shape=[
            jax.ShapeDtypeStruct((span, HEADS * HEAD), jnp.bfloat16),
            jax.ShapeDtypeStruct((span, width), jnp.bfloat16),
            jax.ShapeDtypeStruct((sent, width), jnp.bfloat16),
        ],
        input_output_aliases={13 + len(riders) + i: i for i in range(len(filled))},
        scratch_shapes=[
            pltpu.VMEM((key_count, 2 * LANES), jnp.bfloat16),
            pltpu.VMEM((key_count, 2 * LANES), jnp.bfloat16),
            pltpu.VMEM((2 * GROUP * rows, 2 * LANES), jnp.bfloat16),
            pltpu.VMEM((rows, width), jnp.float32),
        ],
        compiler_params=params(58),
        cost_estimate=pl.CostEstimate(
            flops=16 * HEADS * rows * key_count * LANES,
            bytes_accessed=10_000_000,
            transcendentals=HEADS * rows * key_count,
        ),
        name="attend_rows",
    )(
        place,
        queries,
        k_cache,
        k_other,
        v_cache,
        v_other,
        own_span,
        other_span,
        own_span,
        other_span,
        w_out,
        tokens,
        gain,
        *riders,
        *extra,
    )


def plan_kernel(pieces, first, capacity, top, slot_ref, *refs):
    pick_ref, back_ref, share_ref = refs[pieces:]
    slots = slot_ref.shape[0]
    sources, _, tokens = pick_ref.shape
    deep = sources // pieces
    earlier = jnp.where(
        lax.broadcasted_iota(jnp.int32, (tokens, tokens), 0)
        < lax.broadcasted_iota(jnp.int32, (tokens, tokens), 1),
        1.0,
        0.0,
    ).astype(jnp.bfloat16)
    place = lax.broadcasted_iota(jnp.int32, (capacity, tokens), 0).astype(jnp.float32)
    hot_rows, share_lines = [], []
    for source in range(sources):
        packed = refs[source // deep][source % deep, first:].astype(jnp.float32)
        across = packed.shape[1] // tokens
        lines = [
            packed[i // across : i // across + 1, i % across * tokens : (i % across + 1) * tokens]
            for i in range(3 * top)
        ]
        ids = jnp.concatenate(lines[:top], axis=0)
        shares = jnp.concatenate(lines[top : 2 * top], axis=0)
        shares += jnp.concatenate(lines[2 * top :], axis=0)
        for slot in range(slots):
            match = ids == slot_ref[slot].astype(jnp.float32)
            hot_rows.append(jnp.max(jnp.where(match, 1.0, 0.0), axis=0, keepdims=True))
            share_lines.append(jnp.sum(jnp.where(match, shares, 0.0), axis=0, keepdims=True))
    hot = jnp.concatenate(hot_rows, axis=0)
    rank = jnp.dot(hot.astype(jnp.bfloat16), earlier, preferred_element_type=jnp.float32)
    rank = jnp.where(hot > 0.0, rank, -1.0)
    for source in range(sources):
        picks = []
        for slot in range(slots):
            line = source * slots + slot
            chosen = jnp.where(place == rank[line : line + 1], 1.0, 0.0)
            share_ref[slot, source * capacity : (source + 1) * capacity] = jnp.sum(
                chosen * share_lines[line], axis=1, keepdims=True
            )
            picks.append(chosen)
        picked = jnp.concatenate(picks, axis=0)
        pick_ref[source] = picked.astype(jnp.bfloat16)
        back_ref[source] = jnp.transpose(picked).astype(jnp.bfloat16)


def plan_routes(slot_ids, pieces, first, tokens, capacity, top):
    slots = slot_ids.shape[0]
    sources = sum(p.shape[0] for p in pieces)
    return pl.pallas_call(
        functools.partial(plan_kernel, len(pieces), first, capacity, top),
        in_specs=[pl.BlockSpec(memory_space=pltpu.SMEM)] + [vmem_spec()] * len(pieces),
        out_specs=[vmem_spec()] * 3,
        out_shape=[
            jax.ShapeDtypeStruct((sources, slots * capacity, tokens), jnp.bfloat16),
            jax.ShapeDtypeStruct((sources, tokens, slots * capacity), jnp.bfloat16),
            jax.ShapeDtypeStruct((slots, sources * capacity, 1), jnp.float32),
        ],
        compiler_params=params(24),
        cost_estimate=pl.CostEstimate(
            flops=1_000_000_000, bytes_accessed=2_000_000, transcendentals=0
        ),
        name="plan_routes",
    )(slot_ids, *pieces)


def expert_kernel(pieces, in_cuts, out_cuts, extra, *refs):
    halves = len(in_cuts)
    row_refs = refs[: pieces * halves]
    rest = refs[pieces * halves :]
    pick_ref, back_ref, share_ref, up_ref, up_other_ref, down_ref, down_other_ref = rest[:7]
    out_refs = rest[7 + extra : 7 + extra + pieces * len(out_cuts)]
    held = rest[-1]
    step = pl.program_id(0)
    slots = held.shape[0]
    own_slots = slots // 2
    sources = pick_ref.shape[0]
    deep = sources // pieces
    capacity = held.shape[1] // sources
    hidden = down_ref.shape[1]

    @pl.when(step == 0)
    def _():
        for source in range(sources):
            piece = source // deep
            rows = jnp.concatenate(
                [
                    row_refs[piece * halves + index][source % deep, :count]
                    for index, count in enumerate(in_cuts)
                ],
                axis=0,
            )
            rows = jnp.dot(
                pick_ref[source], rows, preferred_element_type=jnp.float32
            ).astype(jnp.bfloat16)
            for slot in range(slots):
                held[slot, source * capacity : (source + 1) * capacity] = rows[
                    slot * capacity : (slot + 1) * capacity
                ]

    def run(up, down):
        gate_up = jnp.dot(held[step], up[0], preferred_element_type=jnp.float32)
        active = (
            jax.nn.silu(gate_up[:, :hidden]) * gate_up[:, hidden:] * share_ref[step]
        ).astype(jnp.bfloat16)
        held[step] = jnp.dot(active, down[0], preferred_element_type=jnp.float32).astype(
            jnp.bfloat16
        )

    @pl.when(step < own_slots)
    def _():
        run(up_ref, down_ref)

    @pl.when(step >= own_slots)
    def _():
        run(up_other_ref, down_other_ref)

    @pl.when(step == slots - 1)
    def _():
        for source in range(sources):
            rows = jnp.concatenate(
                [
                    held[slot, source * capacity : (source + 1) * capacity]
                    for slot in range(slots)
                ],
                axis=0,
            )
            mixed = jnp.dot(back_ref[source], rows, preferred_element_type=jnp.float32)
            start = 0
            for index, count in enumerate(out_cuts):
                ref = out_refs[source // deep * len(out_cuts) + index]
                ref[source % deep] = mixed[start : start + count].astype(jnp.bfloat16)
                start += count


def run_experts(rows, plan, ups, downs, in_cuts, out_cuts, after):
    pieces, halves = len(rows), len(rows[0])
    deep, _, width = rows[0][0].shape
    own_slots, _, double = ups[0].shape
    hidden = double // 2
    slots = 2 * own_slots
    places = plan[2].shape[1]

    def own(j):
        return (jnp.minimum(j, own_slots - 1), 0, 0)

    def other(j):
        return (jnp.maximum(j - own_slots, 0), 0, 0)

    flat = pl.pallas_call(
        functools.partial(expert_kernel, pieces, tuple(in_cuts), tuple(out_cuts), len(after)),
        grid=(slots,),
        in_specs=[vmem_spec()] * (pieces * halves + 3)
        + [
            pl.BlockSpec((1, width, double), own),
            pl.BlockSpec((1, width, double), other),
            pl.BlockSpec((1, hidden, width), own),
            pl.BlockSpec((1, hidden, width), other),
        ]
        + [pl.BlockSpec(memory_space=pl.ANY)] * len(after),
        out_specs=[vmem_spec()] * (pieces * len(out_cuts)),
        out_shape=[jax.ShapeDtypeStruct((deep, c, width), jnp.bfloat16) for c in out_cuts]
        * pieces,
        scratch_shapes=[pltpu.VMEM((slots, places, width), jnp.bfloat16)],
        compiler_params=params(44),
        cost_estimate=pl.CostEstimate(
            flops=10 * slots * places * width * hidden,
            bytes_accessed=26_000_000,
            transcendentals=slots * places * hidden,
        ),
        name="run_experts",
    )(*[r for piece in rows for r in piece], *plan, ups[0], ups[1], downs[0], downs[1], *after)
    count = len(out_cuts)
    return [flat[i * count : (i + 1) * count] for i in range(pieces)]


def stack_kernel(count, *refs):
    out_ref = refs[-1]
    for index in range(count):
        out_ref[index] = refs[index][...]


def stack_rows(parts, after):
    return pl.pallas_call(
        functools.partial(stack_kernel, len(parts)),
        in_specs=[vmem_spec()] * len(parts) + [pl.BlockSpec(memory_space=pl.ANY)] * len(after),
        out_specs=vmem_spec(),
        out_shape=jax.ShapeDtypeStruct((len(parts), *parts[0].shape), parts[0].dtype),
        compiler_params=params(16),
        name="stack_rows",
    )(*parts, *after)


def chip_shape(chips):
    depth = 4 if chips % 4 == 0 else 1
    plane = chips // depth
    side = math.isqrt(plane)
    while plane % side:
        side -= 1
    return depth, plane // side, side


def make_shift(chips, cores):
    depth, tall, wide = chip_shape(chips)
    swap = tall == wide
    sizes = {"z": depth, "a": tall, "b": wide}

    def pairs(role, offset):
        out = []
        for z in range(depth):
            for y in range(tall):
                for x in range(wide):
                    for core in range(cores):
                        axis = role
                        if swap and core % 2 == 1:
                            axis = {"z": "z", "a": "b", "b": "a"}[role]
                        to_z, to_y, to_x = z, y, x
                        if axis == "z":
                            to_z = (z + offset) % depth
                        elif axis == "a":
                            to_y = (y + offset) % tall
                        else:
                            to_x = (x + offset) % wide
                        source = ((z * tall + y) * wide + x) * cores + core
                        target = ((to_z * tall + to_y) * wide + to_x) * cores + core
                        out.append((source, target))
        return out

    def shift(value, role, offset):
        return lax.ppermute(value, BOTH, pairs(role, offset % sizes[role]))

    return shift, sizes


def gather_line(value, shift, sizes):
    return [value] + [shift(value, "z", k) for k in range(1, sizes["z"])]


def gather_planes(line, shift, sizes):
    plane = [line] + [shift(line, "a", j) for j in range(1, sizes["a"])]
    return [plane] + [[shift(v, "b", k) for v in plane] for k in range(1, sizes["b"])]


def add_all(terms):
    total = terms[0].astype(jnp.float32)
    for term in terms[1:]:
        total = total + term.astype(jnp.float32)
    return total.astype(terms[0].dtype)


def scatter_chunks(chunks, shift, sizes):
    tall = sizes["a"]
    sums, before = [], []
    for planes in chunks:
        sending = planes[1:]
        if before:
            sending, _ = lax.optimization_barrier((sending, before))
        arrived = {}
        for j in range(tall - 1, -1, -1):
            arrived[j] = [shift(plane[j], "b", -k - 1) for k, plane in enumerate(sending)]
        before = [v for moved in arrived.values() for v in moved]
        arrived = [[planes[0][j]] + arrived[j] for j in range(tall)]
        line = [shift(add_all(arrived[j]), "a", -j) for j in range(1, tall)] + arrived[0]
        moved = [
            shift(add_all([t[i] for t in line]), "z", -i) for i in range(1, sizes["z"])
        ]
        sums.append(add_all([t[0] for t in line] + moved))
    return jnp.concatenate(sums, axis=0)


def rope_tables(positions):
    half = HEAD // 2
    frequency = rope_base ** (-jnp.arange(half, dtype=jnp.float32) / half)
    angles = positions.astype(jnp.float32)[:, None] * frequency[None, :]
    cosine, sine = jnp.cos(angles), jnp.sin(angles)
    return (
        jnp.concatenate([cosine] * 4, axis=1),
        jnp.concatenate([-sine, sine, -sine, sine], axis=1),
    )


def shards(
    tokens,
    attn_gain,
    w_qkv,
    w_out,
    k_cache,
    v_cache,
    cache_len,
    ffn_gain,
    routes,
    route_scores,
    replica_slot,
    expert_up,
    expert_down,
):
    row_count, top_count = routes.shape
    chips, cores = lax.axis_size("req"), lax.axis_size("seq")
    seq_index = lax.axis_index("seq")
    length = cache_len[0]
    slots_dev = expert_up.shape[0]
    slot_total = chips * cores * slots_dev
    capacity = 2 * ((row_count * top_count + slot_total - 1) // slot_total)
    shift, sizes = make_shift(chips, cores)

    def swap(value):
        return lax.ppermute(value, "seq", [(0, 1), (1, 0)])

    other_tokens = swap(tokens)
    k_other, v_other = swap(k_cache), swap(v_cache)
    experts = jnp.arange(replica_slot.shape[1], dtype=jnp.int32)
    slot_of = jnp.sum(
        jnp.where(routes[:, :, None] == experts, replica_slot[:, None, :], 0), axis=2
    )
    shares = route_scores / jnp.sum(route_scores, axis=1, keepdims=True)
    coarse = lax.reduce_precision(shares, 8, 7)
    table = jnp.concatenate([slot_of.astype(jnp.float32), coarse, shares - coarse], axis=1)
    table = table.astype(jnp.bfloat16).T.reshape(-1, tokens.shape[1])
    table = jnp.pad(table, ((0, 16 - table.shape[0]), (0, 0)))
    chip = lax.axis_index("req")
    chip_slots = jnp.arange(slots_dev, dtype=jnp.int32)
    slot_ids = jnp.concatenate(
        [
            (chip * cores + seq_index) * slots_dev + chip_slots,
            (chip * cores + 1 - seq_index) * slots_dev + chip_slots,
        ]
    ).astype(jnp.int32)

    row_index = jnp.arange(row_count, dtype=jnp.int32)
    cosine, sine = rope_tables(
        length
        + jnp.concatenate(
            [seq_index * row_count + row_index, (1 - seq_index) * row_count + row_index]
        )
    )
    queries, appended, other_span = project(
        tokens, other_tokens, attn_gain, cosine, sine, w_qkv, [k_other, v_other]
    )
    place = jnp.stack([seq_index, length]).astype(jnp.int32)
    later_up, later_down, _ = lax.optimization_barrier((expert_up, expert_down, appended))
    up_other, down_other = swap(later_up), swap(later_down)
    half = row_count // 2
    filled, lines = [], []
    for index in range(2):
        attended, stream, expert_in = attend(
            place,
            queries,
            (k_cache, k_other, v_cache, v_other),
            (appended, other_span),
            w_out,
            tokens,
            ffn_gain,
            index * half,
            half,
            [] if index else [table],
            filled,
            [up_other, down_other] if index else [],
        )
        filled = [attended, stream]
        lines.append(gather_line(expert_in, shift, sizes))
    halves, after = [], [expert_in]
    for line in lines:
        planes = gather_planes(stack_rows(line, after), shift, sizes)
        halves.append(planes)
        after = [v for plane in planes[1:] for v in plane]
    cut = row_count // 2
    results = []
    for index in range(sizes["b"]):
        plan = plan_routes(slot_ids, halves[0][index], half, row_count, capacity, top_count)
        results.append(
            run_experts(
                [[planes[index][j] for planes in halves] for j in range(sizes["a"])],
                plan,
                (expert_up, up_other),
                (expert_down, down_other),
                (half, row_count - half),
                (cut, row_count - cut),
                results[-1][0][:1] if results else [],
            )
        )
    expert_mix = scatter_chunks(
        [[[piece[i] for piece in r] for r in results] for i in range(2)], shift, sizes
    )
    return (attended, stream, expert_mix, appended)


def solution(mesh):
    return jax.shard_map(
        shards,
        mesh=mesh,
        in_specs=(
            P(("req", "seq"), None),
            P(),
            P(),
            P(),
            P("req", "seq", None),
            P("req", "seq", None),
            P("req"),
            P(),
            P(("req", "seq"), None),
            P(("req", "seq"), None),
            P(("req", "seq"), None),
            P(("req", "seq"), None, None),
            P(("req", "seq"), None, None),
        ),
        out_specs=(
            P(("req", "seq"), None),
            P(("req", "seq"), None),
            P(("req", "seq"), None),
            P(("req", "seq"), None),
        ),
        check_vma=False,
    )
```

```python
import functools
import math

import jax
import jax.numpy as jnp
from jax import lax
from jax.experimental import pallas as pl
from jax.experimental.pallas import tpu as pltpu
from jax.sharding import PartitionSpec as P

HEADS = 24
KV_HEADS = 8
HEAD = 64
GROUP = HEADS // KV_HEADS
LANES = 128
PAIR = 2 * GROUP * HEAD

epsilon = 1e-06
residual_scale = 0.22
score_scale = 0.015625
rope_base = 10000.0
neg_big = -1e30

BOTH = ("req", "seq")


def vmem_spec():
    return pl.BlockSpec(memory_space=pltpu.VMEM)


def params(mebibytes):
    return pltpu.CompilerParams(vmem_limit_bytes=mebibytes * 2**20)


def qkv_kernel(own_ref, other_ref, gain_ref, cos_ref, sin_ref, w_ref, *refs):
    q_ref, kv_ref, kvo_ref, normed = refs[-4:]
    step = pl.program_id(0)
    rows = own_ref.shape[0]
    width = w_ref.shape[1]

    @pl.when(step == 0)
    def _():
        for index, ref in enumerate((own_ref, other_ref)):
            wide = ref[...].astype(jnp.float32)
            mean_square = jnp.mean(wide * wide, axis=-1, keepdims=True)
            normed[index * rows : (index + 1) * rows] = (
                wide * lax.rsqrt(mean_square + epsilon) * gain_ref[...][None, :]
            ).astype(jnp.bfloat16)

    def rotated(x, row_slice):
        lane = lax.broadcasted_iota(jnp.int32, x.shape, 1)
        low = (lane & (HEAD - 1)) < HEAD // 2
        swapped = jnp.where(
            low, pltpu.roll(x, width - HEAD // 2, 1), pltpu.roll(x, HEAD // 2, 1)
        )
        times = width // LANES
        cosine = jnp.concatenate([cos_ref[row_slice]] * times, axis=1)
        sine = jnp.concatenate([sin_ref[row_slice]] * times, axis=1)
        return x * cosine + swapped * sine

    @pl.when(step < 3)
    def _():
        x = jnp.dot(normed[:rows], w_ref[...], preferred_element_type=jnp.float32)
        q_ref[...] = (rotated(x, slice(0, rows)) * score_scale).astype(jnp.bfloat16)

    @pl.when(step == 3)
    def _():
        x = jnp.dot(normed[...], w_ref[...], preferred_element_type=jnp.float32)
        x = rotated(x, slice(0, 2 * rows)).astype(jnp.bfloat16)
        kv_ref[...] = x[:rows]
        kvo_ref[...] = x[rows:]

    @pl.when(step == 4)
    def _():
        x = jnp.dot(normed[...], w_ref[...], preferred_element_type=jnp.float32)
        x = x.astype(jnp.bfloat16)
        kv_ref[...] = x[:rows]
        kvo_ref[...] = x[rows:]


def project(own, other, gain, cosine, sine, w_qkv, after):
    rows, width = own.shape
    tile = KV_HEADS * HEAD
    return pl.pallas_call(
        qkv_kernel,
        grid=(5,),
        in_specs=[vmem_spec()] * 5
        + [pl.BlockSpec((width, tile), lambda i: (0, i))]
        + [pl.BlockSpec(memory_space=pl.ANY)] * len(after),
        out_specs=[
            pl.BlockSpec((rows, tile), lambda i: (0, jnp.minimum(i, 2))),
            pl.BlockSpec((rows, tile), lambda i: (0, jnp.maximum(i - 3, 0))),
            pl.BlockSpec((rows, tile), lambda i: (0, jnp.maximum(i - 3, 0))),
        ],
        out_shape=[
            jax.ShapeDtypeStruct((rows, HEADS * HEAD), jnp.bfloat16),
            jax.ShapeDtypeStruct((rows, 2 * tile), jnp.bfloat16),
            jax.ShapeDtypeStruct((rows, 2 * tile), jnp.bfloat16),
        ],
        scratch_shapes=[pltpu.VMEM((2 * rows, width), jnp.bfloat16)],
        compiler_params=params(58),
        cost_estimate=pl.CostEstimate(
            flops=2 * rows * width * 3584, bytes_accessed=9_500_000, transcendentals=0
        ),
        name="project_rows",
    )(own, other, gain, cosine, sine, w_qkv, *after)


def attend_kernel(first_row, riders, extra, place_ref, q_ref, kc_ref, kco_ref, vc_ref, vco_ref, ks_ref, kso_ref, vs_ref, vso_ref, w_out_ref, tokens_ref, gain_ref, *refs):
    attended_ref, stream_ref, expert_in_ref, keys, values, wide_q, total = refs[riders + extra :]
    step = pl.program_id(0)
    rows = q_ref.shape[0]
    cached = kc_ref.shape[1]
    span = ks_ref.shape[0]
    seq_index = place_ref[0]
    length = place_ref[1]

    @pl.when(step == 0)
    def _():
        position = lax.broadcasted_iota(jnp.int32, (cached, LANES), 0)
        for index, half in enumerate((seq_index, 1 - seq_index)):
            visible = position + half * cached < length
            keys[index * cached : (index + 1) * cached, LANES:] = jnp.where(
                visible, 0.0, neg_big
            ).astype(jnp.bfloat16)
        key = lax.broadcasted_iota(jnp.int32, (span, LANES), 0)
        row = lax.broadcasted_iota(jnp.int32, (span, LANES), 1)
        keys[2 * cached : 2 * cached + span, LANES:] = jnp.where(key <= row, 0.0, neg_big).astype(
            jnp.bfloat16
        )
        keys[2 * cached + span :, LANES:] = jnp.where(
            jnp.zeros((span, LANES), jnp.int32) < seq_index, 0.0, neg_big
        ).astype(jnp.bfloat16)
        values[:, LANES:] = jnp.ones((values.shape[0], LANES), jnp.bfloat16)
        row = lax.broadcasted_iota(jnp.int32, (rows, LANES), 0) + first_row
        lane = lax.broadcasted_iota(jnp.int32, (rows, LANES), 1)
        chosen = jnp.where(row == lane, 1.0, 0.0).astype(jnp.bfloat16)
        for head in range(2 * GROUP):
            wide_q[head * rows : (head + 1) * rows, LANES:] = chosen

    for ref, parts in ((keys, (kc_ref, kco_ref)), (values, (vc_ref, vco_ref))):
        for index, part in enumerate(parts):
            ref[index * cached : (index + 1) * cached, :LANES] = part[0]
    for ref, parts in ((keys, (ks_ref, kso_ref)), (values, (vs_ref, vso_ref))):
        for index, part in enumerate(parts):
            start = 2 * cached + index * span
            ref[start : start + span, :LANES] = part[...]

    low = lax.broadcasted_iota(jnp.int32, (rows, LANES), 1) < HEAD
    tiles = [q_ref[:, i * LANES : (i + 1) * LANES].astype(jnp.float32) for i in range(3)]
    parts = [
        jnp.where(low, tiles[0], 0.0),
        jnp.where(low, pltpu.roll(tiles[0], HEAD, 1), 0.0),
        jnp.where(low, tiles[1], 0.0),
        jnp.where(low, 0.0, tiles[1]),
        jnp.where(low, 0.0, pltpu.roll(tiles[2], HEAD, 1)),
        jnp.where(low, 0.0, tiles[2]),
    ]
    for head, part in enumerate(parts):
        wide_q[head * rows : (head + 1) * rows, :LANES] = part.astype(jnp.bfloat16)

    heads = []
    batch = GROUP * rows
    for first in range(0, 2 * GROUP * rows, batch):
        scores = lax.dot_general(
            wide_q[first : first + batch],
            keys[...],
            (((1,), (1,)), ((), ())),
            preferred_element_type=jnp.float32,
        )
        best = jnp.max(scores, axis=-1, keepdims=True)
        weights = jnp.exp(scores - best).astype(jnp.bfloat16)
        sums = jnp.dot(weights, values[...], preferred_element_type=jnp.float32)
        mean = sums[:, :LANES] / sums[:, LANES:]
        heads += [mean[i : i + rows] for i in range(0, batch, rows)]
    merged = jnp.concatenate(
        [
            jnp.where(low, heads[0], pltpu.roll(heads[1], HEAD, 1)),
            jnp.where(low, heads[2], heads[3]),
            jnp.where(low, pltpu.roll(heads[4], HEAD, 1), heads[5]),
        ],
        axis=1,
    ).astype(jnp.bfloat16)
    attended_ref[...] = merged
    product = jnp.dot(merged, w_out_ref[...], preferred_element_type=jnp.float32)

    @pl.when(step == 0)
    def _():
        total[...] = product

    @pl.when(step > 0)
    def _():
        total[...] += product

    @pl.when(step == pl.num_programs(0) - 1)
    def _():
        stream = (tokens_ref[...].astype(jnp.float32) + residual_scale * total[...]).astype(
            jnp.bfloat16
        )
        stream_ref[...] = stream
        wide = stream.astype(jnp.float32)
        mean_square = jnp.mean(wide * wide, axis=-1, keepdims=True)
        sent = (wide * lax.rsqrt(mean_square + epsilon) * gain_ref[...][None, :]).astype(
            jnp.bfloat16
        )
        expert_in_ref[...] = jnp.concatenate([sent, *[r[...] for r in refs[:riders]]], axis=0)


def attend(place, queries, caches, spans, w_out, tokens, gain, first_row, rows, riders, filled, after):
    k_cache, k_other, v_cache, v_other = caches
    own_span, other_span = spans
    cached = k_cache.shape[1]
    span, width = tokens.shape
    pairs = KV_HEADS // 2
    part = first_row // rows
    key_count = 2 * cached + 2 * span
    cache_spec = pl.BlockSpec((1, cached, LANES), lambda j: (0, 0, j))
    key_spec = pl.BlockSpec((span, LANES), lambda j: (0, j))
    value_spec = pl.BlockSpec((span, LANES), lambda j: (0, pairs + j))
    extra = [*filled, *after]
    sent = rows + sum(r.shape[0] for r in riders)
    return pl.pallas_call(
        functools.partial(attend_kernel, first_row, len(riders), len(extra)),
        grid=(pairs,),
        in_specs=[
            pl.BlockSpec(memory_space=pltpu.SMEM),
            pl.BlockSpec((rows, PAIR), lambda j: (part, j)),
            cache_spec,
            cache_spec,
            cache_spec,
            cache_spec,
            key_spec,
            key_spec,
            value_spec,
            value_spec,
            pl.BlockSpec((PAIR, width), lambda j: (j, 0)),
            pl.BlockSpec((rows, width), lambda j: (part, 0)),
            vmem_spec(),
        ]
        + [vmem_spec()] * len(riders)
        + [pl.BlockSpec(memory_space=pl.ANY)] * len(extra),
        out_specs=[
            pl.BlockSpec((rows, PAIR), lambda j: (part, j)),
            pl.BlockSpec((rows, width), lambda j: (part, 0)),
            pl.BlockSpec((sent, width), lambda j: (0, 0)),
        ],
        out_shape=[
            jax.ShapeDtypeStruct((span, HEADS * HEAD), jnp.bfloat16),
            jax.ShapeDtypeStruct((span, width), jnp.bfloat16),
            jax.ShapeDtypeStruct((sent, width), jnp.bfloat16),
        ],
        input_output_aliases={13 + len(riders) + i: i for i in range(len(filled))},
        scratch_shapes=[
            pltpu.VMEM((key_count, 2 * LANES), jnp.bfloat16),
            pltpu.VMEM((key_count, 2 * LANES), jnp.bfloat16),
            pltpu.VMEM((2 * GROUP * rows, 2 * LANES), jnp.bfloat16),
            pltpu.VMEM((rows, width), jnp.float32),
        ],
        compiler_params=params(58),
        cost_estimate=pl.CostEstimate(
            flops=16 * HEADS * rows * key_count * LANES,
            bytes_accessed=10_000_000,
            transcendentals=HEADS * rows * key_count,
        ),
        name="attend_rows",
    )(
        place,
        queries,
        k_cache,
        k_other,
        v_cache,
        v_other,
        own_span,
        other_span,
        own_span,
        other_span,
        w_out,
        tokens,
        gain,
        *riders,
        *extra,
    )


def plan_kernel(pieces, first, capacity, top, slot_ref, *refs):
    pick_ref, back_ref, share_ref = refs[pieces:]
    slots = slot_ref.shape[0]
    sources, _, tokens = pick_ref.shape
    deep = sources // pieces
    earlier = jnp.where(
        lax.broadcasted_iota(jnp.int32, (tokens, tokens), 0)
        < lax.broadcasted_iota(jnp.int32, (tokens, tokens), 1),
        1.0,
        0.0,
    ).astype(jnp.bfloat16)
    place = lax.broadcasted_iota(jnp.int32, (capacity, tokens), 0).astype(jnp.float32)
    hot_rows, share_lines = [], []
    for source in range(sources):
        packed = refs[source // deep][source % deep][first:].astype(jnp.float32)
        across = packed.shape[1] // tokens
        lines = [
            packed[i // across : i // across + 1, i % across * tokens : (i % across + 1) * tokens]
            for i in range(3 * top)
        ]
        ids = jnp.concatenate(lines[:top], axis=0)
        shares = jnp.concatenate(lines[top : 2 * top], axis=0)
        shares += jnp.concatenate(lines[2 * top :], axis=0)
        for slot in range(slots):
            match = ids == slot_ref[slot].astype(jnp.float32)
            hot_rows.append(jnp.max(jnp.where(match, 1.0, 0.0), axis=0, keepdims=True))
            share_lines.append(jnp.sum(jnp.where(match, shares, 0.0), axis=0, keepdims=True))
    hot = jnp.concatenate(hot_rows, axis=0)
    rank = jnp.dot(hot.astype(jnp.bfloat16), earlier, preferred_element_type=jnp.float32)
    rank = jnp.where(hot > 0.0, rank, -1.0)
    for source in range(sources):
        picks = []
        for slot in range(slots):
            line = source * slots + slot
            chosen = jnp.where(place == rank[line : line + 1], 1.0, 0.0)
            share_ref[slot, source * capacity : (source + 1) * capacity] = jnp.sum(
                chosen * share_lines[line], axis=1, keepdims=True
            )
            picks.append(chosen)
        picked = jnp.concatenate(picks, axis=0)
        pick_ref[source] = picked.astype(jnp.bfloat16)
        back_ref[source] = jnp.transpose(picked).astype(jnp.bfloat16)


def plan_routes(slot_ids, pieces, first, tokens, capacity, top):
    slots = slot_ids.shape[0]
    sources = sum(p.shape[0] for p in pieces)
    return pl.pallas_call(
        functools.partial(plan_kernel, len(pieces), first, capacity, top),
        in_specs=[pl.BlockSpec(memory_space=pltpu.SMEM)] + [vmem_spec()] * len(pieces),
        out_specs=[vmem_spec()] * 3,
        out_shape=[
            jax.ShapeDtypeStruct((sources, slots * capacity, tokens), jnp.bfloat16),
            jax.ShapeDtypeStruct((sources, tokens, slots * capacity), jnp.bfloat16),
            jax.ShapeDtypeStruct((slots, sources * capacity, 1), jnp.float32),
        ],
        compiler_params=params(24),
        cost_estimate=pl.CostEstimate(
            flops=1_000_000_000, bytes_accessed=2_000_000, transcendentals=0
        ),
        name="plan_routes",
    )(slot_ids, *pieces)


def expert_kernel(pieces, in_cuts, extra, *refs):
    halves = len(in_cuts)
    row_refs = refs[: pieces * halves]
    pick_ref, share_ref, up_ref, up_other_ref, down_ref, down_other_ref = refs[
        pieces * halves : pieces * halves + 6
    ]
    out_ref, held = refs[-2:]
    step = pl.program_id(0)
    slots = held.shape[0]
    own_slots = slots // 2
    sources = pick_ref.shape[0]
    deep = sources // pieces
    capacity = held.shape[1] // sources
    hidden = down_ref.shape[1]

    @pl.when(step == 0)
    def _():
        for source in range(sources):
            piece = source // deep
            rows = jnp.concatenate(
                [
                    row_refs[piece * halves + index][source % deep, :count]
                    for index, count in enumerate(in_cuts)
                ],
                axis=0,
            )
            rows = jnp.dot(
                pick_ref[source], rows, preferred_element_type=jnp.float32
            ).astype(jnp.bfloat16)
            for slot in range(slots):
                held[slot, source * capacity : (source + 1) * capacity] = rows[
                    slot * capacity : (slot + 1) * capacity
                ]

    def run(up, down):
        gate_up = jnp.dot(held[step], up[0], preferred_element_type=jnp.float32)
        active = (
            jax.nn.silu(gate_up[:, :hidden]) * gate_up[:, hidden:] * share_ref[step]
        ).astype(jnp.bfloat16)
        out_ref[step] = jnp.dot(active, down[0], preferred_element_type=jnp.float32).astype(
            jnp.bfloat16
        )

    @pl.when(step < own_slots)
    def _():
        run(up_ref, down_ref)

    @pl.when(step >= own_slots)
    def _():
        run(up_other_ref, down_other_ref)


def run_experts(rows, pick, share, ups, downs, in_cuts, after):
    pieces, halves = len(rows), len(rows[0])
    width = rows[0][0].shape[2]
    own_slots, _, double = ups[0].shape
    hidden = double // 2
    slots = 2 * own_slots
    places = share.shape[1]

    def own(j):
        return (jnp.minimum(j, own_slots - 1), 0, 0)

    def other(j):
        return (jnp.maximum(j - own_slots, 0), 0, 0)

    return pl.pallas_call(
        functools.partial(expert_kernel, pieces, tuple(in_cuts), len(after)),
        grid=(slots,),
        in_specs=[vmem_spec()] * (pieces * halves + 2)
        + [
            pl.BlockSpec((1, width, double), own),
            pl.BlockSpec((1, width, double), other),
            pl.BlockSpec((1, hidden, width), own),
            pl.BlockSpec((1, hidden, width), other),
        ]
        + [pl.BlockSpec(memory_space=pl.ANY)] * len(after),
        out_specs=vmem_spec(),
        out_shape=jax.ShapeDtypeStruct((slots, places, width), jnp.bfloat16),
        scratch_shapes=[pltpu.VMEM((slots, places, width), jnp.bfloat16)],
        compiler_params=params(44),
        cost_estimate=pl.CostEstimate(
            flops=10 * slots * places * width * hidden,
            bytes_accessed=26_000_000,
            transcendentals=slots * places * hidden,
        ),
        name="run_experts",
    )(*[r for piece in rows for r in piece], pick, share, ups[0], ups[1], downs[0], downs[1], *after)


def mix_kernel(pieces, out_cuts, held_ref, back_ref, *refs):
    count = len(out_cuts)
    out_refs = refs[-pieces * count :]
    slots, places, _ = held_ref.shape
    sources = back_ref.shape[0]
    deep = sources // pieces
    capacity = places // sources
    for source in range(sources):
        rows = jnp.concatenate(
            [
                held_ref[slot, source * capacity : (source + 1) * capacity]
                for slot in range(slots)
            ],
            axis=0,
        )
        mixed = jnp.dot(back_ref[source], rows, preferred_element_type=jnp.float32)
        start = 0
        for index, cut in enumerate(out_cuts):
            ref = out_refs[source // deep * count + index]
            ref[source % deep] = mixed[start : start + cut].astype(jnp.bfloat16)
            start += cut


def mix_rows(held, back, pieces, out_cuts, after):
    width = held.shape[2]
    deep = back.shape[0] // pieces
    flat = pl.pallas_call(
        functools.partial(mix_kernel, pieces, tuple(out_cuts)),
        in_specs=[vmem_spec()] * 2 + [pl.BlockSpec(memory_space=pl.ANY)] * len(after),
        out_specs=[vmem_spec()] * (pieces * len(out_cuts)),
        out_shape=[jax.ShapeDtypeStruct((deep, c, width), jnp.bfloat16) for c in out_cuts]
        * pieces,
        compiler_params=params(24),
        cost_estimate=pl.CostEstimate(
            flops=2_000_000_000, bytes_accessed=6_000_000, transcendentals=0
        ),
        name="mix_rows",
    )(held, back, *after)
    count = len(out_cuts)
    return [flat[i * count : (i + 1) * count] for i in range(pieces)]


def stack_kernel(count, *refs):
    out_ref = refs[-1]
    for index in range(count):
        out_ref[index] = refs[index][...]


def stack_rows(parts, after):
    return pl.pallas_call(
        functools.partial(stack_kernel, len(parts)),
        in_specs=[vmem_spec()] * len(parts) + [pl.BlockSpec(memory_space=pl.ANY)] * len(after),
        out_specs=vmem_spec(),
        out_shape=jax.ShapeDtypeStruct((len(parts), *parts[0].shape), parts[0].dtype),
        compiler_params=params(16),
        name="stack_rows",
    )(*parts, *after)


def chip_shape(chips):
    depth = 4 if chips % 4 == 0 else 1
    plane = chips // depth
    side = math.isqrt(plane)
    while plane % side:
        side -= 1
    return depth, plane // side, side


def make_shift(chips, cores):
    depth, tall, wide = chip_shape(chips)
    swap = tall == wide
    sizes = {"z": depth, "a": tall, "b": wide}

    def pairs(role, offset):
        out = []
        for z in range(depth):
            for y in range(tall):
                for x in range(wide):
                    for core in range(cores):
                        axis = role
                        if swap and core % 2 == 1:
                            axis = {"z": "z", "a": "b", "b": "a"}[role]
                        to_z, to_y, to_x = z, y, x
                        if axis == "z":
                            to_z = (z + offset) % depth
                        elif axis == "a":
                            to_y = (y + offset) % tall
                        else:
                            to_x = (x + offset) % wide
                        source = ((z * tall + y) * wide + x) * cores + core
                        target = ((to_z * tall + to_y) * wide + to_x) * cores + core
                        out.append((source, target))
        return out

    def shift(value, role, offset):
        return lax.ppermute(value, BOTH, pairs(role, offset % sizes[role]))

    return shift, sizes


def gather_line(value, shift, sizes):
    return [value] + [shift(value, "z", k) for k in range(1, sizes["z"])]


def gather_planes(line, shift, sizes, before):
    plane = [line] + [shift(line, "a", j) for j in range(1, sizes["a"])]
    forwarded = plane[1:]
    if before:
        forwarded, _ = lax.optimization_barrier((forwarded, before))
    return [plane] + [
        [shift(v, "b", k) for v in [line, *forwarded]] for k in range(1, sizes["b"])
    ]


def add_all(terms):
    total = terms[0].astype(jnp.float32)
    for term in terms[1:]:
        total = total + term.astype(jnp.float32)
    return total.astype(terms[0].dtype)


def leave_along_a(plane, shift):
    return [plane[0]] + [shift(v, "a", -j) for j, v in enumerate(plane) if j]


def scatter_chunks(own, others, shift, sizes):
    sums, before = [], []
    for line, sending in zip(own, others):
        if before:
            sending, _ = lax.optimization_barrier((sending, before))
        terms = [leave_along_a(plane, shift) for plane in sending]
        before = [v for moved in terms for v in moved[1:]]
        line = line + [shift(add_all(t), "b", -k - 1) for k, t in enumerate(terms)]
        moved = [
            shift(add_all([t[i] for t in line]), "z", -i) for i in range(1, sizes["z"])
        ]
        sums.append(add_all([t[0] for t in line] + moved))
    return jnp.concatenate(sums, axis=0)


def rope_tables(positions):
    half = HEAD // 2
    frequency = rope_base ** (-jnp.arange(half, dtype=jnp.float32) / half)
    angles = positions.astype(jnp.float32)[:, None] * frequency[None, :]
    cosine, sine = jnp.cos(angles), jnp.sin(angles)
    return (
        jnp.concatenate([cosine] * 4, axis=1),
        jnp.concatenate([-sine, sine, -sine, sine], axis=1),
    )


def shards(
    tokens,
    attn_gain,
    w_qkv,
    w_out,
    k_cache,
    v_cache,
    cache_len,
    ffn_gain,
    routes,
    route_scores,
    replica_slot,
    expert_up,
    expert_down,
):
    row_count, top_count = routes.shape
    chips, cores = lax.axis_size("req"), lax.axis_size("seq")
    seq_index = lax.axis_index("seq")
    length = cache_len[0]
    slots_dev = expert_up.shape[0]
    slot_total = chips * cores * slots_dev
    capacity = 2 * ((row_count * top_count + slot_total - 1) // slot_total)
    shift, sizes = make_shift(chips, cores)

    def swap(value):
        return lax.ppermute(value, "seq", [(0, 1), (1, 0)])

    other_tokens = swap(tokens)
    k_other, v_other = swap(k_cache), swap(v_cache)
    experts = jnp.arange(replica_slot.shape[1], dtype=jnp.int32)
    slot_of = jnp.sum(
        jnp.where(routes[:, :, None] == experts, replica_slot[:, None, :], 0), axis=2
    )
    shares = route_scores / jnp.sum(route_scores, axis=1, keepdims=True)
    coarse = lax.reduce_precision(shares, 8, 7)
    table = jnp.concatenate([slot_of.astype(jnp.float32), coarse, shares - coarse], axis=1)
    table = table.astype(jnp.bfloat16).T.reshape(-1, tokens.shape[1])
    table = jnp.pad(table, ((0, -table.shape[0] % 8), (0, 0)))
    chip = lax.axis_index("req")
    chip_slots = jnp.arange(slots_dev, dtype=jnp.int32)
    slot_ids = jnp.concatenate(
        [
            (chip * cores + seq_index) * slots_dev + chip_slots,
            (chip * cores + 1 - seq_index) * slots_dev + chip_slots,
        ]
    ).astype(jnp.int32)

    row_index = jnp.arange(row_count, dtype=jnp.int32)
    cosine, sine = rope_tables(
        length
        + jnp.concatenate(
            [seq_index * row_count + row_index, (1 - seq_index) * row_count + row_index]
        )
    )
    queries, appended, other_span = project(
        tokens, other_tokens, attn_gain, cosine, sine, w_qkv, [k_other, v_other]
    )
    place = jnp.stack([seq_index, length]).astype(jnp.int32)
    later_up, later_down, _ = lax.optimization_barrier((expert_up, expert_down, appended))
    up_other, down_other = swap(later_up), swap(later_down)
    half = row_count // 2
    filled, lines = [], []
    for index in range(2):
        attended, stream, expert_in = attend(
            place,
            queries,
            (k_cache, k_other, v_cache, v_other),
            (appended, other_span),
            w_out,
            tokens,
            ffn_gain,
            index * half,
            half,
            [] if index else [table],
            filled,
            [up_other, down_other] if index else [],
        )
        filled = [attended, stream]
        lines.append(gather_line(expert_in, shift, sizes))
    first, second = lines
    planes = gather_planes(stack_rows(first, [expert_in]), shift, sizes, second[1:])
    stacked = stack_rows(second, [plane[0] for plane in planes[1:]])
    halves = [planes, gather_planes(stacked, shift, sizes, [])]
    cuts = (row_count // 2, row_count - row_count // 2)
    own, others, held = [], [], None
    for index in range(sizes["b"]):
        pick, back, share = plan_routes(
            slot_ids, halves[0][index], half, row_count, capacity, top_count
        )
        held = run_experts(
            [[planes[index][j] for planes in halves] for j in range(sizes["a"])],
            pick,
            share,
            (expert_up, up_other),
            (expert_down, down_other),
            (half, row_count - half),
            [] if index == 0 else [held],
        )
        mixed = mix_rows(held, back, sizes["a"], cuts, [v for line in own for v in line[1:]])
        chunks = [[piece[i] for piece in mixed] for i in range(len(cuts))]
        if index == 0:
            own = [leave_along_a(plane, shift) for plane in chunks]
        else:
            others.append(chunks)
    others = [[planes[i] for planes in others] for i in range(len(cuts))]
    expert_mix = scatter_chunks(own, others, shift, sizes)
    return (attended, stream, expert_mix, appended)


def solution(mesh):
    return jax.shard_map(
        shards,
        mesh=mesh,
        in_specs=(
            P(("req", "seq"), None),
            P(),
            P(),
            P(),
            P("req", "seq", None),
            P("req", "seq", None),
            P("req"),
            P(),
            P(("req", "seq"), None),
            P(("req", "seq"), None),
            P(("req", "seq"), None),
            P(("req", "seq"), None, None),
            P(("req", "seq"), None, None),
        ),
        out_specs=(
            P(("req", "seq"), None),
            P(("req", "seq"), None),
            P(("req", "seq"), None),
            P(("req", "seq"), None),
        ),
        check_vma=False,
    )
```

```python
import functools
import math

import jax
import jax.numpy as jnp
from jax import lax
from jax.experimental import pallas as pl
from jax.experimental.pallas import tpu as pltpu
from jax.sharding import PartitionSpec as P

HEADS = 24
KV_HEADS = 8
HEAD = 64
GROUP = HEADS // KV_HEADS
LANES = 128
PAIR = 2 * GROUP * HEAD

epsilon = 1e-06
residual_scale = 0.22
score_scale = 0.015625
rope_base = 10000.0
neg_big = -1e30
log2_e = math.log2(math.e)

BOTH = ("req", "seq")


def vmem_spec():
    return pl.BlockSpec(memory_space=pltpu.VMEM)


def params(mebibytes):
    return pltpu.CompilerParams(vmem_limit_bytes=mebibytes * 2**20)


def qkv_kernel(own_ref, other_ref, gain_ref, cos_ref, sin_ref, w_ref, *refs):
    q_ref, kv_ref, kvo_ref, normed = refs[-4:]
    step = pl.program_id(0)
    rows = own_ref.shape[0]
    width = w_ref.shape[1]

    @pl.when(step == 0)
    def _():
        for index, ref in enumerate((own_ref, other_ref)):
            wide = ref[...].astype(jnp.float32)
            mean_square = jnp.mean(wide * wide, axis=-1, keepdims=True)
            normed[index * rows : (index + 1) * rows] = (
                wide * lax.rsqrt(mean_square + epsilon) * gain_ref[...][None, :]
            ).astype(jnp.bfloat16)

    def rotated(x, row_slice):
        lane = lax.broadcasted_iota(jnp.int32, x.shape, 1)
        low = (lane & (HEAD - 1)) < HEAD // 2
        swapped = jnp.where(
            low, pltpu.roll(x, width - HEAD // 2, 1), pltpu.roll(x, HEAD // 2, 1)
        )
        times = width // LANES
        cosine = jnp.concatenate([cos_ref[row_slice]] * times, axis=1)
        sine = jnp.concatenate([sin_ref[row_slice]] * times, axis=1)
        return x * cosine + swapped * sine

    @pl.when(step < 3)
    def _():
        x = jnp.dot(normed[:rows], w_ref[...], preferred_element_type=jnp.float32)
        q_ref[...] = (rotated(x, slice(0, rows)) * score_scale).astype(jnp.bfloat16)

    @pl.when(step == 3)
    def _():
        x = jnp.dot(normed[...], w_ref[...], preferred_element_type=jnp.float32)
        x = rotated(x, slice(0, 2 * rows)).astype(jnp.bfloat16)
        kv_ref[...] = x[:rows]
        kvo_ref[...] = x[rows:]

    @pl.when(step == 4)
    def _():
        x = jnp.dot(normed[...], w_ref[...], preferred_element_type=jnp.float32)
        x = x.astype(jnp.bfloat16)
        kv_ref[...] = x[:rows]
        kvo_ref[...] = x[rows:]


def project(own, other, gain, cosine, sine, w_qkv, after):
    rows, width = own.shape
    tile = KV_HEADS * HEAD
    return pl.pallas_call(
        qkv_kernel,
        grid=(5,),
        in_specs=[vmem_spec()] * 5
        + [pl.BlockSpec((width, tile), lambda i: (0, i))]
        + [pl.BlockSpec(memory_space=pl.ANY)] * len(after),
        out_specs=[
            pl.BlockSpec((rows, tile), lambda i: (0, jnp.minimum(i, 2))),
            pl.BlockSpec((rows, tile), lambda i: (0, jnp.maximum(i - 3, 0))),
            pl.BlockSpec((rows, tile), lambda i: (0, jnp.maximum(i - 3, 0))),
        ],
        out_shape=[
            jax.ShapeDtypeStruct((rows, HEADS * HEAD), jnp.bfloat16),
            jax.ShapeDtypeStruct((rows, 2 * tile), jnp.bfloat16),
            jax.ShapeDtypeStruct((rows, 2 * tile), jnp.bfloat16),
        ],
        scratch_shapes=[pltpu.VMEM((2 * rows, width), jnp.bfloat16)],
        compiler_params=params(58),
        cost_estimate=pl.CostEstimate(
            flops=2 * rows * width * 3584, bytes_accessed=9_500_000, transcendentals=0
        ),
        name="project_rows",
    )(own, other, gain, cosine, sine, w_qkv, *after)


def attend_kernel(first_row, riders, extra, place_ref, q_ref, kc_ref, kco_ref, vc_ref, vco_ref, ks_ref, kso_ref, vs_ref, vso_ref, w_out_ref, tokens_ref, gain_ref, *refs):
    attended_ref, stream_ref, expert_in_ref, keys, values, wide_q, total = refs[riders + extra :]
    step = pl.program_id(0)
    rows = q_ref.shape[0]
    cached = kc_ref.shape[1]
    span = ks_ref.shape[0]
    seq_index = lax.axis_index("seq")
    length = place_ref[0]

    @pl.when(step == 0)
    def _():
        position = lax.broadcasted_iota(jnp.int32, (cached, LANES), 0)
        for index, half in enumerate((seq_index, 1 - seq_index)):
            visible = position + half * cached < length
            keys[index * cached : (index + 1) * cached, LANES:] = jnp.where(
                visible, 0.0, neg_big
            ).astype(jnp.bfloat16)
        key = lax.broadcasted_iota(jnp.int32, (span, LANES), 0)
        row = lax.broadcasted_iota(jnp.int32, (span, LANES), 1)
        keys[2 * cached : 2 * cached + span, LANES:] = jnp.where(key <= row, 0.0, neg_big).astype(
            jnp.bfloat16
        )
        keys[2 * cached + span :, LANES:] = jnp.where(
            jnp.zeros((span, LANES), jnp.int32) < seq_index, 0.0, neg_big
        ).astype(jnp.bfloat16)
        values[:, LANES:] = jnp.ones((values.shape[0], LANES), jnp.bfloat16)
        row = lax.broadcasted_iota(jnp.int32, (rows, LANES), 0) + first_row
        lane = lax.broadcasted_iota(jnp.int32, (rows, LANES), 1)
        chosen = jnp.where(row == lane, 1.0, 0.0).astype(jnp.bfloat16)
        for head in range(2 * GROUP):
            wide_q[head * rows : (head + 1) * rows, LANES:] = chosen

    for ref, parts in ((keys, (kc_ref, kco_ref)), (values, (vc_ref, vco_ref))):
        for index, part in enumerate(parts):
            ref[index * cached : (index + 1) * cached, :LANES] = part[0]
    for ref, parts in ((keys, (ks_ref, kso_ref)), (values, (vs_ref, vso_ref))):
        for index, part in enumerate(parts):
            start = 2 * cached + index * span
            ref[start : start + span, :LANES] = part[...]

    low = lax.broadcasted_iota(jnp.int32, (rows, LANES), 1) < HEAD
    tiles = [q_ref[:, i * LANES : (i + 1) * LANES].astype(jnp.float32) for i in range(3)]
    parts = [
        jnp.where(low, tiles[0], 0.0),
        jnp.where(low, pltpu.roll(tiles[0], HEAD, 1), 0.0),
        jnp.where(low, tiles[1], 0.0),
        jnp.where(low, 0.0, tiles[1]),
        jnp.where(low, 0.0, pltpu.roll(tiles[2], HEAD, 1)),
        jnp.where(low, 0.0, tiles[2]),
    ]
    for head, part in enumerate(parts):
        wide_q[head * rows : (head + 1) * rows, :LANES] = part.astype(jnp.bfloat16)

    heads = []
    batch = GROUP * rows
    for first in range(0, 2 * GROUP * rows, batch):
        scores = lax.dot_general(
            wide_q[first : first + batch],
            keys[...],
            (((1,), (1,)), ((), ())),
            preferred_element_type=jnp.float32,
        )
        best = jnp.max(scores, axis=-1, keepdims=True)
        weights = jnp.exp2(((scores - best) * log2_e).astype(jnp.bfloat16))
        sums = jnp.dot(weights, values[...], preferred_element_type=jnp.float32)
        mean = sums[:, :LANES] / sums[:, LANES:]
        heads += [mean[i : i + rows] for i in range(0, batch, rows)]
    merged = jnp.concatenate(
        [
            jnp.where(low, heads[0], pltpu.roll(heads[1], HEAD, 1)),
            jnp.where(low, heads[2], heads[3]),
            jnp.where(low, pltpu.roll(heads[4], HEAD, 1), heads[5]),
        ],
        axis=1,
    ).astype(jnp.bfloat16)
    attended_ref[...] = merged
    product = jnp.dot(merged, w_out_ref[...], preferred_element_type=jnp.float32)

    @pl.when(step == 0)
    def _():
        total[...] = product

    @pl.when(step > 0)
    def _():
        total[...] += product

    @pl.when(step == pl.num_programs(0) - 1)
    def _():
        stream = (tokens_ref[...].astype(jnp.float32) + residual_scale * total[...]).astype(
            jnp.bfloat16
        )
        stream_ref[...] = stream
        wide = stream.astype(jnp.float32)
        mean_square = jnp.mean(wide * wide, axis=-1, keepdims=True)
        sent = (wide * lax.rsqrt(mean_square + epsilon) * gain_ref[...][None, :]).astype(
            jnp.bfloat16
        )
        expert_in_ref[...] = jnp.concatenate([sent, *[r[...] for r in refs[:riders]]], axis=0)


def attend(place, queries, caches, spans, w_out, tokens, gain, first_row, rows, riders, filled, after):
    k_cache, k_other, v_cache, v_other = caches
    own_span, other_span = spans
    cached = k_cache.shape[1]
    span, width = tokens.shape
    pairs = KV_HEADS // 2
    part = first_row // rows
    key_count = 2 * cached + 2 * span
    cache_spec = pl.BlockSpec((1, cached, LANES), lambda j: (0, 0, j))
    key_spec = pl.BlockSpec((span, LANES), lambda j: (0, j))
    value_spec = pl.BlockSpec((span, LANES), lambda j: (0, pairs + j))
    extra = [*filled, *after]
    sent = rows + sum(r.shape[0] for r in riders)
    return pl.pallas_call(
        functools.partial(attend_kernel, first_row, len(riders), len(extra)),
        grid=(pairs,),
        in_specs=[
            pl.BlockSpec(memory_space=pltpu.SMEM),
            pl.BlockSpec((rows, PAIR), lambda j: (part, j)),
            cache_spec,
            cache_spec,
            cache_spec,
            cache_spec,
            key_spec,
            key_spec,
            value_spec,
            value_spec,
            pl.BlockSpec((PAIR, width), lambda j: (j, 0)),
            pl.BlockSpec((rows, width), lambda j: (part, 0)),
            vmem_spec(),
        ]
        + [vmem_spec()] * len(riders)
        + [pl.BlockSpec(memory_space=pl.ANY)] * len(extra),
        out_specs=[
            pl.BlockSpec((rows, PAIR), lambda j: (part, j)),
            pl.BlockSpec((rows, width), lambda j: (part, 0)),
            pl.BlockSpec((sent, width), lambda j: (0, 0)),
        ],
        out_shape=[
            jax.ShapeDtypeStruct((span, HEADS * HEAD), jnp.bfloat16),
            jax.ShapeDtypeStruct((span, width), jnp.bfloat16),
            jax.ShapeDtypeStruct((sent, width), jnp.bfloat16),
        ],
        input_output_aliases={13 + len(riders) + i: i for i in range(len(filled))},
        scratch_shapes=[
            pltpu.VMEM((key_count, 2 * LANES), jnp.bfloat16),
            pltpu.VMEM((key_count, 2 * LANES), jnp.bfloat16),
            pltpu.VMEM((2 * GROUP * rows, 2 * LANES), jnp.bfloat16),
            pltpu.VMEM((rows, width), jnp.float32),
        ],
        compiler_params=params(58),
        cost_estimate=pl.CostEstimate(
            flops=16 * HEADS * rows * key_count * LANES,
            bytes_accessed=10_000_000,
            transcendentals=HEADS * rows * key_count,
        ),
        name="attend_rows",
    )(
        place,
        queries,
        k_cache,
        k_other,
        v_cache,
        v_other,
        own_span,
        other_span,
        own_span,
        other_span,
        w_out,
        tokens,
        gain,
        *riders,
        *extra,
    )


def plan_kernel(pieces, first, capacity, top, slot_ref, *refs):
    pick_ref, back_ref, share_ref = refs[pieces:]
    slots = slot_ref.shape[0]
    sources, _, tokens = pick_ref.shape
    deep = sources // pieces
    earlier = jnp.where(
        lax.broadcasted_iota(jnp.int32, (tokens, tokens), 0)
        < lax.broadcasted_iota(jnp.int32, (tokens, tokens), 1),
        1.0,
        0.0,
    ).astype(jnp.bfloat16)
    place = lax.broadcasted_iota(jnp.int32, (capacity, tokens), 0).astype(jnp.float32)
    hot_rows, share_lines = [], []
    for source in range(sources):
        packed = refs[source // deep][source % deep][first:].astype(jnp.float32)
        across = packed.shape[1] // tokens
        lines = [
            packed[i // across : i // across + 1, i % across * tokens : (i % across + 1) * tokens]
            for i in range(3 * top)
        ]
        ids = jnp.concatenate(lines[:top], axis=0)
        shares = jnp.concatenate(lines[top : 2 * top], axis=0)
        shares += jnp.concatenate(lines[2 * top :], axis=0)
        for slot in range(slots):
            match = ids == slot_ref[slot].astype(jnp.float32)
            hot_rows.append(jnp.max(jnp.where(match, 1.0, 0.0), axis=0, keepdims=True))
            share_lines.append(jnp.sum(jnp.where(match, shares, 0.0), axis=0, keepdims=True))
    hot = jnp.concatenate(hot_rows, axis=0)
    rank = jnp.dot(hot.astype(jnp.bfloat16), earlier, preferred_element_type=jnp.float32)
    rank = jnp.where(hot > 0.0, rank, -1.0)
    for source in range(sources):
        picks = []
        for slot in range(slots):
            line = source * slots + slot
            chosen = jnp.where(place == rank[line : line + 1], 1.0, 0.0)
            share_ref[slot, source * capacity : (source + 1) * capacity] = jnp.sum(
                chosen * share_lines[line], axis=1, keepdims=True
            )
            picks.append(chosen)
        picked = jnp.concatenate(picks, axis=0)
        pick_ref[source] = picked.astype(jnp.bfloat16)
        back_ref[source] = jnp.transpose(picked).astype(jnp.bfloat16)


def plan_routes(slot_ids, pieces, first, tokens, capacity, top):
    slots = slot_ids.shape[0]
    sources = sum(p.shape[0] for p in pieces)
    return pl.pallas_call(
        functools.partial(plan_kernel, len(pieces), first, capacity, top),
        in_specs=[pl.BlockSpec(memory_space=pltpu.SMEM)] + [vmem_spec()] * len(pieces),
        out_specs=[vmem_spec()] * 3,
        out_shape=[
            jax.ShapeDtypeStruct((sources, slots * capacity, tokens), jnp.bfloat16),
            jax.ShapeDtypeStruct((sources, tokens, slots * capacity), jnp.bfloat16),
            jax.ShapeDtypeStruct((slots, sources * capacity, 1), jnp.float32),
        ],
        compiler_params=params(24),
        cost_estimate=pl.CostEstimate(
            flops=1_000_000_000, bytes_accessed=2_000_000, transcendentals=0
        ),
        name="plan_routes",
    )(slot_ids, *pieces)


def expert_kernel(pieces, in_cuts, extra, *refs):
    halves = len(in_cuts)
    row_refs = refs[: pieces * halves]
    pick_ref, share_ref, up_ref, up_other_ref, down_ref, down_other_ref = refs[
        pieces * halves : pieces * halves + 6
    ]
    out_ref, held = refs[-2:]
    step = pl.program_id(0)
    slots = held.shape[0]
    own_slots = slots // 2
    sources = pick_ref.shape[0]
    deep = sources // pieces
    capacity = held.shape[1] // sources
    hidden = down_ref.shape[1]

    @pl.when(step == 0)
    def _():
        for source in range(sources):
            piece = source // deep
            rows = jnp.concatenate(
                [
                    row_refs[piece * halves + index][source % deep, :count]
                    for index, count in enumerate(in_cuts)
                ],
                axis=0,
            )
            rows = jnp.dot(
                pick_ref[source], rows, preferred_element_type=jnp.float32
            ).astype(jnp.bfloat16)
            for slot in range(slots):
                held[slot, source * capacity : (source + 1) * capacity] = rows[
                    slot * capacity : (slot + 1) * capacity
                ]

    def run(up, down):
        gate_up = jnp.dot(held[step], up[0], preferred_element_type=jnp.float32)
        active = (
            jax.nn.silu(gate_up[:, :hidden]) * gate_up[:, hidden:] * share_ref[step]
        ).astype(jnp.bfloat16)
        out_ref[step] = jnp.dot(active, down[0], preferred_element_type=jnp.float32).astype(
            jnp.bfloat16
        )

    @pl.when(step < own_slots)
    def _():
        run(up_ref, down_ref)

    @pl.when(step >= own_slots)
    def _():
        run(up_other_ref, down_other_ref)


def run_experts(rows, pick, share, ups, downs, in_cuts, after):
    pieces, halves = len(rows), len(rows[0])
    width = rows[0][0].shape[2]
    own_slots, _, double = ups[0].shape
    hidden = double // 2
    slots = 2 * own_slots
    places = share.shape[1]

    def own(j):
        return (jnp.minimum(j, own_slots - 1), 0, 0)

    def other(j):
        return (jnp.maximum(j - own_slots, 0), 0, 0)

    return pl.pallas_call(
        functools.partial(expert_kernel, pieces, tuple(in_cuts), len(after)),
        grid=(slots,),
        in_specs=[vmem_spec()] * (pieces * halves + 2)
        + [
            pl.BlockSpec((1, width, double), own),
            pl.BlockSpec((1, width, double), other),
            pl.BlockSpec((1, hidden, width), own),
            pl.BlockSpec((1, hidden, width), other),
        ]
        + [pl.BlockSpec(memory_space=pl.ANY)] * len(after),
        out_specs=vmem_spec(),
        out_shape=jax.ShapeDtypeStruct((slots, places, width), jnp.bfloat16),
        scratch_shapes=[pltpu.VMEM((slots, places, width), jnp.bfloat16)],
        compiler_params=params(44),
        cost_estimate=pl.CostEstimate(
            flops=10 * slots * places * width * hidden,
            bytes_accessed=26_000_000,
            transcendentals=slots * places * hidden,
        ),
        name="run_experts",
    )(*[r for piece in rows for r in piece], pick, share, ups[0], ups[1], downs[0], downs[1], *after)


def mix_kernel(pieces, out_cuts, held_ref, back_ref, *refs):
    count = len(out_cuts)
    out_refs = refs[-pieces * count :]
    slots, places, _ = held_ref.shape
    sources = back_ref.shape[0]
    deep = sources // pieces
    capacity = places // sources
    for source in range(sources):
        rows = jnp.concatenate(
            [
                held_ref[slot, source * capacity : (source + 1) * capacity]
                for slot in range(slots)
            ],
            axis=0,
        )
        mixed = jnp.dot(back_ref[source], rows, preferred_element_type=jnp.float32)
        start = 0
        for index, cut in enumerate(out_cuts):
            ref = out_refs[source // deep * count + index]
            ref[source % deep] = mixed[start : start + cut].astype(jnp.bfloat16)
            start += cut


def mix_rows(held, back, pieces, out_cuts, after):
    width = held.shape[2]
    deep = back.shape[0] // pieces
    flat = pl.pallas_call(
        functools.partial(mix_kernel, pieces, tuple(out_cuts)),
        in_specs=[vmem_spec()] * 2 + [pl.BlockSpec(memory_space=pl.ANY)] * len(after),
        out_specs=[vmem_spec()] * (pieces * len(out_cuts)),
        out_shape=[jax.ShapeDtypeStruct((deep, c, width), jnp.bfloat16) for c in out_cuts]
        * pieces,
        compiler_params=params(24),
        cost_estimate=pl.CostEstimate(
            flops=2_000_000_000, bytes_accessed=6_000_000, transcendentals=0
        ),
        name="mix_rows",
    )(held, back, *after)
    count = len(out_cuts)
    return [flat[i * count : (i + 1) * count] for i in range(pieces)]


def stack_kernel(count, *refs):
    out_ref = refs[-1]
    for index in range(count):
        out_ref[index] = refs[index][...]


def stack_rows(parts, after):
    return pl.pallas_call(
        functools.partial(stack_kernel, len(parts)),
        in_specs=[vmem_spec()] * len(parts) + [pl.BlockSpec(memory_space=pl.ANY)] * len(after),
        out_specs=vmem_spec(),
        out_shape=jax.ShapeDtypeStruct((len(parts), *parts[0].shape), parts[0].dtype),
        compiler_params=params(16),
        name="stack_rows",
    )(*parts, *after)


def chip_shape(chips):
    depth = 4 if chips % 4 == 0 else 1
    plane = chips // depth
    side = math.isqrt(plane)
    while plane % side:
        side -= 1
    return depth, plane // side, side


def make_shift(chips, cores):
    depth, tall, wide = chip_shape(chips)
    swap = tall == wide
    sizes = {"z": depth, "a": tall, "b": wide}

    def pairs(role, offset):
        out = []
        for z in range(depth):
            for y in range(tall):
                for x in range(wide):
                    for core in range(cores):
                        axis = role
                        if swap and core % 2 == 1:
                            axis = {"z": "z", "a": "b", "b": "a"}[role]
                        to_z, to_y, to_x = z, y, x
                        if axis == "z":
                            to_z = z ^ offset
                        elif axis == "a":
                            to_y = (y + offset) % tall
                        else:
                            to_x = (x + offset) % wide
                        source = ((z * tall + y) * wide + x) * cores + core
                        target = ((to_z * tall + to_y) * wide + to_x) * cores + core
                        out.append((source, target))
        return out

    def shift(value, role, offset):
        if role != "z":
            offset %= sizes[role]
        return lax.ppermute(value, BOTH, pairs(role, offset))

    return shift, sizes


def gather_line(value, shift, sizes):
    return [value] + [shift(value, "z", k) for k in range(1, sizes["z"])]


def gather_line_doubling(value, shift, sizes):
    line, step = {0: value}, sizes["z"] // 2
    while step:
        known = sorted(line)
        if len(known) == 1:
            arrived = [shift(line[0], "z", step)]
        else:
            arrived = shift(jnp.stack([line[k] for k in known]), "z", step)
        for place, k in enumerate(known):
            line[k ^ step] = arrived[place]
        step //= 2
    return [line[k] for k in range(sizes["z"])]


def scatter_line(line, shift, sizes):
    step = 1
    while step < sizes["z"]:
        kept = [k for k in range(0, sizes["z"], step) if not k & step]
        if len(kept) == 1:
            arrived = [shift(add_all(line[step]), "z", step)]
        else:
            arrived = shift(jnp.stack([add_all(line[k | step]) for k in kept]), "z", step)
        for place, k in enumerate(kept):
            line[k] = line[k] + [arrived[place]]
        step *= 2
    return add_all(line[0])


def gather_planes(line, shift, sizes, before):
    plane = [line] + [shift(line, "a", j) for j in range(1, sizes["a"])]
    forwarded = plane[1:]
    if before:
        forwarded, _ = lax.optimization_barrier((forwarded, before))
    return [plane] + [
        [shift(v, "b", k) for v in [line, *forwarded]] for k in range(1, sizes["b"])
    ]


def add_all(terms):
    total = terms[0].astype(jnp.float32)
    for term in terms[1:]:
        total = total + term.astype(jnp.float32)
    return total.astype(terms[0].dtype)


def leave_along_a(plane, shift):
    return [plane[0]] + [shift(v, "a", -j) for j, v in enumerate(plane) if j]


def scatter_chunks(own, others, shift, sizes):
    sums, before = [], []
    for line, sending in zip(own, others):
        if before:
            sending, _ = lax.optimization_barrier((sending, before))
        terms = [leave_along_a(plane, shift) for plane in sending]
        before = [v for moved in terms for v in moved[1:]]
        line = line + [shift(add_all(t), "b", -k - 1) for k, t in enumerate(terms)]
        parts = {i: [t[i] for t in line] for i in range(sizes["z"])}
        sums.append(scatter_line(parts, shift, sizes))
    total = jnp.zeros((sum(v.shape[0] for v in sums), sums[0].shape[1]), sums[0].dtype)
    first = 0
    for value in sums:
        total = lax.dynamic_update_slice(total, value, (first, 0))
        first += value.shape[0]
    return total


def rope_tables(positions):
    half = HEAD // 2
    frequency = rope_base ** (-jnp.arange(half, dtype=jnp.float32) / half)
    angles = positions.astype(jnp.float32)[:, None] * frequency[None, :]
    cosine, sine = jnp.cos(angles), jnp.sin(angles)
    return (
        jnp.concatenate([cosine] * 4, axis=1),
        jnp.concatenate([-sine, sine, -sine, sine], axis=1),
    )


def shards(
    tokens,
    attn_gain,
    w_qkv,
    w_out,
    k_cache,
    v_cache,
    cache_len,
    ffn_gain,
    routes,
    route_scores,
    replica_slot,
    expert_up,
    expert_down,
):
    row_count, top_count = routes.shape
    chips, cores = lax.axis_size("req"), lax.axis_size("seq")
    seq_index = lax.axis_index("seq")
    length = cache_len[0]
    slots_dev = expert_up.shape[0]
    slot_total = chips * cores * slots_dev
    capacity = 2 * ((row_count * top_count + slot_total - 1) // slot_total)
    shift, sizes = make_shift(chips, cores)

    def swap(value):
        return lax.ppermute(value, "seq", [(0, 1), (1, 0)])

    other_tokens = swap(tokens)
    k_other, v_other = swap(k_cache), swap(v_cache)
    experts = jnp.arange(replica_slot.shape[1], dtype=jnp.int32)
    slot_of = jnp.sum(
        jnp.where(routes[:, :, None] == experts, replica_slot[:, None, :], 0), axis=2
    )
    shares = route_scores / jnp.sum(route_scores, axis=1, keepdims=True)
    coarse = lax.reduce_precision(shares, 8, 7)
    table = jnp.concatenate([slot_of.astype(jnp.float32), coarse, shares - coarse], axis=1)
    table = table.astype(jnp.bfloat16).T.reshape(-1, tokens.shape[1])
    table = jnp.pad(table, ((0, -table.shape[0] % 8), (0, 0)))
    chip = lax.axis_index("req")
    chip_slots = jnp.arange(slots_dev, dtype=jnp.int32)
    slot_ids = jnp.concatenate(
        [
            (chip * cores + seq_index) * slots_dev + chip_slots,
            (chip * cores + 1 - seq_index) * slots_dev + chip_slots,
        ]
    ).astype(jnp.int32)

    row_index = jnp.arange(row_count, dtype=jnp.int32)
    cosine, sine = rope_tables(
        length
        + jnp.concatenate(
            [seq_index * row_count + row_index, (1 - seq_index) * row_count + row_index]
        )
    )
    queries, appended, other_span = project(
        tokens, other_tokens, attn_gain, cosine, sine, w_qkv, [k_other, v_other]
    )
    later_up, later_down, _ = lax.optimization_barrier((expert_up, expert_down, appended))
    up_other, down_other = swap(later_up), swap(later_down)
    half = row_count // 2
    filled, lines = [], []
    for index in range(2):
        attended, stream, expert_in = attend(
            cache_len,
            queries,
            (k_cache, k_other, v_cache, v_other),
            (appended, other_span),
            w_out,
            tokens,
            ffn_gain,
            index * half,
            half,
            [] if index else [table],
            filled,
            [up_other, down_other] if index else [],
        )
        filled = [attended, stream]
        gather = gather_line_doubling if index else gather_line
        lines.append(gather(expert_in, shift, sizes))
    first, second = lines
    planes = gather_planes(stack_rows(first, [expert_in]), shift, sizes, second[1:])
    stacked = stack_rows(second, [plane[0] for plane in planes[1:]])
    halves = [planes, gather_planes(stacked, shift, sizes, [])]
    cuts = (row_count // 2, row_count - row_count // 2)
    own, others, held = [], [], None
    for index in range(sizes["b"]):
        pick, back, share = plan_routes(
            slot_ids, halves[0][index], half, row_count, capacity, top_count
        )
        held = run_experts(
            [[planes[index][j] for planes in halves] for j in range(sizes["a"])],
            pick,
            share,
            (expert_up, up_other),
            (expert_down, down_other),
            (half, row_count - half),
            [] if index == 0 else [held],
        )
        mixed = mix_rows(held, back, sizes["a"], cuts, [v for line in own for v in line[1:]])
        chunks = [[piece[i] for piece in mixed] for i in range(len(cuts))]
        if index == 0:
            own = [leave_along_a(plane, shift) for plane in chunks]
        else:
            others.append(chunks)
    others = [[planes[i] for planes in others] for i in range(len(cuts))]
    expert_mix = scatter_chunks(own, others, shift, sizes)
    return (attended, stream, expert_mix, appended)


def solution(mesh):
    return jax.shard_map(
        shards,
        mesh=mesh,
        in_specs=(
            P(("req", "seq"), None),
            P(),
            P(),
            P(),
            P("req", "seq", None),
            P("req", "seq", None),
            P("req"),
            P(),
            P(("req", "seq"), None),
            P(("req", "seq"), None),
            P(("req", "seq"), None),
            P(("req", "seq"), None, None),
            P(("req", "seq"), None, None),
        ),
        out_specs=(
            P(("req", "seq"), None),
            P(("req", "seq"), None),
            P(("req", "seq"), None),
            P(("req", "seq"), None),
        ),
        check_vma=False,
    )
```

```python
import functools
import math

import jax
import jax.numpy as jnp
from jax import lax
from jax.experimental import pallas as pl
from jax.experimental.pallas import tpu as pltpu
from jax.sharding import PartitionSpec as P

HEADS = 24
KV_HEADS = 8
HEAD = 64
GROUP = HEADS // KV_HEADS
LANES = 128
PAIR = 2 * GROUP * HEAD

epsilon = 1e-06
residual_scale = 0.22
score_scale = 0.015625
rope_base = 10000.0
neg_big = -1e30

BOTH = ("req", "seq")


def vmem_spec():
    return pl.BlockSpec(memory_space=pltpu.VMEM)


def params(mebibytes):
    return pltpu.CompilerParams(vmem_limit_bytes=mebibytes * 2**20)


def qkv_kernel(own_ref, other_ref, gain_ref, cos_ref, sin_ref, w_ref, *refs):
    q_ref, kv_ref, kvo_ref, normed = refs[-4:]
    step = pl.program_id(0)
    rows = own_ref.shape[0]
    width = w_ref.shape[1]

    @pl.when(step == 0)
    def _():
        for index, ref in enumerate((own_ref, other_ref)):
            wide = ref[...].astype(jnp.float32)
            mean_square = jnp.mean(wide * wide, axis=-1, keepdims=True)
            normed[index * rows : (index + 1) * rows] = (
                wide * lax.rsqrt(mean_square + epsilon) * gain_ref[...][None, :]
            ).astype(jnp.bfloat16)

    def rotated(x, row_slice):
        lane = lax.broadcasted_iota(jnp.int32, x.shape, 1)
        low = (lane & (HEAD - 1)) < HEAD // 2
        swapped = jnp.where(
            low, pltpu.roll(x, width - HEAD // 2, 1), pltpu.roll(x, HEAD // 2, 1)
        )
        times = width // LANES
        cosine = jnp.concatenate([cos_ref[row_slice]] * times, axis=1)
        sine = jnp.concatenate([sin_ref[row_slice]] * times, axis=1)
        return x * cosine + swapped * sine

    @pl.when(step < 3)
    def _():
        x = jnp.dot(normed[:rows], w_ref[...], preferred_element_type=jnp.float32)
        q_ref[...] = (rotated(x, slice(0, rows)) * score_scale).astype(jnp.bfloat16)

    @pl.when(step == 3)
    def _():
        x = jnp.dot(normed[...], w_ref[...], preferred_element_type=jnp.float32)
        x = rotated(x, slice(0, 2 * rows)).astype(jnp.bfloat16)
        kv_ref[...] = x[:rows]
        kvo_ref[...] = x[rows:]

    @pl.when(step == 4)
    def _():
        x = jnp.dot(normed[...], w_ref[...], preferred_element_type=jnp.float32)
        x = x.astype(jnp.bfloat16)
        kv_ref[...] = x[:rows]
        kvo_ref[...] = x[rows:]


def project(own, other, gain, cosine, sine, w_qkv, after):
    rows, width = own.shape
    tile = KV_HEADS * HEAD
    return pl.pallas_call(
        qkv_kernel,
        grid=(5,),
        in_specs=[vmem_spec()] * 5
        + [pl.BlockSpec((width, tile), lambda i: (0, i))]
        + [pl.BlockSpec(memory_space=pl.ANY)] * len(after),
        out_specs=[
            pl.BlockSpec((rows, tile), lambda i: (0, jnp.minimum(i, 2))),
            pl.BlockSpec((rows, tile), lambda i: (0, jnp.maximum(i - 3, 0))),
            pl.BlockSpec((rows, tile), lambda i: (0, jnp.maximum(i - 3, 0))),
        ],
        out_shape=[
            jax.ShapeDtypeStruct((rows, HEADS * HEAD), jnp.bfloat16),
            jax.ShapeDtypeStruct((rows, 2 * tile), jnp.bfloat16),
            jax.ShapeDtypeStruct((rows, 2 * tile), jnp.bfloat16),
        ],
        scratch_shapes=[pltpu.VMEM((2 * rows, width), jnp.bfloat16)],
        compiler_params=params(58),
        cost_estimate=pl.CostEstimate(
            flops=2 * rows * width * 3584, bytes_accessed=9_500_000, transcendentals=0
        ),
        name="project_rows",
    )(own, other, gain, cosine, sine, w_qkv, *after)


def attend_kernel(first_row, riders, extra, place_ref, q_ref, kc_ref, kco_ref, vc_ref, vco_ref, ks_ref, kso_ref, vs_ref, vso_ref, w_out_ref, tokens_ref, gain_ref, *refs):
    attended_ref, stream_ref, expert_in_ref, keys, values, wide_q, total = refs[riders + extra :]
    step = pl.program_id(0)
    rows = q_ref.shape[0]
    cached = kc_ref.shape[1]
    span = ks_ref.shape[0]
    seq_index = lax.axis_index("seq")
    length = place_ref[0]

    @pl.when(step == 0)
    def _():
        position = lax.broadcasted_iota(jnp.int32, (cached, LANES), 0)
        for index, half in enumerate((seq_index, 1 - seq_index)):
            visible = position + half * cached < length
            keys[index * cached : (index + 1) * cached, LANES:] = jnp.where(
                visible, 0.0, neg_big
            ).astype(jnp.bfloat16)
        key = lax.broadcasted_iota(jnp.int32, (span, LANES), 0)
        row = lax.broadcasted_iota(jnp.int32, (span, LANES), 1)
        keys[2 * cached : 2 * cached + span, LANES:] = jnp.where(key <= row, 0.0, neg_big).astype(
            jnp.bfloat16
        )
        keys[2 * cached + span :, LANES:] = jnp.where(
            jnp.zeros((span, LANES), jnp.int32) < seq_index, 0.0, neg_big
        ).astype(jnp.bfloat16)
        values[:, LANES:] = jnp.ones((values.shape[0], LANES), jnp.bfloat16)
        row = lax.broadcasted_iota(jnp.int32, (rows, LANES), 0) + first_row
        lane = lax.broadcasted_iota(jnp.int32, (rows, LANES), 1)
        chosen = jnp.where(row == lane, 1.0, 0.0).astype(jnp.bfloat16)
        for head in range(2 * GROUP):
            wide_q[head * rows : (head + 1) * rows, LANES:] = chosen

    for ref, parts in ((keys, (kc_ref, kco_ref)), (values, (vc_ref, vco_ref))):
        for index, part in enumerate(parts):
            ref[index * cached : (index + 1) * cached, :LANES] = part[0]
    for ref, parts in ((keys, (ks_ref, kso_ref)), (values, (vs_ref, vso_ref))):
        for index, part in enumerate(parts):
            start = 2 * cached + index * span
            ref[start : start + span, :LANES] = part[...]

    low = lax.broadcasted_iota(jnp.int32, (rows, LANES), 1) < HEAD
    tiles = [q_ref[:, i * LANES : (i + 1) * LANES].astype(jnp.float32) for i in range(3)]
    parts = [
        jnp.where(low, tiles[0], 0.0),
        jnp.where(low, pltpu.roll(tiles[0], HEAD, 1), 0.0),
        jnp.where(low, tiles[1], 0.0),
        jnp.where(low, 0.0, tiles[1]),
        jnp.where(low, 0.0, pltpu.roll(tiles[2], HEAD, 1)),
        jnp.where(low, 0.0, tiles[2]),
    ]
    for head, part in enumerate(parts):
        wide_q[head * rows : (head + 1) * rows, :LANES] = part.astype(jnp.bfloat16)

    heads = []
    batch = GROUP * rows
    for first in range(0, 2 * GROUP * rows, batch):
        scores = lax.dot_general(
            wide_q[first : first + batch],
            keys[...],
            (((1,), (1,)), ((), ())),
            preferred_element_type=jnp.float32,
        )
        best = jnp.max(scores, axis=-1, keepdims=True)
        weights = jnp.exp(scores - best).astype(jnp.bfloat16)
        sums = jnp.dot(weights, values[...], preferred_element_type=jnp.float32)
        mean = sums[:, :LANES] / sums[:, LANES:]
        heads += [mean[i : i + rows] for i in range(0, batch, rows)]
    merged = jnp.concatenate(
        [
            jnp.where(low, heads[0], pltpu.roll(heads[1], HEAD, 1)),
            jnp.where(low, heads[2], heads[3]),
            jnp.where(low, pltpu.roll(heads[4], HEAD, 1), heads[5]),
        ],
        axis=1,
    ).astype(jnp.bfloat16)
    attended_ref[...] = merged
    product = jnp.dot(merged, w_out_ref[...], preferred_element_type=jnp.float32)

    @pl.when(step == 0)
    def _():
        total[...] = product

    @pl.when(step > 0)
    def _():
        total[...] += product

    @pl.when(step == pl.num_programs(0) - 1)
    def _():
        stream = (tokens_ref[...].astype(jnp.float32) + residual_scale * total[...]).astype(
            jnp.bfloat16
        )
        stream_ref[...] = stream
        wide = stream.astype(jnp.float32)
        mean_square = jnp.mean(wide * wide, axis=-1, keepdims=True)
        sent = (wide * lax.rsqrt(mean_square + epsilon) * gain_ref[...][None, :]).astype(
            jnp.bfloat16
        )
        expert_in_ref[...] = jnp.concatenate([sent, *[r[...] for r in refs[:riders]]], axis=0)


def attend(place, queries, caches, spans, w_out, tokens, gain, first_row, rows, riders, filled, after):
    k_cache, k_other, v_cache, v_other = caches
    own_span, other_span = spans
    cached = k_cache.shape[1]
    span, width = tokens.shape
    pairs = KV_HEADS // 2
    part = first_row // rows
    key_count = 2 * cached + 2 * span
    cache_spec = pl.BlockSpec((1, cached, LANES), lambda j: (0, 0, j))
    key_spec = pl.BlockSpec((span, LANES), lambda j: (0, j))
    value_spec = pl.BlockSpec((span, LANES), lambda j: (0, pairs + j))
    extra = [*filled, *after]
    sent = rows + sum(r.shape[0] for r in riders)
    return pl.pallas_call(
        functools.partial(attend_kernel, first_row, len(riders), len(extra)),
        grid=(pairs,),
        in_specs=[
            pl.BlockSpec(memory_space=pltpu.SMEM),
            pl.BlockSpec((rows, PAIR), lambda j: (part, j)),
            cache_spec,
            cache_spec,
            cache_spec,
            cache_spec,
            key_spec,
            key_spec,
            value_spec,
            value_spec,
            pl.BlockSpec((PAIR, width), lambda j: (j, 0)),
            pl.BlockSpec((rows, width), lambda j: (part, 0)),
            vmem_spec(),
        ]
        + [vmem_spec()] * len(riders)
        + [pl.BlockSpec(memory_space=pl.ANY)] * len(extra),
        out_specs=[
            pl.BlockSpec((rows, PAIR), lambda j: (part, j)),
            pl.BlockSpec((rows, width), lambda j: (part, 0)),
            pl.BlockSpec((sent, width), lambda j: (0, 0)),
        ],
        out_shape=[
            jax.ShapeDtypeStruct((span, HEADS * HEAD), jnp.bfloat16),
            jax.ShapeDtypeStruct((span, width), jnp.bfloat16),
            jax.ShapeDtypeStruct((sent, width), jnp.bfloat16),
        ],
        input_output_aliases={13 + len(riders) + i: i for i in range(len(filled))},
        scratch_shapes=[
            pltpu.VMEM((key_count, 2 * LANES), jnp.bfloat16),
            pltpu.VMEM((key_count, 2 * LANES), jnp.bfloat16),
            pltpu.VMEM((2 * GROUP * rows, 2 * LANES), jnp.bfloat16),
            pltpu.VMEM((rows, width), jnp.float32),
        ],
        compiler_params=params(58),
        cost_estimate=pl.CostEstimate(
            flops=16 * HEADS * rows * key_count * LANES,
            bytes_accessed=10_000_000,
            transcendentals=HEADS * rows * key_count,
        ),
        name="attend_rows",
    )(
        place,
        queries,
        k_cache,
        k_other,
        v_cache,
        v_other,
        own_span,
        other_span,
        own_span,
        other_span,
        w_out,
        tokens,
        gain,
        *riders,
        *extra,
    )


def plan_kernel(pieces, first, capacity, top, slot_ref, *refs):
    pick_ref, back_ref, share_ref = refs[pieces:]
    slots = slot_ref.shape[0]
    sources, _, tokens = pick_ref.shape
    deep = sources // pieces
    earlier = jnp.where(
        lax.broadcasted_iota(jnp.int32, (tokens, tokens), 0)
        < lax.broadcasted_iota(jnp.int32, (tokens, tokens), 1),
        1.0,
        0.0,
    ).astype(jnp.bfloat16)
    place = lax.broadcasted_iota(jnp.int32, (capacity, tokens), 0).astype(jnp.float32)
    hot_rows, share_lines = [], []
    for source in range(sources):
        packed = refs[source // deep][source % deep][first:].astype(jnp.float32)
        across = packed.shape[1] // tokens
        lines = [
            packed[i // across : i // across + 1, i % across * tokens : (i % across + 1) * tokens]
            for i in range(3 * top)
        ]
        ids = jnp.concatenate(lines[:top], axis=0)
        shares = jnp.concatenate(lines[top : 2 * top], axis=0)
        shares += jnp.concatenate(lines[2 * top :], axis=0)
        for slot in range(slots):
            match = ids == slot_ref[slot].astype(jnp.float32)
            hot_rows.append(jnp.max(jnp.where(match, 1.0, 0.0), axis=0, keepdims=True))
            share_lines.append(jnp.sum(jnp.where(match, shares, 0.0), axis=0, keepdims=True))
    hot = jnp.concatenate(hot_rows, axis=0)
    rank = jnp.dot(hot.astype(jnp.bfloat16), earlier, preferred_element_type=jnp.float32)
    rank = jnp.where(hot > 0.0, rank, -1.0)
    for source in range(sources):
        picks = []
        for slot in range(slots):
            line = source * slots + slot
            chosen = jnp.where(place == rank[line : line + 1], 1.0, 0.0)
            share_ref[slot, source * capacity : (source + 1) * capacity] = jnp.sum(
                chosen * share_lines[line], axis=1, keepdims=True
            )
            picks.append(chosen)
        picked = jnp.concatenate(picks, axis=0)
        pick_ref[source] = picked.astype(jnp.bfloat16)
        back_ref[source] = jnp.transpose(picked).astype(jnp.bfloat16)


def plan_routes(slot_ids, pieces, first, tokens, capacity, top):
    slots = slot_ids.shape[0]
    sources = sum(p.shape[0] for p in pieces)
    return pl.pallas_call(
        functools.partial(plan_kernel, len(pieces), first, capacity, top),
        in_specs=[pl.BlockSpec(memory_space=pltpu.SMEM)] + [vmem_spec()] * len(pieces),
        out_specs=[vmem_spec()] * 3,
        out_shape=[
            jax.ShapeDtypeStruct((sources, slots * capacity, tokens), jnp.bfloat16),
            jax.ShapeDtypeStruct((sources, tokens, slots * capacity), jnp.bfloat16),
            jax.ShapeDtypeStruct((slots, sources * capacity, 1), jnp.float32),
        ],
        compiler_params=params(24),
        cost_estimate=pl.CostEstimate(
            flops=1_000_000_000, bytes_accessed=2_000_000, transcendentals=0
        ),
        name="plan_routes",
    )(slot_ids, *pieces)


def expert_kernel(pieces, in_cuts, extra, *refs):
    halves = len(in_cuts)
    row_refs = refs[: pieces * halves]
    pick_ref, share_ref, up_ref, up_other_ref, down_ref, down_other_ref = refs[
        pieces * halves : pieces * halves + 6
    ]
    out_ref, held = refs[-2:]
    step = pl.program_id(0)
    slots = held.shape[0]
    own_slots = slots // 2
    sources = pick_ref.shape[0]
    deep = sources // pieces
    capacity = held.shape[1] // sources
    hidden = down_ref.shape[1]

    @pl.when(step == 0)
    def _():
        for source in range(sources):
            piece = source // deep
            rows = jnp.concatenate(
                [
                    row_refs[piece * halves + index][source % deep, :count]
                    for index, count in enumerate(in_cuts)
                ],
                axis=0,
            )
            rows = jnp.dot(
                pick_ref[source], rows, preferred_element_type=jnp.float32
            ).astype(jnp.bfloat16)
            for slot in range(slots):
                held[slot, source * capacity : (source + 1) * capacity] = rows[
                    slot * capacity : (slot + 1) * capacity
                ]

    def run(up, down):
        gate_up = jnp.dot(held[step], up[0], preferred_element_type=jnp.float32)
        active = (
            jax.nn.silu(gate_up[:, :hidden]) * gate_up[:, hidden:] * share_ref[step]
        ).astype(jnp.bfloat16)
        out_ref[step] = jnp.dot(active, down[0], preferred_element_type=jnp.float32).astype(
            jnp.bfloat16
        )

    @pl.when(step < own_slots)
    def _():
        run(up_ref, down_ref)

    @pl.when(step >= own_slots)
    def _():
        run(up_other_ref, down_other_ref)


def run_experts(rows, pick, share, ups, downs, in_cuts, after):
    pieces, halves = len(rows), len(rows[0])
    width = rows[0][0].shape[2]
    own_slots, _, double = ups[0].shape
    hidden = double // 2
    slots = 2 * own_slots
    places = share.shape[1]

    def own(j):
        return (jnp.minimum(j, own_slots - 1), 0, 0)

    def other(j):
        return (jnp.maximum(j - own_slots, 0), 0, 0)

    return pl.pallas_call(
        functools.partial(expert_kernel, pieces, tuple(in_cuts), len(after)),
        grid=(slots,),
        in_specs=[vmem_spec()] * (pieces * halves + 2)
        + [
            pl.BlockSpec((1, width, double), own),
            pl.BlockSpec((1, width, double), other),
            pl.BlockSpec((1, hidden, width), own),
            pl.BlockSpec((1, hidden, width), other),
        ]
        + [pl.BlockSpec(memory_space=pl.ANY)] * len(after),
        out_specs=vmem_spec(),
        out_shape=jax.ShapeDtypeStruct((slots, places, width), jnp.bfloat16),
        scratch_shapes=[pltpu.VMEM((slots, places, width), jnp.bfloat16)],
        compiler_params=params(44),
        cost_estimate=pl.CostEstimate(
            flops=10 * slots * places * width * hidden,
            bytes_accessed=26_000_000,
            transcendentals=slots * places * hidden,
        ),
        name="run_experts",
    )(*[r for piece in rows for r in piece], pick, share, ups[0], ups[1], downs[0], downs[1], *after)


def mix_kernel(pieces, out_cuts, held_ref, back_ref, *refs):
    count = len(out_cuts)
    out_refs = refs[-pieces * count :]
    slots, places, _ = held_ref.shape
    sources = back_ref.shape[0]
    deep = sources // pieces
    capacity = places // sources
    for source in range(sources):
        rows = jnp.concatenate(
            [
                held_ref[slot, source * capacity : (source + 1) * capacity]
                for slot in range(slots)
            ],
            axis=0,
        )
        mixed = jnp.dot(back_ref[source], rows, preferred_element_type=jnp.float32)
        start = 0
        for index, cut in enumerate(out_cuts):
            ref = out_refs[source // deep * count + index]
            ref[source % deep] = mixed[start : start + cut].astype(jnp.bfloat16)
            start += cut


def mix_rows(held, back, pieces, out_cuts, after):
    width = held.shape[2]
    deep = back.shape[0] // pieces
    flat = pl.pallas_call(
        functools.partial(mix_kernel, pieces, tuple(out_cuts)),
        in_specs=[vmem_spec()] * 2 + [pl.BlockSpec(memory_space=pl.ANY)] * len(after),
        out_specs=[vmem_spec()] * (pieces * len(out_cuts)),
        out_shape=[jax.ShapeDtypeStruct((deep, c, width), jnp.bfloat16) for c in out_cuts]
        * pieces,
        compiler_params=params(24),
        cost_estimate=pl.CostEstimate(
            flops=2_000_000_000, bytes_accessed=6_000_000, transcendentals=0
        ),
        name="mix_rows",
    )(held, back, *after)
    count = len(out_cuts)
    return [flat[i * count : (i + 1) * count] for i in range(pieces)]


def stack_kernel(count, *refs):
    out_ref = refs[-1]
    for index in range(count):
        out_ref[index] = refs[index][...]


def stack_rows(parts, after):
    return pl.pallas_call(
        functools.partial(stack_kernel, len(parts)),
        in_specs=[vmem_spec()] * len(parts) + [pl.BlockSpec(memory_space=pl.ANY)] * len(after),
        out_specs=vmem_spec(),
        out_shape=jax.ShapeDtypeStruct((len(parts), *parts[0].shape), parts[0].dtype),
        compiler_params=params(16),
        name="stack_rows",
    )(*parts, *after)


def chip_shape(chips):
    depth = 4 if chips % 4 == 0 else 1
    plane = chips // depth
    side = math.isqrt(plane)
    while plane % side:
        side -= 1
    return depth, plane // side, side


def make_shift(chips, cores):
    depth, tall, wide = chip_shape(chips)
    swap = tall == wide
    sizes = {"z": depth, "a": tall, "b": wide}

    def pairs(role, offset):
        out = []
        for z in range(depth):
            for y in range(tall):
                for x in range(wide):
                    for core in range(cores):
                        axis = role
                        if swap and core % 2 == 1:
                            axis = {"z": "z", "a": "b", "b": "a"}[role]
                        to_z, to_y, to_x = z, y, x
                        if axis == "z":
                            to_z = z ^ offset
                        elif axis == "a":
                            to_y = (y + offset) % tall
                        else:
                            to_x = (x + offset) % wide
                        source = ((z * tall + y) * wide + x) * cores + core
                        target = ((to_z * tall + to_y) * wide + to_x) * cores + core
                        out.append((source, target))
        return out

    def shift(value, role, offset):
        if role != "z":
            offset %= sizes[role]
        return lax.ppermute(value, BOTH, pairs(role, offset))

    return shift, sizes


def gather_line(value, shift, sizes):
    return [value] + [shift(value, "z", k) for k in range(1, sizes["z"])]


def scatter_line(line, shift, sizes):
    step = 1
    while step < sizes["z"]:
        kept = [k for k in range(0, sizes["z"], step) if not k & step]
        if len(kept) == 1:
            arrived = [shift(add_all(line[step]), "z", step)]
        else:
            arrived = shift(jnp.stack([add_all(line[k | step]) for k in kept]), "z", step)
        for place, k in enumerate(kept):
            line[k] = line[k] + [arrived[place]]
        step *= 2
    return line[0]


def gather_planes(line, shift, sizes, before):
    plane = [line] + [shift(line, "a", j) for j in range(1, sizes["a"])]
    forwarded = plane[1:]
    if before:
        forwarded, _ = lax.optimization_barrier((forwarded, before))
    return [plane] + [
        [shift(v, "b", k) for v in [line, *forwarded]] for k in range(1, sizes["b"])
    ]


def add_all(terms):
    total = terms[0].astype(jnp.float32)
    for term in terms[1:]:
        total = total + term.astype(jnp.float32)
    return total.astype(terms[0].dtype)


def leave_along_a(plane, shift):
    return [plane[0]] + [shift(v, "a", -j) for j, v in enumerate(plane) if j]


def scatter_plane(terms, shift, sizes):
    return scatter_line({i: [t[i] for t in terms] for i in range(sizes["z"])}, shift, sizes)


def scatter_chunks(own, others, shift, sizes):
    sums = []
    for terms, sending in zip(own, others):
        found = scatter_plane(terms, shift, sizes)
        for k, plane in enumerate(sending):
            part = scatter_plane(leave_along_a(plane, shift), shift, sizes)
            found = found + [shift(add_all(part), "b", -k - 1)]
        sums.append(add_all(found))
    total = jnp.zeros((sum(v.shape[0] for v in sums), sums[0].shape[1]), sums[0].dtype)
    first = 0
    for value in sums:
        total = lax.dynamic_update_slice(total, value, (first, 0))
        first += value.shape[0]
    return total


def rope_tables(positions):
    half = HEAD // 2
    frequency = rope_base ** (-jnp.arange(half, dtype=jnp.float32) / half)
    angles = positions.astype(jnp.float32)[:, None] * frequency[None, :]
    cosine, sine = jnp.cos(angles), jnp.sin(angles)
    return (
        jnp.concatenate([cosine] * 4, axis=1),
        jnp.concatenate([-sine, sine, -sine, sine], axis=1),
    )


def shards(
    tokens,
    attn_gain,
    w_qkv,
    w_out,
    k_cache,
    v_cache,
    cache_len,
    ffn_gain,
    routes,
    route_scores,
    replica_slot,
    expert_up,
    expert_down,
):
    row_count, top_count = routes.shape
    chips, cores = lax.axis_size("req"), lax.axis_size("seq")
    seq_index = lax.axis_index("seq")
    length = cache_len[0]
    slots_dev = expert_up.shape[0]
    slot_total = chips * cores * slots_dev
    capacity = 2 * ((row_count * top_count + slot_total - 1) // slot_total)
    shift, sizes = make_shift(chips, cores)

    def swap(value):
        return lax.ppermute(value, "seq", [(0, 1), (1, 0)])

    other_tokens = swap(tokens)
    k_other, v_other = swap(k_cache), swap(v_cache)
    experts = jnp.arange(replica_slot.shape[1], dtype=jnp.int32)
    slot_of = jnp.sum(
        jnp.where(routes[:, :, None] == experts, replica_slot[:, None, :], 0), axis=2
    )
    shares = route_scores / jnp.sum(route_scores, axis=1, keepdims=True)
    coarse = lax.reduce_precision(shares, 8, 7)
    table = jnp.concatenate([slot_of.astype(jnp.float32), coarse, shares - coarse], axis=1)
    table = table.astype(jnp.bfloat16).T.reshape(-1, tokens.shape[1])
    table = jnp.pad(table, ((0, -table.shape[0] % 8), (0, 0)))
    chip = lax.axis_index("req")
    chip_slots = jnp.arange(slots_dev, dtype=jnp.int32)
    slot_ids = jnp.concatenate(
        [
            (chip * cores + seq_index) * slots_dev + chip_slots,
            (chip * cores + 1 - seq_index) * slots_dev + chip_slots,
        ]
    ).astype(jnp.int32)

    row_index = jnp.arange(row_count, dtype=jnp.int32)
    cosine, sine = rope_tables(
        length
        + jnp.concatenate(
            [seq_index * row_count + row_index, (1 - seq_index) * row_count + row_index]
        )
    )
    queries, appended, other_span = project(
        tokens, other_tokens, attn_gain, cosine, sine, w_qkv, [k_other, v_other]
    )
    later_up, later_down, _ = lax.optimization_barrier((expert_up, expert_down, appended))
    up_other, down_other = swap(later_up), swap(later_down)
    half = row_count // 2
    filled, lines = [], []
    for index in range(2):
        attended, stream, expert_in = attend(
            cache_len,
            queries,
            (k_cache, k_other, v_cache, v_other),
            (appended, other_span),
            w_out,
            tokens,
            ffn_gain,
            index * half,
            half,
            [] if index else [table],
            filled,
            [up_other, down_other] if index else [],
        )
        filled = [attended, stream]
        sent = expert_in
        if index:
            sent, _ = lax.optimization_barrier((sent, lines[0][1:]))
        lines.append(gather_line(sent, shift, sizes))
    first, second = lines
    planes = gather_planes(stack_rows(first, [expert_in]), shift, sizes, second[1:])
    stacked = stack_rows(second, [plane[0] for plane in planes[1:]])
    halves = [planes, gather_planes(stacked, shift, sizes, [])]
    cuts = (row_count // 2, row_count - row_count // 2)
    own, others, held = [], [], None
    for index in range(sizes["b"]):
        pick, back, share = plan_routes(
            slot_ids, halves[0][index], half, row_count, capacity, top_count
        )
        held = run_experts(
            [[planes[index][j] for planes in halves] for j in range(sizes["a"])],
            pick,
            share,
            (expert_up, up_other),
            (expert_down, down_other),
            (half, row_count - half),
            [] if index == 0 else [held],
        )
        mixed = mix_rows(held, back, sizes["a"], cuts, [v for line in own for v in line[1:]])
        chunks = [[piece[i] for piece in mixed] for i in range(len(cuts))]
        if index == 0:
            chunks, _ = lax.optimization_barrier((chunks, halves[1][1:]))
            own = [leave_along_a(plane, shift) for plane in chunks]
        else:
            others.append(chunks)
    others = [[planes[i] for planes in others] for i in range(len(cuts))]
    expert_mix = scatter_chunks(own, others, shift, sizes)
    return (attended, stream, expert_mix, appended)


def solution(mesh):
    return jax.shard_map(
        shards,
        mesh=mesh,
        in_specs=(
            P(("req", "seq"), None),
            P(),
            P(),
            P(),
            P("req", "seq", None),
            P("req", "seq", None),
            P("req"),
            P(),
            P(("req", "seq"), None),
            P(("req", "seq"), None),
            P(("req", "seq"), None),
            P(("req", "seq"), None, None),
            P(("req", "seq"), None, None),
        ),
        out_specs=(
            P(("req", "seq"), None),
            P(("req", "seq"), None),
            P(("req", "seq"), None),
            P(("req", "seq"), None),
        ),
        check_vma=False,
    )
```

```python
import functools
import math

import jax
import jax.numpy as jnp
from jax import lax
from jax.experimental import pallas as pl
from jax.experimental.pallas import tpu as pltpu
from jax.sharding import PartitionSpec as P

HEADS = 24
KV_HEADS = 8
HEAD = 64
GROUP = HEADS // KV_HEADS
LANES = 128
PAIR = 2 * GROUP * HEAD

epsilon = 1e-06
residual_scale = 0.22
score_scale = 0.015625
rope_base = 10000.0
neg_big = -1e30

BOTH = ("req", "seq")


def vmem_spec():
    return pl.BlockSpec(memory_space=pltpu.VMEM)


def params(mebibytes):
    return pltpu.CompilerParams(vmem_limit_bytes=mebibytes * 2**20)


def qkv_kernel(own_ref, other_ref, gain_ref, cos_ref, sin_ref, w_ref, *refs):
    q_ref, kv_ref, kvo_ref, normed = refs[-4:]
    step = pl.program_id(0)
    rows = own_ref.shape[0]
    width = w_ref.shape[1]

    @pl.when(step == 0)
    def _():
        for index, ref in enumerate((own_ref, other_ref)):
            wide = ref[...].astype(jnp.float32)
            mean_square = jnp.mean(wide * wide, axis=-1, keepdims=True)
            normed[index * rows : (index + 1) * rows] = (
                wide * lax.rsqrt(mean_square + epsilon) * gain_ref[...][None, :]
            ).astype(jnp.bfloat16)

    def rotated(x, row_slice):
        lane = lax.broadcasted_iota(jnp.int32, x.shape, 1)
        low = (lane & (HEAD - 1)) < HEAD // 2
        swapped = jnp.where(
            low, pltpu.roll(x, width - HEAD // 2, 1), pltpu.roll(x, HEAD // 2, 1)
        )
        times = width // LANES
        cosine = jnp.concatenate([cos_ref[row_slice]] * times, axis=1)
        sine = jnp.concatenate([sin_ref[row_slice]] * times, axis=1)
        return x * cosine + swapped * sine

    @pl.when(step < 3)
    def _():
        x = jnp.dot(normed[:rows], w_ref[...], preferred_element_type=jnp.float32)
        q_ref[...] = (rotated(x, slice(0, rows)) * score_scale).astype(jnp.bfloat16)

    @pl.when(step == 3)
    def _():
        x = jnp.dot(normed[...], w_ref[...], preferred_element_type=jnp.float32)
        x = rotated(x, slice(0, 2 * rows)).astype(jnp.bfloat16)
        kv_ref[...] = x[:rows]
        kvo_ref[...] = x[rows:]

    @pl.when(step == 4)
    def _():
        x = jnp.dot(normed[...], w_ref[...], preferred_element_type=jnp.float32)
        x = x.astype(jnp.bfloat16)
        kv_ref[...] = x[:rows]
        kvo_ref[...] = x[rows:]


def project(own, other, gain, cosine, sine, w_qkv, after):
    rows, width = own.shape
    tile = KV_HEADS * HEAD
    return pl.pallas_call(
        qkv_kernel,
        grid=(5,),
        in_specs=[vmem_spec()] * 5
        + [pl.BlockSpec((width, tile), lambda i: (0, i))]
        + [pl.BlockSpec(memory_space=pl.ANY)] * len(after),
        out_specs=[
            pl.BlockSpec((rows, tile), lambda i: (0, jnp.minimum(i, 2))),
            pl.BlockSpec((rows, tile), lambda i: (0, jnp.maximum(i - 3, 0))),
            pl.BlockSpec((rows, tile), lambda i: (0, jnp.maximum(i - 3, 0))),
        ],
        out_shape=[
            jax.ShapeDtypeStruct((rows, HEADS * HEAD), jnp.bfloat16),
            jax.ShapeDtypeStruct((rows, 2 * tile), jnp.bfloat16),
            jax.ShapeDtypeStruct((rows, 2 * tile), jnp.bfloat16),
        ],
        scratch_shapes=[pltpu.VMEM((2 * rows, width), jnp.bfloat16)],
        compiler_params=params(58),
        cost_estimate=pl.CostEstimate(
            flops=2 * rows * width * 3584, bytes_accessed=9_500_000, transcendentals=0
        ),
        name="project_rows",
    )(own, other, gain, cosine, sine, w_qkv, *after)


def attend_kernel(first_row, riders, extra, place_ref, q_ref, kc_ref, kco_ref, vc_ref, vco_ref, ks_ref, kso_ref, vs_ref, vso_ref, w_out_ref, tokens_ref, gain_ref, *refs):
    attended_ref, stream_ref, expert_in_ref, keys, values, wide_q, total = refs[riders + extra :]
    step = pl.program_id(0)
    rows = q_ref.shape[0]
    cached = kc_ref.shape[1]
    span = ks_ref.shape[0]
    seq_index = lax.axis_index("seq")
    length = place_ref[0]

    @pl.when(step == 0)
    def _():
        position = lax.broadcasted_iota(jnp.int32, (cached, LANES), 0)
        for index, half in enumerate((seq_index, 1 - seq_index)):
            visible = position + half * cached < length
            keys[index * cached : (index + 1) * cached, LANES:] = jnp.where(
                visible, 0.0, neg_big
            ).astype(jnp.bfloat16)
        key = lax.broadcasted_iota(jnp.int32, (span, LANES), 0)
        row = lax.broadcasted_iota(jnp.int32, (span, LANES), 1)
        keys[2 * cached : 2 * cached + span, LANES:] = jnp.where(key <= row, 0.0, neg_big).astype(
            jnp.bfloat16
        )
        keys[2 * cached + span :, LANES:] = jnp.where(
            jnp.zeros((span, LANES), jnp.int32) < seq_index, 0.0, neg_big
        ).astype(jnp.bfloat16)
        values[:, LANES:] = jnp.ones((values.shape[0], LANES), jnp.bfloat16)
        row = lax.broadcasted_iota(jnp.int32, (rows, LANES), 0) + first_row
        lane = lax.broadcasted_iota(jnp.int32, (rows, LANES), 1)
        chosen = jnp.where(row == lane, 1.0, 0.0).astype(jnp.bfloat16)
        for head in range(2 * GROUP):
            wide_q[head * rows : (head + 1) * rows, LANES:] = chosen

    for ref, parts in ((keys, (kc_ref, kco_ref)), (values, (vc_ref, vco_ref))):
        for index, part in enumerate(parts):
            ref[index * cached : (index + 1) * cached, :LANES] = part[0]
    for ref, parts in ((keys, (ks_ref, kso_ref)), (values, (vs_ref, vso_ref))):
        for index, part in enumerate(parts):
            start = 2 * cached + index * span
            ref[start : start + span, :LANES] = part[...]

    low = lax.broadcasted_iota(jnp.int32, (rows, LANES), 1) < HEAD
    tiles = [q_ref[:, i * LANES : (i + 1) * LANES].astype(jnp.float32) for i in range(3)]
    parts = [
        jnp.where(low, tiles[0], 0.0),
        jnp.where(low, pltpu.roll(tiles[0], HEAD, 1), 0.0),
        jnp.where(low, tiles[1], 0.0),
        jnp.where(low, 0.0, tiles[1]),
        jnp.where(low, 0.0, pltpu.roll(tiles[2], HEAD, 1)),
        jnp.where(low, 0.0, tiles[2]),
    ]
    for head, part in enumerate(parts):
        wide_q[head * rows : (head + 1) * rows, :LANES] = part.astype(jnp.bfloat16)

    heads = []
    batch = 2 * GROUP * rows
    for first in range(0, 2 * GROUP * rows, batch):
        scores = lax.dot_general(
            wide_q[first : first + batch],
            keys[...],
            (((1,), (1,)), ((), ())),
            preferred_element_type=jnp.float32,
        )
        best = jnp.max(scores, axis=-1, keepdims=True)
        weights = jnp.exp(scores - best).astype(jnp.bfloat16)
        sums = jnp.dot(weights, values[...], preferred_element_type=jnp.float32)
        mean = sums[:, :LANES] / sums[:, LANES:]
        heads += [mean[i : i + rows] for i in range(0, batch, rows)]
    merged = jnp.concatenate(
        [
            jnp.where(low, heads[0], pltpu.roll(heads[1], HEAD, 1)),
            jnp.where(low, heads[2], heads[3]),
            jnp.where(low, pltpu.roll(heads[4], HEAD, 1), heads[5]),
        ],
        axis=1,
    ).astype(jnp.bfloat16)
    attended_ref[...] = merged
    product = jnp.dot(merged, w_out_ref[...], preferred_element_type=jnp.float32)

    @pl.when(step == 0)
    def _():
        total[...] = product

    @pl.when(step > 0)
    def _():
        total[...] += product

    @pl.when(step == pl.num_programs(0) - 1)
    def _():
        stream = (tokens_ref[...].astype(jnp.float32) + residual_scale * total[...]).astype(
            jnp.bfloat16
        )
        stream_ref[...] = stream
        wide = stream.astype(jnp.float32)
        mean_square = jnp.mean(wide * wide, axis=-1, keepdims=True)
        sent = (wide * lax.rsqrt(mean_square + epsilon) * gain_ref[...][None, :]).astype(
            jnp.bfloat16
        )
        expert_in_ref[...] = jnp.concatenate([sent, *[r[...] for r in refs[:riders]]], axis=0)


def attend(place, queries, caches, spans, w_out, tokens, gain, first_row, rows, riders, filled, after):
    k_cache, k_other, v_cache, v_other = caches
    own_span, other_span = spans
    cached = k_cache.shape[1]
    span, width = tokens.shape
    pairs = KV_HEADS // 2
    part = first_row // rows
    key_count = 2 * cached + 2 * span
    cache_spec = pl.BlockSpec((1, cached, LANES), lambda j: (0, 0, j))
    key_spec = pl.BlockSpec((span, LANES), lambda j: (0, j))
    value_spec = pl.BlockSpec((span, LANES), lambda j: (0, pairs + j))
    extra = [*filled, *after]
    sent = rows + sum(r.shape[0] for r in riders)
    return pl.pallas_call(
        functools.partial(attend_kernel, first_row, len(riders), len(extra)),
        grid=(pairs,),
        in_specs=[
            pl.BlockSpec(memory_space=pltpu.SMEM),
            pl.BlockSpec((rows, PAIR), lambda j: (part, j)),
            cache_spec,
            cache_spec,
            cache_spec,
            cache_spec,
            key_spec,
            key_spec,
            value_spec,
            value_spec,
            pl.BlockSpec((PAIR, width), lambda j: (j, 0)),
            pl.BlockSpec((rows, width), lambda j: (part, 0)),
            vmem_spec(),
        ]
        + [vmem_spec()] * len(riders)
        + [pl.BlockSpec(memory_space=pl.ANY)] * len(extra),
        out_specs=[
            pl.BlockSpec((rows, PAIR), lambda j: (part, j)),
            pl.BlockSpec((rows, width), lambda j: (part, 0)),
            pl.BlockSpec((sent, width), lambda j: (0, 0)),
        ],
        out_shape=[
            jax.ShapeDtypeStruct((span, HEADS * HEAD), jnp.bfloat16),
            jax.ShapeDtypeStruct((span, width), jnp.bfloat16),
            jax.ShapeDtypeStruct((sent, width), jnp.bfloat16),
        ],
        input_output_aliases={13 + len(riders) + i: i for i in range(len(filled))},
        scratch_shapes=[
            pltpu.VMEM((key_count, 2 * LANES), jnp.bfloat16),
            pltpu.VMEM((key_count, 2 * LANES), jnp.bfloat16),
            pltpu.VMEM((2 * GROUP * rows, 2 * LANES), jnp.bfloat16),
            pltpu.VMEM((rows, width), jnp.float32),
        ],
        compiler_params=params(58),
        cost_estimate=pl.CostEstimate(
            flops=16 * HEADS * rows * key_count * LANES,
            bytes_accessed=10_000_000,
            transcendentals=HEADS * rows * key_count,
        ),
        name="attend_rows",
    )(
        place,
        queries,
        k_cache,
        k_other,
        v_cache,
        v_other,
        own_span,
        other_span,
        own_span,
        other_span,
        w_out,
        tokens,
        gain,
        *riders,
        *extra,
    )


def plan_kernel(pieces, first, capacity, top, slot_ref, *refs):
    pick_ref, back_ref, share_ref = refs[pieces:]
    slots = slot_ref.shape[0]
    sources, _, tokens = pick_ref.shape
    deep = sources // pieces
    earlier = jnp.where(
        lax.broadcasted_iota(jnp.int32, (tokens, tokens), 0)
        < lax.broadcasted_iota(jnp.int32, (tokens, tokens), 1),
        1.0,
        0.0,
    ).astype(jnp.bfloat16)
    place = lax.broadcasted_iota(jnp.int32, (capacity, tokens), 0).astype(jnp.float32)
    hot_rows, share_lines = [], []
    for source in range(sources):
        packed = refs[source // deep][source % deep][first:].astype(jnp.float32)
        across = packed.shape[1] // tokens
        lines = [
            packed[i // across : i // across + 1, i % across * tokens : (i % across + 1) * tokens]
            for i in range(3 * top)
        ]
        ids = jnp.concatenate(lines[:top], axis=0)
        shares = jnp.concatenate(lines[top : 2 * top], axis=0)
        shares += jnp.concatenate(lines[2 * top :], axis=0)
        for slot in range(slots):
            match = ids == slot_ref[slot].astype(jnp.float32)
            hot_rows.append(jnp.max(jnp.where(match, 1.0, 0.0), axis=0, keepdims=True))
            share_lines.append(jnp.sum(jnp.where(match, shares, 0.0), axis=0, keepdims=True))
    hot = jnp.concatenate(hot_rows, axis=0)
    rank = jnp.dot(hot.astype(jnp.bfloat16), earlier, preferred_element_type=jnp.float32)
    rank = jnp.where(hot > 0.0, rank, -1.0)
    for source in range(sources):
        picks = []
        for slot in range(slots):
            line = source * slots + slot
            chosen = jnp.where(place == rank[line : line + 1], 1.0, 0.0)
            share_ref[slot, source * capacity : (source + 1) * capacity] = jnp.sum(
                chosen * share_lines[line], axis=1, keepdims=True
            )
            picks.append(chosen)
        picked = jnp.concatenate(picks, axis=0)
        pick_ref[source] = picked.astype(jnp.bfloat16)
        back_ref[source] = jnp.transpose(picked).astype(jnp.bfloat16)


def plan_routes(slot_ids, pieces, first, tokens, capacity, top):
    slots = slot_ids.shape[0]
    sources = sum(p.shape[0] for p in pieces)
    return pl.pallas_call(
        functools.partial(plan_kernel, len(pieces), first, capacity, top),
        in_specs=[pl.BlockSpec(memory_space=pltpu.SMEM)] + [vmem_spec()] * len(pieces),
        out_specs=[vmem_spec()] * 3,
        out_shape=[
            jax.ShapeDtypeStruct((sources, slots * capacity, tokens), jnp.bfloat16),
            jax.ShapeDtypeStruct((sources, tokens, slots * capacity), jnp.bfloat16),
            jax.ShapeDtypeStruct((slots, sources * capacity, 1), jnp.float32),
        ],
        compiler_params=params(24),
        cost_estimate=pl.CostEstimate(
            flops=1_000_000_000, bytes_accessed=2_000_000, transcendentals=0
        ),
        name="plan_routes",
    )(slot_ids, *pieces)


def expert_kernel(pieces, in_cuts, extra, *refs):
    halves = len(in_cuts)
    row_refs = refs[: pieces * halves]
    pick_ref, share_ref, up_ref, up_other_ref, down_ref, down_other_ref = refs[
        pieces * halves : pieces * halves + 6
    ]
    out_ref, held = refs[-2:]
    step = pl.program_id(0)
    slots = held.shape[0]
    own_slots = slots // 2
    sources = pick_ref.shape[0]
    deep = sources // pieces
    capacity = held.shape[1] // sources
    hidden = down_ref.shape[1]

    @pl.when(step == 0)
    def _():
        for source in range(sources):
            piece = source // deep
            rows = jnp.concatenate(
                [
                    row_refs[piece * halves + index][source % deep, :count]
                    for index, count in enumerate(in_cuts)
                ],
                axis=0,
            )
            rows = jnp.dot(
                pick_ref[source], rows, preferred_element_type=jnp.float32
            ).astype(jnp.bfloat16)
            for slot in range(slots):
                held[slot, source * capacity : (source + 1) * capacity] = rows[
                    slot * capacity : (slot + 1) * capacity
                ]

    def run(up, down):
        gate_up = jnp.dot(held[step], up[0], preferred_element_type=jnp.float32)
        active = (
            jax.nn.silu(gate_up[:, :hidden]) * gate_up[:, hidden:] * share_ref[step]
        ).astype(jnp.bfloat16)
        out_ref[step] = jnp.dot(active, down[0], preferred_element_type=jnp.float32).astype(
            jnp.bfloat16
        )

    @pl.when(step < own_slots)
    def _():
        run(up_ref, down_ref)

    @pl.when(step >= own_slots)
    def _():
        run(up_other_ref, down_other_ref)


def run_experts(rows, pick, share, ups, downs, in_cuts, after):
    pieces, halves = len(rows), len(rows[0])
    width = rows[0][0].shape[2]
    own_slots, _, double = ups[0].shape
    hidden = double // 2
    slots = 2 * own_slots
    places = share.shape[1]

    def own(j):
        return (jnp.minimum(j, own_slots - 1), 0, 0)

    def other(j):
        return (jnp.maximum(j - own_slots, 0), 0, 0)

    return pl.pallas_call(
        functools.partial(expert_kernel, pieces, tuple(in_cuts), len(after)),
        grid=(slots,),
        in_specs=[vmem_spec()] * (pieces * halves + 2)
        + [
            pl.BlockSpec((1, width, double), own),
            pl.BlockSpec((1, width, double), other),
            pl.BlockSpec((1, hidden, width), own),
            pl.BlockSpec((1, hidden, width), other),
        ]
        + [pl.BlockSpec(memory_space=pl.ANY)] * len(after),
        out_specs=vmem_spec(),
        out_shape=jax.ShapeDtypeStruct((slots, places, width), jnp.bfloat16),
        scratch_shapes=[pltpu.VMEM((slots, places, width), jnp.bfloat16)],
        compiler_params=params(44),
        cost_estimate=pl.CostEstimate(
            flops=10 * slots * places * width * hidden,
            bytes_accessed=26_000_000,
            transcendentals=slots * places * hidden,
        ),
        name="run_experts",
    )(*[r for piece in rows for r in piece], pick, share, ups[0], ups[1], downs[0], downs[1], *after)


def mix_kernel(pieces, out_cuts, held_ref, back_ref, *refs):
    count = len(out_cuts)
    out_refs = refs[-pieces * count :]
    slots, places, _ = held_ref.shape
    sources = back_ref.shape[0]
    deep = sources // pieces
    capacity = places // sources
    for source in range(sources):
        rows = jnp.concatenate(
            [
                held_ref[slot, source * capacity : (source + 1) * capacity]
                for slot in range(slots)
            ],
            axis=0,
        )
        mixed = jnp.dot(back_ref[source], rows, preferred_element_type=jnp.float32)
        start = 0
        for index, cut in enumerate(out_cuts):
            ref = out_refs[source // deep * count + index]
            ref[source % deep] = mixed[start : start + cut].astype(jnp.bfloat16)
            start += cut


def mix_rows(held, back, pieces, out_cuts, after):
    width = held.shape[2]
    deep = back.shape[0] // pieces
    flat = pl.pallas_call(
        functools.partial(mix_kernel, pieces, tuple(out_cuts)),
        in_specs=[vmem_spec()] * 2 + [pl.BlockSpec(memory_space=pl.ANY)] * len(after),
        out_specs=[vmem_spec()] * (pieces * len(out_cuts)),
        out_shape=[jax.ShapeDtypeStruct((deep, c, width), jnp.bfloat16) for c in out_cuts]
        * pieces,
        compiler_params=params(24),
        cost_estimate=pl.CostEstimate(
            flops=2_000_000_000, bytes_accessed=6_000_000, transcendentals=0
        ),
        name="mix_rows",
    )(held, back, *after)
    count = len(out_cuts)
    return [flat[i * count : (i + 1) * count] for i in range(pieces)]


def stack_kernel(count, *refs):
    out_ref = refs[-1]
    for index in range(count):
        out_ref[index] = refs[index][...]


def stack_rows(parts, after):
    return pl.pallas_call(
        functools.partial(stack_kernel, len(parts)),
        in_specs=[vmem_spec()] * len(parts) + [pl.BlockSpec(memory_space=pl.ANY)] * len(after),
        out_specs=vmem_spec(),
        out_shape=jax.ShapeDtypeStruct((len(parts), *parts[0].shape), parts[0].dtype),
        compiler_params=params(16),
        name="stack_rows",
    )(*parts, *after)


def chip_shape(chips):
    depth = 4 if chips % 4 == 0 else 1
    plane = chips // depth
    side = math.isqrt(plane)
    while plane % side:
        side -= 1
    return depth, plane // side, side


def make_shift(chips, cores):
    depth, tall, wide = chip_shape(chips)
    swap = tall == wide
    sizes = {"z": depth, "a": tall, "b": wide}

    def pairs(role, offset):
        out = []
        for z in range(depth):
            for y in range(tall):
                for x in range(wide):
                    for core in range(cores):
                        axis = role
                        if swap and core % 2 == 1:
                            axis = {"z": "z", "a": "b", "b": "a"}[role]
                        to_z, to_y, to_x = z, y, x
                        if axis == "z":
                            to_z = z ^ offset
                        elif axis == "a":
                            to_y = (y + offset) % tall
                        else:
                            to_x = (x + offset) % wide
                        source = ((z * tall + y) * wide + x) * cores + core
                        target = ((to_z * tall + to_y) * wide + to_x) * cores + core
                        out.append((source, target))
        return out

    def shift(value, role, offset):
        if role != "z":
            offset %= sizes[role]
        return lax.ppermute(value, BOTH, pairs(role, offset))

    return shift, sizes


def gather_line(value, shift, sizes):
    return [value] + [shift(value, "z", k) for k in range(1, sizes["z"])]


def scatter_line(line, shift, sizes):
    step = 1
    while step < sizes["z"]:
        kept = [k for k in range(0, sizes["z"], step) if not k & step]
        if len(kept) == 1:
            arrived = [shift(add_all(line[step]), "z", step)]
        else:
            arrived = shift(jnp.stack([add_all(line[k | step]) for k in kept]), "z", step)
        for place, k in enumerate(kept):
            line[k] = line[k] + [arrived[place]]
        step *= 2
    return line[0]


def gather_planes(line, shift, sizes, before):
    plane = [line] + [shift(line, "a", j) for j in range(1, sizes["a"])]
    forwarded = plane[1:]
    if before:
        forwarded, _ = lax.optimization_barrier((forwarded, before))
    return [plane] + [
        [shift(v, "b", k) for v in [line, *forwarded]] for k in range(1, sizes["b"])
    ]


def add_all(terms):
    total = terms[0].astype(jnp.float32)
    for term in terms[1:]:
        total = total + term.astype(jnp.float32)
    return total.astype(terms[0].dtype)


def leave_along_a(plane, shift):
    return [plane[0]] + [shift(v, "a", -j) for j, v in enumerate(plane) if j]


def scatter_plane(terms, shift, sizes):
    return scatter_line({i: [t[i] for t in terms] for i in range(sizes["z"])}, shift, sizes)


def scatter_chunks(own, others, shift, sizes):
    sums = []
    for index, (terms, sending) in enumerate(zip(own, others)):
        planes = [leave_along_a(plane, shift) for plane in sending]
        if index == len(own) - 1:
            for k, part in enumerate(planes):
                terms = terms + [shift(add_all(part), "b", -k - 1)]
            found = scatter_plane(terms, shift, sizes)
        else:
            found = scatter_plane(terms, shift, sizes)
            for k, part in enumerate(planes):
                total = add_all(scatter_plane(part, shift, sizes))
                found = found + [shift(total, "b", -k - 1)]
        sums.append(add_all(found))
    total = jnp.zeros((sum(v.shape[0] for v in sums), sums[0].shape[1]), sums[0].dtype)
    first = 0
    for value in sums:
        total = lax.dynamic_update_slice(total, value, (first, 0))
        first += value.shape[0]
    return total


def rope_tables(positions):
    half = HEAD // 2
    frequency = rope_base ** (-jnp.arange(half, dtype=jnp.float32) / half)
    angles = positions.astype(jnp.float32)[:, None] * frequency[None, :]
    cosine, sine = jnp.cos(angles), jnp.sin(angles)
    return (
        jnp.concatenate([cosine] * 4, axis=1),
        jnp.concatenate([-sine, sine, -sine, sine], axis=1),
    )


def shards(
    tokens,
    attn_gain,
    w_qkv,
    w_out,
    k_cache,
    v_cache,
    cache_len,
    ffn_gain,
    routes,
    route_scores,
    replica_slot,
    expert_up,
    expert_down,
):
    row_count, top_count = routes.shape
    chips, cores = lax.axis_size("req"), lax.axis_size("seq")
    seq_index = lax.axis_index("seq")
    length = cache_len[0]
    slots_dev = expert_up.shape[0]
    slot_total = chips * cores * slots_dev
    capacity = 2 * ((row_count * top_count + slot_total - 1) // slot_total)
    shift, sizes = make_shift(chips, cores)

    def swap(value):
        return lax.ppermute(value, "seq", [(0, 1), (1, 0)])

    other_tokens = swap(tokens)
    k_other, v_other = swap(k_cache), swap(v_cache)
    experts = jnp.arange(replica_slot.shape[1], dtype=jnp.int32)
    slot_of = jnp.sum(
        jnp.where(routes[:, :, None] == experts, replica_slot[:, None, :], 0), axis=2
    )
    shares = route_scores / jnp.sum(route_scores, axis=1, keepdims=True)
    coarse = lax.reduce_precision(shares, 8, 7)
    table = jnp.concatenate([slot_of.astype(jnp.float32), coarse, shares - coarse], axis=1)
    table = table.astype(jnp.bfloat16).T.reshape(-1, tokens.shape[1])
    table = jnp.pad(table, ((0, -table.shape[0] % 8), (0, 0)))
    chip = lax.axis_index("req")
    chip_slots = jnp.arange(slots_dev, dtype=jnp.int32)
    slot_ids = jnp.concatenate(
        [
            (chip * cores + seq_index) * slots_dev + chip_slots,
            (chip * cores + 1 - seq_index) * slots_dev + chip_slots,
        ]
    ).astype(jnp.int32)

    row_index = jnp.arange(row_count, dtype=jnp.int32)
    cosine, sine = rope_tables(
        length
        + jnp.concatenate(
            [seq_index * row_count + row_index, (1 - seq_index) * row_count + row_index]
        )
    )
    queries, appended, other_span = project(
        tokens, other_tokens, attn_gain, cosine, sine, w_qkv, [k_other, v_other]
    )
    later_up, later_down, _ = lax.optimization_barrier((expert_up, expert_down, appended))
    up_other, down_other = swap(later_up), swap(later_down)
    half = row_count // 2
    filled, lines = [], []
    for index in range(2):
        attended, stream, expert_in = attend(
            cache_len,
            queries,
            (k_cache, k_other, v_cache, v_other),
            (appended, other_span),
            w_out,
            tokens,
            ffn_gain,
            index * half,
            half,
            [] if index else [table],
            filled,
            [up_other, down_other] if index else [],
        )
        filled = [attended, stream]
        sent = expert_in
        if index:
            sent, _ = lax.optimization_barrier((sent, lines[0][1:]))
        lines.append(gather_line(sent, shift, sizes))
    first, second = lines
    planes = gather_planes(stack_rows(first, [expert_in]), shift, sizes, second[1:])
    stacked = stack_rows(second, [plane[0] for plane in planes[1:]])
    halves = [planes, gather_planes(stacked, shift, sizes, [])]
    cuts = (5 * row_count // 8, row_count - 5 * row_count // 8)
    own, others, held = [], [], None
    for index in range(sizes["b"]):
        pick, back, share = plan_routes(
            slot_ids, halves[0][index], half, row_count, capacity, top_count
        )
        held = run_experts(
            [[planes[index][j] for planes in halves] for j in range(sizes["a"])],
            pick,
            share,
            (expert_up, up_other),
            (expert_down, down_other),
            (half, row_count - half),
            [held] if index else [v for plane in halves[0][1:] for v in plane],
        )
        mixed = mix_rows(held, back, sizes["a"], cuts, [v for line in own for v in line[1:]])
        chunks = [[piece[i] for piece in mixed] for i in range(len(cuts))]
        if index == 0:
            chunks, _ = lax.optimization_barrier((chunks, halves[1][1:]))
            own = [leave_along_a(plane, shift) for plane in chunks]
        else:
            others.append(chunks)
    others = [[planes[i] for planes in others] for i in range(len(cuts))]
    own, _ = lax.optimization_barrier((own, held))
    expert_mix = scatter_chunks(own, others, shift, sizes)
    return (attended, stream, expert_mix, appended)


def solution(mesh):
    return jax.shard_map(
        shards,
        mesh=mesh,
        in_specs=(
            P(("req", "seq"), None),
            P(),
            P(),
            P(),
            P("req", "seq", None),
            P("req", "seq", None),
            P("req"),
            P(),
            P(("req", "seq"), None),
            P(("req", "seq"), None),
            P(("req", "seq"), None),
            P(("req", "seq"), None, None),
            P(("req", "seq"), None, None),
        ),
        out_specs=(
            P(("req", "seq"), None),
            P(("req", "seq"), None),
            P(("req", "seq"), None),
            P(("req", "seq"), None),
        ),
        check_vma=False,
    )
```

```python
import functools
import math

import jax
import jax.numpy as jnp
from jax import lax
from jax.experimental import pallas as pl
from jax.experimental.pallas import tpu as pltpu
from jax.sharding import PartitionSpec as P

HEADS = 24
KV_HEADS = 8
HEAD = 64
GROUP = HEADS // KV_HEADS
LANES = 128
PAIR = 2 * GROUP * HEAD

epsilon = 1e-06
residual_scale = 0.22
score_scale = 0.015625
rope_base = 10000.0
neg_big = -1e30

BOTH = ("req", "seq")


def vmem_spec():
    return pl.BlockSpec(memory_space=pltpu.VMEM)


def params(mebibytes):
    return pltpu.CompilerParams(vmem_limit_bytes=mebibytes * 2**20)


def qkv_kernel(own_ref, other_ref, gain_ref, cos_ref, sin_ref, w_ref, *refs):
    q_ref, kv_ref, kvo_ref, normed = refs[-4:]
    step = pl.program_id(0)
    rows = own_ref.shape[0]
    width = w_ref.shape[1]

    @pl.when(step == 0)
    def _():
        for index, ref in enumerate((own_ref, other_ref)):
            wide = ref[...].astype(jnp.float32)
            mean_square = jnp.mean(wide * wide, axis=-1, keepdims=True)
            normed[index * rows : (index + 1) * rows] = (
                wide * lax.rsqrt(mean_square + epsilon) * gain_ref[...][None, :]
            ).astype(jnp.bfloat16)

    def rotated(x, row_slice):
        lane = lax.broadcasted_iota(jnp.int32, x.shape, 1)
        low = (lane & (HEAD - 1)) < HEAD // 2
        swapped = jnp.where(
            low, pltpu.roll(x, width - HEAD // 2, 1), pltpu.roll(x, HEAD // 2, 1)
        )
        times = width // LANES
        cosine = jnp.concatenate([cos_ref[row_slice]] * times, axis=1)
        sine = jnp.concatenate([sin_ref[row_slice]] * times, axis=1)
        return x * cosine + swapped * sine

    @pl.when(step < 3)
    def _():
        x = jnp.dot(normed[:rows], w_ref[...], preferred_element_type=jnp.float32)
        q_ref[...] = (rotated(x, slice(0, rows)) * score_scale).astype(jnp.bfloat16)

    @pl.when(step == 3)
    def _():
        x = jnp.dot(normed[...], w_ref[...], preferred_element_type=jnp.float32)
        x = rotated(x, slice(0, 2 * rows)).astype(jnp.bfloat16)
        kv_ref[...] = x[:rows]
        kvo_ref[...] = x[rows:]

    @pl.when(step == 4)
    def _():
        x = jnp.dot(normed[...], w_ref[...], preferred_element_type=jnp.float32)
        x = x.astype(jnp.bfloat16)
        kv_ref[...] = x[:rows]
        kvo_ref[...] = x[rows:]


def project(own, other, gain, cosine, sine, w_qkv, after):
    rows, width = own.shape
    tile = KV_HEADS * HEAD
    return pl.pallas_call(
        qkv_kernel,
        grid=(5,),
        in_specs=[vmem_spec()] * 5
        + [pl.BlockSpec((width, tile), lambda i: (0, i))]
        + [pl.BlockSpec(memory_space=pl.ANY)] * len(after),
        out_specs=[
            pl.BlockSpec((rows, tile), lambda i: (0, jnp.minimum(i, 2))),
            pl.BlockSpec((rows, tile), lambda i: (0, jnp.maximum(i - 3, 0))),
            pl.BlockSpec((rows, tile), lambda i: (0, jnp.maximum(i - 3, 0))),
        ],
        out_shape=[
            jax.ShapeDtypeStruct((rows, HEADS * HEAD), jnp.bfloat16),
            jax.ShapeDtypeStruct((rows, 2 * tile), jnp.bfloat16),
            jax.ShapeDtypeStruct((rows, 2 * tile), jnp.bfloat16),
        ],
        scratch_shapes=[pltpu.VMEM((2 * rows, width), jnp.bfloat16)],
        compiler_params=params(58),
        cost_estimate=pl.CostEstimate(
            flops=2 * rows * width * 3584, bytes_accessed=9_500_000, transcendentals=0
        ),
        name="project_rows",
    )(own, other, gain, cosine, sine, w_qkv, *after)


def attend_kernel(first_row, riders, extra, place_ref, q_ref, kc_ref, kco_ref, vc_ref, vco_ref, ks_ref, kso_ref, vs_ref, vso_ref, w_out_ref, tokens_ref, gain_ref, *refs):
    attended_ref, stream_ref, expert_in_ref, keys, values, wide_q, total = refs[riders + extra :]
    step = pl.program_id(0)
    rows = q_ref.shape[0]
    cached = kc_ref.shape[1]
    span = ks_ref.shape[0]
    seq_index = lax.axis_index("seq")
    length = place_ref[0]

    @pl.when(step == 0)
    def _():
        position = lax.broadcasted_iota(jnp.int32, (cached, LANES), 0)
        for index, half in enumerate((seq_index, 1 - seq_index)):
            visible = position + half * cached < length
            keys[index * cached : (index + 1) * cached, LANES:] = jnp.where(
                visible, 0.0, neg_big
            ).astype(jnp.bfloat16)
        key = lax.broadcasted_iota(jnp.int32, (span, LANES), 0)
        row = lax.broadcasted_iota(jnp.int32, (span, LANES), 1)
        keys[2 * cached : 2 * cached + span, LANES:] = jnp.where(key <= row, 0.0, neg_big).astype(
            jnp.bfloat16
        )
        keys[2 * cached + span :, LANES:] = jnp.where(
            jnp.zeros((span, LANES), jnp.int32) < seq_index, 0.0, neg_big
        ).astype(jnp.bfloat16)
        values[:, LANES:] = jnp.ones((values.shape[0], LANES), jnp.bfloat16)
        row = lax.broadcasted_iota(jnp.int32, (rows, LANES), 0) + first_row
        lane = lax.broadcasted_iota(jnp.int32, (rows, LANES), 1)
        chosen = jnp.where(row == lane, 1.0, 0.0).astype(jnp.bfloat16)
        for head in range(2 * GROUP):
            wide_q[head * rows : (head + 1) * rows, LANES:] = chosen

    for ref, parts in ((keys, (kc_ref, kco_ref)), (values, (vc_ref, vco_ref))):
        for index, part in enumerate(parts):
            ref[index * cached : (index + 1) * cached, :LANES] = part[0]
    for ref, parts in ((keys, (ks_ref, kso_ref)), (values, (vs_ref, vso_ref))):
        for index, part in enumerate(parts):
            start = 2 * cached + index * span
            ref[start : start + span, :LANES] = part[...]

    low = lax.broadcasted_iota(jnp.int32, (rows, LANES), 1) < HEAD
    tiles = [q_ref[:, i * LANES : (i + 1) * LANES].astype(jnp.float32) for i in range(3)]
    parts = [
        jnp.where(low, tiles[0], 0.0),
        jnp.where(low, pltpu.roll(tiles[0], HEAD, 1), 0.0),
        jnp.where(low, tiles[1], 0.0),
        jnp.where(low, 0.0, tiles[1]),
        jnp.where(low, 0.0, pltpu.roll(tiles[2], HEAD, 1)),
        jnp.where(low, 0.0, tiles[2]),
    ]
    for head, part in enumerate(parts):
        wide_q[head * rows : (head + 1) * rows, :LANES] = part.astype(jnp.bfloat16)

    heads = []
    batch = 2 * GROUP * rows
    for first in range(0, 2 * GROUP * rows, batch):
        scores = lax.dot_general(
            wide_q[first : first + batch],
            keys[...],
            (((1,), (1,)), ((), ())),
            preferred_element_type=jnp.float32,
        )
        best = jnp.max(scores, axis=-1, keepdims=True)
        weights = jnp.exp(scores - best).astype(jnp.bfloat16)
        sums = jnp.dot(weights, values[...], preferred_element_type=jnp.float32)
        mean = sums[:, :LANES] / sums[:, LANES:]
        heads += [mean[i : i + rows] for i in range(0, batch, rows)]
    merged = jnp.concatenate(
        [
            jnp.where(low, heads[0], pltpu.roll(heads[1], HEAD, 1)),
            jnp.where(low, heads[2], heads[3]),
            jnp.where(low, pltpu.roll(heads[4], HEAD, 1), heads[5]),
        ],
        axis=1,
    ).astype(jnp.bfloat16)
    attended_ref[...] = merged
    product = jnp.dot(merged, w_out_ref[...], preferred_element_type=jnp.float32)

    @pl.when(step == 0)
    def _():
        total[...] = product

    @pl.when(step > 0)
    def _():
        total[...] += product

    @pl.when(step == pl.num_programs(0) - 1)
    def _():
        stream = (tokens_ref[...].astype(jnp.float32) + residual_scale * total[...]).astype(
            jnp.bfloat16
        )
        stream_ref[...] = stream
        wide = stream.astype(jnp.float32)
        mean_square = jnp.mean(wide * wide, axis=-1, keepdims=True)
        sent = (wide * lax.rsqrt(mean_square + epsilon) * gain_ref[...][None, :]).astype(
            jnp.bfloat16
        )
        expert_in_ref[...] = jnp.concatenate([sent, *[r[...] for r in refs[:riders]]], axis=0)


def attend(place, queries, caches, spans, w_out, tokens, gain, first_row, rows, riders, filled, after):
    k_cache, k_other, v_cache, v_other = caches
    own_span, other_span = spans
    cached = k_cache.shape[1]
    span, width = tokens.shape
    pairs = KV_HEADS // 2
    part = first_row // rows
    key_count = 2 * cached + 2 * span
    cache_spec = pl.BlockSpec((1, cached, LANES), lambda j: (0, 0, j))
    key_spec = pl.BlockSpec((span, LANES), lambda j: (0, j))
    value_spec = pl.BlockSpec((span, LANES), lambda j: (0, pairs + j))
    extra = [*filled, *after]
    sent = rows + sum(r.shape[0] for r in riders)
    return pl.pallas_call(
        functools.partial(attend_kernel, first_row, len(riders), len(extra)),
        grid=(pairs,),
        in_specs=[
            pl.BlockSpec(memory_space=pltpu.SMEM),
            pl.BlockSpec((rows, PAIR), lambda j: (part, j)),
            cache_spec,
            cache_spec,
            cache_spec,
            cache_spec,
            key_spec,
            key_spec,
            value_spec,
            value_spec,
            pl.BlockSpec((PAIR, width), lambda j: (j, 0)),
            pl.BlockSpec((rows, width), lambda j: (part, 0)),
            vmem_spec(),
        ]
        + [vmem_spec()] * len(riders)
        + [pl.BlockSpec(memory_space=pl.ANY)] * len(extra),
        out_specs=[
            pl.BlockSpec((rows, PAIR), lambda j: (part, j)),
            pl.BlockSpec((rows, width), lambda j: (part, 0)),
            pl.BlockSpec((sent, width), lambda j: (0, 0)),
        ],
        out_shape=[
            jax.ShapeDtypeStruct((span, HEADS * HEAD), jnp.bfloat16),
            jax.ShapeDtypeStruct((span, width), jnp.bfloat16),
            jax.ShapeDtypeStruct((sent, width), jnp.bfloat16),
        ],
        input_output_aliases={13 + len(riders) + i: i for i in range(len(filled))},
        scratch_shapes=[
            pltpu.VMEM((key_count, 2 * LANES), jnp.bfloat16),
            pltpu.VMEM((key_count, 2 * LANES), jnp.bfloat16),
            pltpu.VMEM((2 * GROUP * rows, 2 * LANES), jnp.bfloat16),
            pltpu.VMEM((rows, width), jnp.float32),
        ],
        compiler_params=params(58),
        cost_estimate=pl.CostEstimate(
            flops=16 * HEADS * rows * key_count * LANES,
            bytes_accessed=10_000_000,
            transcendentals=HEADS * rows * key_count,
        ),
        name="attend_rows",
    )(
        place,
        queries,
        k_cache,
        k_other,
        v_cache,
        v_other,
        own_span,
        other_span,
        own_span,
        other_span,
        w_out,
        tokens,
        gain,
        *riders,
        *extra,
    )


def plan_kernel(pieces, first, capacity, top, slot_ref, *refs):
    pick_ref, back_ref, share_ref = refs[pieces:]
    slots = slot_ref.shape[0]
    sources, _, tokens = pick_ref.shape
    deep = sources // pieces
    earlier = jnp.where(
        lax.broadcasted_iota(jnp.int32, (tokens, tokens), 0)
        < lax.broadcasted_iota(jnp.int32, (tokens, tokens), 1),
        1.0,
        0.0,
    ).astype(jnp.bfloat16)
    place = lax.broadcasted_iota(jnp.int32, (capacity, tokens), 0).astype(jnp.float32)
    hot_rows, share_lines = [], []
    for source in range(sources):
        packed = refs[source // deep][source % deep][first:].astype(jnp.float32)
        across = packed.shape[1] // tokens
        lines = [
            packed[i // across : i // across + 1, i % across * tokens : (i % across + 1) * tokens]
            for i in range(3 * top)
        ]
        ids = jnp.concatenate(lines[:top], axis=0)
        shares = jnp.concatenate(lines[top : 2 * top], axis=0)
        shares += jnp.concatenate(lines[2 * top :], axis=0)
        for slot in range(slots):
            match = ids == slot_ref[slot].astype(jnp.float32)
            hot_rows.append(jnp.max(jnp.where(match, 1.0, 0.0), axis=0, keepdims=True))
            share_lines.append(jnp.sum(jnp.where(match, shares, 0.0), axis=0, keepdims=True))
    hot = jnp.concatenate(hot_rows, axis=0)
    rank = jnp.dot(hot.astype(jnp.bfloat16), earlier, preferred_element_type=jnp.float32)
    rank = jnp.where(hot > 0.0, rank, -1.0)
    for source in range(sources):
        picks = []
        for slot in range(slots):
            line = source * slots + slot
            chosen = jnp.where(place == rank[line : line + 1], 1.0, 0.0)
            share_ref[slot, source * capacity : (source + 1) * capacity] = jnp.sum(
                chosen * share_lines[line], axis=1, keepdims=True
            )
            picks.append(chosen)
        picked = jnp.concatenate(picks, axis=0)
        pick_ref[source] = picked.astype(jnp.bfloat16)
        back_ref[source] = jnp.transpose(picked).astype(jnp.bfloat16)


def plan_routes(slot_ids, pieces, first, tokens, capacity, top):
    slots = slot_ids.shape[0]
    sources = sum(p.shape[0] for p in pieces)
    return pl.pallas_call(
        functools.partial(plan_kernel, len(pieces), first, capacity, top),
        in_specs=[pl.BlockSpec(memory_space=pltpu.SMEM)] + [vmem_spec()] * len(pieces),
        out_specs=[vmem_spec()] * 3,
        out_shape=[
            jax.ShapeDtypeStruct((sources, slots * capacity, tokens), jnp.bfloat16),
            jax.ShapeDtypeStruct((sources, tokens, slots * capacity), jnp.bfloat16),
            jax.ShapeDtypeStruct((slots, sources * capacity, 1), jnp.float32),
        ],
        compiler_params=params(24),
        cost_estimate=pl.CostEstimate(
            flops=1_000_000_000, bytes_accessed=2_000_000, transcendentals=0
        ),
        name="plan_routes",
    )(slot_ids, *pieces)


def expert_kernel(pieces, in_cuts, extra, *refs):
    halves = len(in_cuts)
    row_refs = refs[: pieces * halves]
    pick_ref, share_ref, up_ref, up_other_ref, down_ref, down_other_ref = refs[
        pieces * halves : pieces * halves + 6
    ]
    out_ref, held = refs[-2:]
    step = pl.program_id(0)
    slots = held.shape[0]
    own_slots = slots // 2
    sources = pick_ref.shape[0]
    deep = sources // pieces
    capacity = held.shape[1] // sources
    hidden = down_ref.shape[1]

    @pl.when(step == 0)
    def _():
        for source in range(sources):
            piece = source // deep
            rows = jnp.concatenate(
                [
                    row_refs[piece * halves + index][source % deep, :count]
                    for index, count in enumerate(in_cuts)
                ],
                axis=0,
            )
            rows = jnp.dot(
                pick_ref[source], rows, preferred_element_type=jnp.float32
            ).astype(jnp.bfloat16)
            for slot in range(slots):
                held[slot, source * capacity : (source + 1) * capacity] = rows[
                    slot * capacity : (slot + 1) * capacity
                ]

    def run(up, down):
        gate_up = jnp.dot(held[step], up[0], preferred_element_type=jnp.float32)
        active = (
            jax.nn.silu(gate_up[:, :hidden]) * gate_up[:, hidden:] * share_ref[step]
        ).astype(jnp.bfloat16)
        out_ref[step] = jnp.dot(active, down[0], preferred_element_type=jnp.float32).astype(
            jnp.bfloat16
        )

    @pl.when(step < own_slots)
    def _():
        run(up_ref, down_ref)

    @pl.when(step >= own_slots)
    def _():
        run(up_other_ref, down_other_ref)


def run_experts(rows, pick, share, ups, downs, in_cuts, after):
    pieces, halves = len(rows), len(rows[0])
    width = rows[0][0].shape[2]
    own_slots, _, double = ups[0].shape
    hidden = double // 2
    slots = 2 * own_slots
    places = share.shape[1]

    def own(j):
        return (jnp.minimum(j, own_slots - 1), 0, 0)

    def other(j):
        return (jnp.maximum(j - own_slots, 0), 0, 0)

    return pl.pallas_call(
        functools.partial(expert_kernel, pieces, tuple(in_cuts), len(after)),
        grid=(slots,),
        in_specs=[vmem_spec()] * (pieces * halves + 2)
        + [
            pl.BlockSpec((1, width, double), own),
            pl.BlockSpec((1, width, double), other),
            pl.BlockSpec((1, hidden, width), own),
            pl.BlockSpec((1, hidden, width), other),
        ]
        + [pl.BlockSpec(memory_space=pl.ANY)] * len(after),
        out_specs=vmem_spec(),
        out_shape=jax.ShapeDtypeStruct((slots, places, width), jnp.bfloat16),
        scratch_shapes=[pltpu.VMEM((slots, places, width), jnp.bfloat16)],
        compiler_params=params(44),
        cost_estimate=pl.CostEstimate(
            flops=10 * slots * places * width * hidden,
            bytes_accessed=26_000_000,
            transcendentals=slots * places * hidden,
        ),
        name="run_experts",
    )(*[r for piece in rows for r in piece], pick, share, ups[0], ups[1], downs[0], downs[1], *after)


def mix_kernel(pieces, out_cuts, held_ref, back_ref, *refs):
    count = len(out_cuts)
    out_refs = refs[-pieces * count :]
    slots, places, _ = held_ref.shape
    sources = back_ref.shape[0]
    deep = sources // pieces
    capacity = places // sources
    for source in range(sources):
        rows = jnp.concatenate(
            [
                held_ref[slot, source * capacity : (source + 1) * capacity]
                for slot in range(slots)
            ],
            axis=0,
        )
        mixed = jnp.dot(back_ref[source], rows, preferred_element_type=jnp.float32)
        start = 0
        for index, cut in enumerate(out_cuts):
            ref = out_refs[source // deep * count + index]
            ref[source % deep] = mixed[start : start + cut].astype(jnp.bfloat16)
            start += cut


def mix_rows(held, back, pieces, out_cuts, after):
    width = held.shape[2]
    deep = back.shape[0] // pieces
    flat = pl.pallas_call(
        functools.partial(mix_kernel, pieces, tuple(out_cuts)),
        in_specs=[vmem_spec()] * 2 + [pl.BlockSpec(memory_space=pl.ANY)] * len(after),
        out_specs=[vmem_spec()] * (pieces * len(out_cuts)),
        out_shape=[jax.ShapeDtypeStruct((deep, c, width), jnp.bfloat16) for c in out_cuts]
        * pieces,
        compiler_params=params(24),
        cost_estimate=pl.CostEstimate(
            flops=2_000_000_000, bytes_accessed=6_000_000, transcendentals=0
        ),
        name="mix_rows",
    )(held, back, *after)
    count = len(out_cuts)
    return [flat[i * count : (i + 1) * count] for i in range(pieces)]


def stack_kernel(count, *refs):
    out_ref = refs[-1]
    for index in range(count):
        out_ref[index] = refs[index][...]


def stack_rows(parts, after):
    return pl.pallas_call(
        functools.partial(stack_kernel, len(parts)),
        in_specs=[vmem_spec()] * len(parts) + [pl.BlockSpec(memory_space=pl.ANY)] * len(after),
        out_specs=vmem_spec(),
        out_shape=jax.ShapeDtypeStruct((len(parts), *parts[0].shape), parts[0].dtype),
        compiler_params=params(16),
        name="stack_rows",
    )(*parts, *after)


def chip_shape(chips):
    depth = 4 if chips % 4 == 0 else 1
    plane = chips // depth
    side = math.isqrt(plane)
    while plane % side:
        side -= 1
    return depth, plane // side, side


def make_shift(chips, cores):
    depth, tall, wide = chip_shape(chips)
    swap = tall == wide
    sizes = {"z": depth, "a": tall, "b": wide}

    def pairs(role, offset):
        out = []
        for z in range(depth):
            for y in range(tall):
                for x in range(wide):
                    for core in range(cores):
                        axis = role
                        if swap and core % 2 == 1:
                            axis = {"z": "z", "a": "b", "b": "a"}[role]
                        to_z, to_y, to_x = z, y, x
                        if axis == "z":
                            to_z = z ^ offset
                        elif axis == "a":
                            to_y = (y + offset) % tall
                        else:
                            to_x = (x + offset) % wide
                        source = ((z * tall + y) * wide + x) * cores + core
                        target = ((to_z * tall + to_y) * wide + to_x) * cores + core
                        out.append((source, target))
        return out

    def shift(value, role, offset):
        if role != "z":
            offset %= sizes[role]
        return lax.ppermute(value, BOTH, pairs(role, offset))

    return shift, sizes


def gather_line(value, shift, sizes):
    return [value] + [shift(value, "z", k) for k in range(1, sizes["z"])]


def scatter_line(line, shift, sizes):
    step = 1
    while step < sizes["z"]:
        kept = [k for k in range(0, sizes["z"], step) if not k & step]
        if len(kept) == 1:
            arrived = [shift(add_all(line[step]), "z", step)]
        else:
            arrived = shift(jnp.stack([add_all(line[k | step]) for k in kept]), "z", step)
        for place, k in enumerate(kept):
            line[k] = line[k] + [arrived[place]]
        step *= 2
    return line[0]


def gather_planes(line, shift, sizes, before):
    plane = [line] + [shift(line, "a", j) for j in range(1, sizes["a"])]
    forwarded = plane[1:]
    if before:
        forwarded, _ = lax.optimization_barrier((forwarded, before))
    return [plane] + [
        [shift(v, "b", k) for v in [line, *forwarded]] for k in range(1, sizes["b"])
    ]


def add_all(terms):
    total = terms[0].astype(jnp.float32)
    for term in terms[1:]:
        total = total + term.astype(jnp.float32)
    return total.astype(terms[0].dtype)


def leave_along_a(plane, shift):
    return [plane[0]] + [shift(v, "a", -j) for j, v in enumerate(plane) if j]


def scatter_plane(terms, shift, sizes):
    return scatter_line({i: [t[i] for t in terms] for i in range(sizes["z"])}, shift, sizes)


def scatter_chunks(own, others, shift, sizes):
    sums, before = [], []
    for index, (terms, sending) in enumerate(zip(own, others)):
        if before:
            sending, _ = lax.optimization_barrier((sending, before))
        planes = [leave_along_a(plane, shift) for plane in sending]
        if index == len(own) - 1:
            for k, part in enumerate(planes):
                terms = terms + [shift(add_all(part), "b", -k - 1)]
            found = scatter_plane(terms, shift, sizes)
        else:
            found = scatter_plane(terms, shift, sizes)
            before = [v for part in planes for v in part[1:]]
            for k, part in enumerate(planes):
                total = add_all(scatter_plane(part, shift, sizes))
                found = found + [shift(total, "b", -k - 1)]
        sums.append(add_all(found))
    total = jnp.zeros((sum(v.shape[0] for v in sums), sums[0].shape[1]), sums[0].dtype)
    first = 0
    for value in sums:
        total = lax.dynamic_update_slice(total, value, (first, 0))
        first += value.shape[0]
    return total


def rope_tables(positions):
    half = HEAD // 2
    frequency = rope_base ** (-jnp.arange(half, dtype=jnp.float32) / half)
    angles = positions.astype(jnp.float32)[:, None] * frequency[None, :]
    cosine, sine = jnp.cos(angles), jnp.sin(angles)
    return (
        jnp.concatenate([cosine] * 4, axis=1),
        jnp.concatenate([-sine, sine, -sine, sine], axis=1),
    )


def shards(
    tokens,
    attn_gain,
    w_qkv,
    w_out,
    k_cache,
    v_cache,
    cache_len,
    ffn_gain,
    routes,
    route_scores,
    replica_slot,
    expert_up,
    expert_down,
):
    row_count, top_count = routes.shape
    chips, cores = lax.axis_size("req"), lax.axis_size("seq")
    seq_index = lax.axis_index("seq")
    length = cache_len[0]
    slots_dev = expert_up.shape[0]
    slot_total = chips * cores * slots_dev
    capacity = 2 * ((row_count * top_count + slot_total - 1) // slot_total)
    shift, sizes = make_shift(chips, cores)

    def swap(value):
        return lax.ppermute(value, "seq", [(0, 1), (1, 0)])

    other_tokens = swap(tokens)
    k_other, v_other = swap(k_cache), swap(v_cache)
    experts = jnp.arange(replica_slot.shape[1], dtype=jnp.int32)
    slot_of = jnp.sum(
        jnp.where(routes[:, :, None] == experts, replica_slot[:, None, :], 0), axis=2
    )
    shares = route_scores / jnp.sum(route_scores, axis=1, keepdims=True)
    coarse = lax.reduce_precision(shares, 8, 7)
    table = jnp.concatenate([slot_of.astype(jnp.float32), coarse, shares - coarse], axis=1)
    table = table.astype(jnp.bfloat16).T.reshape(-1, tokens.shape[1])
    table = jnp.pad(table, ((0, -table.shape[0] % 8), (0, 0)))
    chip = lax.axis_index("req")
    chip_slots = jnp.arange(slots_dev, dtype=jnp.int32)
    slot_ids = jnp.concatenate(
        [
            (chip * cores + seq_index) * slots_dev + chip_slots,
            (chip * cores + 1 - seq_index) * slots_dev + chip_slots,
        ]
    ).astype(jnp.int32)

    row_index = jnp.arange(row_count, dtype=jnp.int32)
    cosine, sine = rope_tables(
        length
        + jnp.concatenate(
            [seq_index * row_count + row_index, (1 - seq_index) * row_count + row_index]
        )
    )
    queries, appended, other_span = project(
        tokens, other_tokens, attn_gain, cosine, sine, w_qkv, [k_other, v_other]
    )
    later_up, later_down, _ = lax.optimization_barrier((expert_up, expert_down, appended))
    up_other, down_other = swap(later_up), swap(later_down)
    half = row_count // 2
    filled, lines = [], []
    for index in range(2):
        attended, stream, expert_in = attend(
            cache_len,
            queries,
            (k_cache, k_other, v_cache, v_other),
            (appended, other_span),
            w_out,
            tokens,
            ffn_gain,
            index * half,
            half,
            [] if index else [table],
            filled,
            [up_other, down_other] if index else [],
        )
        filled = [attended, stream]
        sent = expert_in
        if index:
            sent, _ = lax.optimization_barrier((sent, lines[0][1:]))
        lines.append(gather_line(sent, shift, sizes))
    first, second = lines
    planes = gather_planes(stack_rows(first, [expert_in]), shift, sizes, second[1:])
    stacked = stack_rows(second, [plane[0] for plane in planes[1:]])
    halves = [planes, gather_planes(stacked, shift, sizes, [])]
    cuts = (5 * row_count // 8, row_count - 5 * row_count // 8)
    own, others, held = [], [], None
    for index in range(sizes["b"]):
        pick, back, share = plan_routes(
            slot_ids, halves[0][index], half, row_count, capacity, top_count
        )
        held = run_experts(
            [[planes[index][j] for planes in halves] for j in range(sizes["a"])],
            pick,
            share,
            (expert_up, up_other),
            (expert_down, down_other),
            (half, row_count - half),
            [held] if index else [],
        )
        mixed = mix_rows(held, back, sizes["a"], cuts, [v for line in own for v in line[1:]])
        chunks = [[piece[i] for piece in mixed] for i in range(len(cuts))]
        if index == 0:
            chunks, _ = lax.optimization_barrier((chunks, halves[1][1:]))
            own = [leave_along_a(plane, shift) for plane in chunks]
        else:
            others.append(chunks)
    others = [[planes[i] for planes in others] for i in range(len(cuts))]
    own, _ = lax.optimization_barrier((own, held))
    expert_mix = scatter_chunks(own, others, shift, sizes)
    return (attended, stream, expert_mix, appended)


def solution(mesh):
    return jax.shard_map(
        shards,
        mesh=mesh,
        in_specs=(
            P(("req", "seq"), None),
            P(),
            P(),
            P(),
            P("req", "seq", None),
            P("req", "seq", None),
            P("req"),
            P(),
            P(("req", "seq"), None),
            P(("req", "seq"), None),
            P(("req", "seq"), None),
            P(("req", "seq"), None, None),
            P(("req", "seq"), None, None),
        ),
        out_specs=(
            P(("req", "seq"), None),
            P(("req", "seq"), None),
            P(("req", "seq"), None),
            P(("req", "seq"), None),
        ),
        check_vma=False,
    )
```

```python
import functools
import math

import jax
import jax.numpy as jnp
from jax import lax
from jax.experimental import pallas as pl
from jax.experimental.pallas import tpu as pltpu
from jax.sharding import PartitionSpec as P

HEADS = 24
KV_HEADS = 8
HEAD = 64
GROUP = HEADS // KV_HEADS
LANES = 128
PAIR = 2 * GROUP * HEAD

epsilon = 1e-06
residual_scale = 0.22
score_scale = 0.015625
rope_base = 10000.0
neg_big = -1e30

BOTH = ("req", "seq")


def vmem_spec():
    return pl.BlockSpec(memory_space=pltpu.VMEM)


def params(mebibytes):
    return pltpu.CompilerParams(vmem_limit_bytes=mebibytes * 2**20)


def qkv_kernel(own_ref, other_ref, gain_ref, cos_ref, sin_ref, w_ref, *refs):
    q_ref, kv_ref, kvo_ref, normed = refs[-4:]
    step = pl.program_id(0)
    rows = own_ref.shape[0]
    width = w_ref.shape[1]

    @pl.when(step == 0)
    def _():
        for index, ref in enumerate((own_ref, other_ref)):
            wide = ref[...].astype(jnp.float32)
            mean_square = jnp.mean(wide * wide, axis=-1, keepdims=True)
            normed[index * rows : (index + 1) * rows] = (
                wide * lax.rsqrt(mean_square + epsilon) * gain_ref[...][None, :]
            ).astype(jnp.bfloat16)

    def rotated(x, row_slice):
        lane = lax.broadcasted_iota(jnp.int32, x.shape, 1)
        low = (lane & (HEAD - 1)) < HEAD // 2
        swapped = jnp.where(
            low, pltpu.roll(x, width - HEAD // 2, 1), pltpu.roll(x, HEAD // 2, 1)
        )
        times = width // LANES
        cosine = jnp.concatenate([cos_ref[row_slice]] * times, axis=1)
        sine = jnp.concatenate([sin_ref[row_slice]] * times, axis=1)
        return x * cosine + swapped * sine

    @pl.when(step < 3)
    def _():
        x = jnp.dot(normed[:rows], w_ref[...], preferred_element_type=jnp.float32)
        q_ref[...] = (rotated(x, slice(0, rows)) * score_scale).astype(jnp.bfloat16)

    @pl.when(step == 3)
    def _():
        x = jnp.dot(normed[...], w_ref[...], preferred_element_type=jnp.float32)
        x = rotated(x, slice(0, 2 * rows)).astype(jnp.bfloat16)
        kv_ref[...] = x[:rows]
        kvo_ref[...] = x[rows:]

    @pl.when(step == 4)
    def _():
        x = jnp.dot(normed[...], w_ref[...], preferred_element_type=jnp.float32)
        x = x.astype(jnp.bfloat16)
        kv_ref[...] = x[:rows]
        kvo_ref[...] = x[rows:]


def project(own, other, gain, cosine, sine, w_qkv, after):
    rows, width = own.shape
    tile = KV_HEADS * HEAD
    return pl.pallas_call(
        qkv_kernel,
        grid=(5,),
        in_specs=[vmem_spec()] * 5
        + [pl.BlockSpec((width, tile), lambda i: (0, i))]
        + [pl.BlockSpec(memory_space=pl.ANY)] * len(after),
        out_specs=[
            pl.BlockSpec((rows, tile), lambda i: (0, jnp.minimum(i, 2))),
            pl.BlockSpec((rows, tile), lambda i: (0, jnp.maximum(i - 3, 0))),
            pl.BlockSpec((rows, tile), lambda i: (0, jnp.maximum(i - 3, 0))),
        ],
        out_shape=[
            jax.ShapeDtypeStruct((rows, HEADS * HEAD), jnp.bfloat16),
            jax.ShapeDtypeStruct((rows, 2 * tile), jnp.bfloat16),
            jax.ShapeDtypeStruct((rows, 2 * tile), jnp.bfloat16),
        ],
        scratch_shapes=[pltpu.VMEM((2 * rows, width), jnp.bfloat16)],
        compiler_params=params(58),
        cost_estimate=pl.CostEstimate(
            flops=2 * rows * width * 3584, bytes_accessed=9_500_000, transcendentals=0
        ),
        name="project_rows",
    )(own, other, gain, cosine, sine, w_qkv, *after)


def attend_kernel(first_row, riders, extra, place_ref, q_ref, kc_ref, kco_ref, vc_ref, vco_ref, ks_ref, kso_ref, vs_ref, vso_ref, w_out_ref, tokens_ref, gain_ref, *refs):
    attended_ref, stream_ref, expert_in_ref, keys, values, wide_q, total = refs[riders + extra :]
    step = pl.program_id(0)
    rows = q_ref.shape[0]
    cached = kc_ref.shape[1]
    span = ks_ref.shape[0]
    seq_index = lax.axis_index("seq")
    length = place_ref[0]

    @pl.when(step == 0)
    def _():
        position = lax.broadcasted_iota(jnp.int32, (cached, LANES), 0)
        for index, half in enumerate((seq_index, 1 - seq_index)):
            visible = position + half * cached < length
            keys[index * cached : (index + 1) * cached, LANES:] = jnp.where(
                visible, 0.0, neg_big
            ).astype(jnp.bfloat16)
        key = lax.broadcasted_iota(jnp.int32, (span, LANES), 0)
        row = lax.broadcasted_iota(jnp.int32, (span, LANES), 1)
        keys[2 * cached : 2 * cached + span, LANES:] = jnp.where(key <= row, 0.0, neg_big).astype(
            jnp.bfloat16
        )
        keys[2 * cached + span :, LANES:] = jnp.where(
            jnp.zeros((span, LANES), jnp.int32) < seq_index, 0.0, neg_big
        ).astype(jnp.bfloat16)
        values[:, LANES:] = jnp.ones((values.shape[0], LANES), jnp.bfloat16)
        row = lax.broadcasted_iota(jnp.int32, (rows, LANES), 0) + first_row
        lane = lax.broadcasted_iota(jnp.int32, (rows, LANES), 1)
        chosen = jnp.where(row == lane, 1.0, 0.0).astype(jnp.bfloat16)
        for head in range(2 * GROUP):
            wide_q[head * rows : (head + 1) * rows, LANES:] = chosen

    for ref, parts in ((keys, (kc_ref, kco_ref)), (values, (vc_ref, vco_ref))):
        for index, part in enumerate(parts):
            ref[index * cached : (index + 1) * cached, :LANES] = part[0]
    for ref, parts in ((keys, (ks_ref, kso_ref)), (values, (vs_ref, vso_ref))):
        for index, part in enumerate(parts):
            start = 2 * cached + index * span
            ref[start : start + span, :LANES] = part[...]

    low = lax.broadcasted_iota(jnp.int32, (rows, LANES), 1) < HEAD
    tiles = [q_ref[:, i * LANES : (i + 1) * LANES].astype(jnp.float32) for i in range(3)]
    parts = [
        jnp.where(low, tiles[0], 0.0),
        jnp.where(low, pltpu.roll(tiles[0], HEAD, 1), 0.0),
        jnp.where(low, tiles[1], 0.0),
        jnp.where(low, 0.0, tiles[1]),
        jnp.where(low, 0.0, pltpu.roll(tiles[2], HEAD, 1)),
        jnp.where(low, 0.0, tiles[2]),
    ]
    for head, part in enumerate(parts):
        wide_q[head * rows : (head + 1) * rows, :LANES] = part.astype(jnp.bfloat16)

    heads = []
    batch = 2 * GROUP * rows
    for first in range(0, 2 * GROUP * rows, batch):
        scores = lax.dot_general(
            wide_q[first : first + batch],
            keys[...],
            (((1,), (1,)), ((), ())),
            preferred_element_type=jnp.float32,
        )
        best = jnp.max(scores, axis=-1, keepdims=True)
        weights = jnp.exp(scores - best).astype(jnp.bfloat16)
        sums = jnp.dot(weights, values[...], preferred_element_type=jnp.float32)
        mean = sums[:, :LANES] / sums[:, LANES:]
        heads += [mean[i : i + rows] for i in range(0, batch, rows)]
    merged = jnp.concatenate(
        [
            jnp.where(low, heads[0], pltpu.roll(heads[1], HEAD, 1)),
            jnp.where(low, heads[2], heads[3]),
            jnp.where(low, pltpu.roll(heads[4], HEAD, 1), heads[5]),
        ],
        axis=1,
    ).astype(jnp.bfloat16)
    attended_ref[...] = merged
    product = jnp.dot(merged, w_out_ref[...], preferred_element_type=jnp.float32)

    @pl.when(step == 0)
    def _():
        total[...] = product

    @pl.when(step > 0)
    def _():
        total[...] += product

    @pl.when(step == pl.num_programs(0) - 1)
    def _():
        stream = (tokens_ref[...].astype(jnp.float32) + residual_scale * total[...]).astype(
            jnp.bfloat16
        )
        stream_ref[...] = stream
        wide = stream.astype(jnp.float32)
        mean_square = jnp.mean(wide * wide, axis=-1, keepdims=True)
        sent = (wide * lax.rsqrt(mean_square + epsilon) * gain_ref[...][None, :]).astype(
            jnp.bfloat16
        )
        expert_in_ref[...] = jnp.concatenate([sent, *[r[...] for r in refs[:riders]]], axis=0)


def attend(place, queries, caches, spans, w_out, tokens, gain, first_row, rows, riders, filled, after):
    k_cache, k_other, v_cache, v_other = caches
    own_span, other_span = spans
    cached = k_cache.shape[1]
    span, width = tokens.shape
    pairs = KV_HEADS // 2
    part = first_row // rows
    key_count = 2 * cached + 2 * span
    cache_spec = pl.BlockSpec((1, cached, LANES), lambda j: (0, 0, j))
    key_spec = pl.BlockSpec((span, LANES), lambda j: (0, j))
    value_spec = pl.BlockSpec((span, LANES), lambda j: (0, pairs + j))
    extra = [*filled, *after]
    sent = rows + sum(r.shape[0] for r in riders)
    return pl.pallas_call(
        functools.partial(attend_kernel, first_row, len(riders), len(extra)),
        grid=(pairs,),
        in_specs=[
            pl.BlockSpec(memory_space=pltpu.SMEM),
            pl.BlockSpec((rows, PAIR), lambda j: (part, j)),
            cache_spec,
            cache_spec,
            cache_spec,
            cache_spec,
            key_spec,
            key_spec,
            value_spec,
            value_spec,
            pl.BlockSpec((PAIR, width), lambda j: (j, 0)),
            pl.BlockSpec((rows, width), lambda j: (part, 0)),
            vmem_spec(),
        ]
        + [vmem_spec()] * len(riders)
        + [pl.BlockSpec(memory_space=pl.ANY)] * len(extra),
        out_specs=[
            pl.BlockSpec((rows, PAIR), lambda j: (part, j)),
            pl.BlockSpec((rows, width), lambda j: (part, 0)),
            pl.BlockSpec((sent, width), lambda j: (0, 0)),
        ],
        out_shape=[
            jax.ShapeDtypeStruct((span, HEADS * HEAD), jnp.bfloat16),
            jax.ShapeDtypeStruct((span, width), jnp.bfloat16),
            jax.ShapeDtypeStruct((sent, width), jnp.bfloat16),
        ],
        input_output_aliases={13 + len(riders) + i: i for i in range(len(filled))},
        scratch_shapes=[
            pltpu.VMEM((key_count, 2 * LANES), jnp.bfloat16),
            pltpu.VMEM((key_count, 2 * LANES), jnp.bfloat16),
            pltpu.VMEM((2 * GROUP * rows, 2 * LANES), jnp.bfloat16),
            pltpu.VMEM((rows, width), jnp.float32),
        ],
        compiler_params=params(58),
        cost_estimate=pl.CostEstimate(
            flops=16 * HEADS * rows * key_count * LANES,
            bytes_accessed=10_000_000,
            transcendentals=HEADS * rows * key_count,
        ),
        name="attend_rows",
    )(
        place,
        queries,
        k_cache,
        k_other,
        v_cache,
        v_other,
        own_span,
        other_span,
        own_span,
        other_span,
        w_out,
        tokens,
        gain,
        *riders,
        *extra,
    )


def plan_kernel(pieces, first, capacity, top, slot_ref, *refs):
    pick_ref, back_ref, share_ref = refs[pieces:]
    slots = slot_ref.shape[0]
    sources, _, tokens = pick_ref.shape
    deep = sources // pieces
    earlier = jnp.where(
        lax.broadcasted_iota(jnp.int32, (tokens, tokens), 0)
        < lax.broadcasted_iota(jnp.int32, (tokens, tokens), 1),
        1.0,
        0.0,
    ).astype(jnp.bfloat16)
    place = lax.broadcasted_iota(jnp.int32, (capacity, tokens), 0).astype(jnp.float32)
    hot_rows, share_lines = [], []
    for source in range(sources):
        packed = refs[source // deep][source % deep][first:].astype(jnp.float32)
        across = packed.shape[1] // tokens
        lines = [
            packed[i // across : i // across + 1, i % across * tokens : (i % across + 1) * tokens]
            for i in range(3 * top)
        ]
        ids = jnp.concatenate(lines[:top], axis=0)
        shares = jnp.concatenate(lines[top : 2 * top], axis=0)
        shares += jnp.concatenate(lines[2 * top :], axis=0)
        for slot in range(slots):
            match = ids == slot_ref[slot].astype(jnp.float32)
            hot_rows.append(jnp.max(jnp.where(match, 1.0, 0.0), axis=0, keepdims=True))
            share_lines.append(jnp.sum(jnp.where(match, shares, 0.0), axis=0, keepdims=True))
    hot = jnp.concatenate(hot_rows, axis=0)
    rank = jnp.dot(hot.astype(jnp.bfloat16), earlier, preferred_element_type=jnp.float32)
    rank = jnp.where(hot > 0.0, rank, -1.0)
    for source in range(sources):
        picks = []
        for slot in range(slots):
            line = source * slots + slot
            chosen = jnp.where(place == rank[line : line + 1], 1.0, 0.0)
            share_ref[slot, source * capacity : (source + 1) * capacity] = jnp.sum(
                chosen * share_lines[line], axis=1, keepdims=True
            )
            picks.append(chosen)
        picked = jnp.concatenate(picks, axis=0)
        pick_ref[source] = picked.astype(jnp.bfloat16)
        back_ref[source] = jnp.transpose(picked).astype(jnp.bfloat16)


def plan_routes(slot_ids, pieces, first, tokens, capacity, top):
    slots = slot_ids.shape[0]
    sources = sum(p.shape[0] for p in pieces)
    return pl.pallas_call(
        functools.partial(plan_kernel, len(pieces), first, capacity, top),
        in_specs=[pl.BlockSpec(memory_space=pltpu.SMEM)] + [vmem_spec()] * len(pieces),
        out_specs=[vmem_spec()] * 3,
        out_shape=[
            jax.ShapeDtypeStruct((sources, slots * capacity, tokens), jnp.bfloat16),
            jax.ShapeDtypeStruct((sources, tokens, slots * capacity), jnp.bfloat16),
            jax.ShapeDtypeStruct((slots, sources * capacity, 1), jnp.float32),
        ],
        compiler_params=params(24),
        cost_estimate=pl.CostEstimate(
            flops=1_000_000_000, bytes_accessed=2_000_000, transcendentals=0
        ),
        name="plan_routes",
    )(slot_ids, *pieces)


def expert_kernel(pieces, in_cuts, extra, *refs):
    halves = len(in_cuts)
    row_refs = refs[: pieces * halves]
    pick_ref, share_ref, up_ref, up_other_ref, down_ref, down_other_ref = refs[
        pieces * halves : pieces * halves + 6
    ]
    out_ref, held = refs[-2:]
    step = pl.program_id(0)
    slots = held.shape[0]
    own_slots = slots // 2
    sources = pick_ref.shape[0]
    deep = sources // pieces
    capacity = held.shape[1] // sources
    hidden = down_ref.shape[1]

    @pl.when(step == 0)
    def _():
        for source in range(sources):
            piece = source // deep
            rows = jnp.concatenate(
                [
                    row_refs[piece * halves + index][source % deep, :count]
                    for index, count in enumerate(in_cuts)
                ],
                axis=0,
            )
            rows = jnp.dot(
                pick_ref[source], rows, preferred_element_type=jnp.float32
            ).astype(jnp.bfloat16)
            for slot in range(slots):
                held[slot, source * capacity : (source + 1) * capacity] = rows[
                    slot * capacity : (slot + 1) * capacity
                ]

    def run(up, down):
        gate_up = jnp.dot(held[step], up[0], preferred_element_type=jnp.float32)
        active = (
            jax.nn.silu(gate_up[:, :hidden]) * gate_up[:, hidden:] * share_ref[step]
        ).astype(jnp.bfloat16)
        out_ref[step] = jnp.dot(active, down[0], preferred_element_type=jnp.float32).astype(
            jnp.bfloat16
        )

    @pl.when(step < own_slots)
    def _():
        run(up_ref, down_ref)

    @pl.when(step >= own_slots)
    def _():
        run(up_other_ref, down_other_ref)


def run_experts(rows, pick, share, ups, downs, in_cuts, after):
    pieces, halves = len(rows), len(rows[0])
    width = rows[0][0].shape[2]
    own_slots, _, double = ups[0].shape
    hidden = double // 2
    slots = 2 * own_slots
    places = share.shape[1]

    def own(j):
        return (jnp.minimum(j, own_slots - 1), 0, 0)

    def other(j):
        return (jnp.maximum(j - own_slots, 0), 0, 0)

    return pl.pallas_call(
        functools.partial(expert_kernel, pieces, tuple(in_cuts), len(after)),
        grid=(slots,),
        in_specs=[vmem_spec()] * (pieces * halves + 2)
        + [
            pl.BlockSpec((1, width, double), own),
            pl.BlockSpec((1, width, double), other),
            pl.BlockSpec((1, hidden, width), own),
            pl.BlockSpec((1, hidden, width), other),
        ]
        + [pl.BlockSpec(memory_space=pl.ANY)] * len(after),
        out_specs=vmem_spec(),
        out_shape=jax.ShapeDtypeStruct((slots, places, width), jnp.bfloat16),
        scratch_shapes=[pltpu.VMEM((slots, places, width), jnp.bfloat16)],
        compiler_params=params(44),
        cost_estimate=pl.CostEstimate(
            flops=10 * slots * places * width * hidden,
            bytes_accessed=26_000_000,
            transcendentals=slots * places * hidden,
        ),
        name="run_experts",
    )(*[r for piece in rows for r in piece], pick, share, ups[0], ups[1], downs[0], downs[1], *after)


def mix_kernel(pieces, out_cuts, held_ref, back_ref, *refs):
    count = len(out_cuts)
    out_refs = refs[-pieces * count :]
    slots, places, _ = held_ref.shape
    sources = back_ref.shape[0]
    deep = sources // pieces
    capacity = places // sources
    for source in range(sources):
        rows = jnp.concatenate(
            [
                held_ref[slot, source * capacity : (source + 1) * capacity]
                for slot in range(slots)
            ],
            axis=0,
        )
        mixed = jnp.dot(back_ref[source], rows, preferred_element_type=jnp.float32)
        start = 0
        for index, cut in enumerate(out_cuts):
            ref = out_refs[source // deep * count + index]
            ref[source % deep] = mixed[start : start + cut].astype(jnp.bfloat16)
            start += cut


def mix_rows(held, back, pieces, out_cuts, after):
    width = held.shape[2]
    deep = back.shape[0] // pieces
    flat = pl.pallas_call(
        functools.partial(mix_kernel, pieces, tuple(out_cuts)),
        in_specs=[vmem_spec()] * 2 + [pl.BlockSpec(memory_space=pl.ANY)] * len(after),
        out_specs=[vmem_spec()] * (pieces * len(out_cuts)),
        out_shape=[jax.ShapeDtypeStruct((deep, c, width), jnp.bfloat16) for c in out_cuts]
        * pieces,
        compiler_params=params(24),
        cost_estimate=pl.CostEstimate(
            flops=2_000_000_000, bytes_accessed=6_000_000, transcendentals=0
        ),
        name="mix_rows",
    )(held, back, *after)
    count = len(out_cuts)
    return [flat[i * count : (i + 1) * count] for i in range(pieces)]


def stack_kernel(count, *refs):
    out_ref = refs[-1]
    for index in range(count):
        out_ref[index] = refs[index][...]


def stack_rows(parts, after):
    return pl.pallas_call(
        functools.partial(stack_kernel, len(parts)),
        in_specs=[vmem_spec()] * len(parts) + [pl.BlockSpec(memory_space=pl.ANY)] * len(after),
        out_specs=vmem_spec(),
        out_shape=jax.ShapeDtypeStruct((len(parts), *parts[0].shape), parts[0].dtype),
        compiler_params=params(16),
        name="stack_rows",
    )(*parts, *after)


def chip_shape(chips):
    depth = 4 if chips % 4 == 0 else 1
    plane = chips // depth
    side = math.isqrt(plane)
    while plane % side:
        side -= 1
    return depth, plane // side, side


def make_shift(chips, cores):
    depth, tall, wide = chip_shape(chips)
    swap = tall == wide
    sizes = {"z": depth, "a": tall, "b": wide}

    def pairs(role, offset):
        out = []
        for z in range(depth):
            for y in range(tall):
                for x in range(wide):
                    for core in range(cores):
                        axis = role
                        if swap and core % 2 == 1:
                            axis = {"z": "z", "a": "b", "b": "a"}[role]
                        to_z, to_y, to_x = z, y, x
                        if axis == "z":
                            to_z = z ^ offset
                        elif axis == "a":
                            to_y = (y + offset) % tall
                        else:
                            to_x = (x + offset) % wide
                        source = ((z * tall + y) * wide + x) * cores + core
                        target = ((to_z * tall + to_y) * wide + to_x) * cores + core
                        out.append((source, target))
        return out

    def shift(value, role, offset):
        if role != "z":
            offset %= sizes[role]
        return lax.ppermute(value, BOTH, pairs(role, offset))

    return shift, sizes


def gather_line(value, shift, sizes):
    return [value] + [shift(value, "z", k) for k in range(1, sizes["z"])]


def scatter_line(line, shift, sizes):
    step = 1
    while step < sizes["z"]:
        kept = [k for k in range(0, sizes["z"], step) if not k & step]
        if len(kept) == 1:
            arrived = [shift(add_all(line[step]), "z", step)]
        else:
            arrived = shift(jnp.stack([add_all(line[k | step]) for k in kept]), "z", step)
        for place, k in enumerate(kept):
            line[k] = line[k] + [arrived[place]]
        step *= 2
    return line[0]


def gather_planes(line, shift, sizes, before):
    plane = [line] + [shift(line, "a", j) for j in range(1, sizes["a"])]
    forwarded = plane[1:]
    if before:
        forwarded, _ = lax.optimization_barrier((forwarded, before))
    return [plane] + [
        [shift(v, "b", k) for v in [line, *forwarded]] for k in range(1, sizes["b"])
    ]


def add_all(terms):
    total = terms[0].astype(jnp.float32)
    for term in terms[1:]:
        total = total + term.astype(jnp.float32)
    return total.astype(terms[0].dtype)


def leave_along_a(plane, shift):
    return [plane[0]] + [shift(v, "a", -j) for j, v in enumerate(plane) if j]


def scatter_plane(terms, shift, sizes):
    return scatter_line({i: [t[i] for t in terms] for i in range(sizes["z"])}, shift, sizes)


def scatter_chunks(own, others, shift, sizes):
    sums, before, early = [], [], []
    for index, (terms, sending) in enumerate(zip(own, others)):
        if before:
            sending, _ = lax.optimization_barrier((sending, before))
        planes = [leave_along_a(plane, shift) for plane in sending]
        if index == len(own) - 1:
            for k, part in enumerate(planes):
                total = add_all(part)
                if early:
                    total, _ = lax.optimization_barrier((total, early))
                terms = terms + [shift(total, "b", -k - 1)]
            found = scatter_plane(terms, shift, sizes)
        else:
            found = scatter_plane(terms, shift, sizes)
            before = [v for part in planes for v in part[1:]]
            early = found[-1:]
            for k, part in enumerate(planes):
                total = add_all(scatter_plane(part, shift, sizes))
                found = found + [shift(total, "b", -k - 1)]
        sums.append(add_all(found))
    total = jnp.zeros((sum(v.shape[0] for v in sums), sums[0].shape[1]), sums[0].dtype)
    first = 0
    for value in sums:
        total = lax.dynamic_update_slice(total, value, (first, 0))
        first += value.shape[0]
    return total


def rope_tables(positions):
    half = HEAD // 2
    frequency = rope_base ** (-jnp.arange(half, dtype=jnp.float32) / half)
    angles = positions.astype(jnp.float32)[:, None] * frequency[None, :]
    cosine, sine = jnp.cos(angles), jnp.sin(angles)
    return (
        jnp.concatenate([cosine] * 4, axis=1),
        jnp.concatenate([-sine, sine, -sine, sine], axis=1),
    )


def shards(
    tokens,
    attn_gain,
    w_qkv,
    w_out,
    k_cache,
    v_cache,
    cache_len,
    ffn_gain,
    routes,
    route_scores,
    replica_slot,
    expert_up,
    expert_down,
):
    row_count, top_count = routes.shape
    chips, cores = lax.axis_size("req"), lax.axis_size("seq")
    seq_index = lax.axis_index("seq")
    length = cache_len[0]
    slots_dev = expert_up.shape[0]
    slot_total = chips * cores * slots_dev
    capacity = 2 * ((row_count * top_count + slot_total - 1) // slot_total)
    shift, sizes = make_shift(chips, cores)

    def swap(value):
        return lax.ppermute(value, "seq", [(0, 1), (1, 0)])

    other_tokens = swap(tokens)
    k_other, v_other = swap(k_cache), swap(v_cache)
    experts = jnp.arange(replica_slot.shape[1], dtype=jnp.int32)
    slot_of = jnp.sum(
        jnp.where(routes[:, :, None] == experts, replica_slot[:, None, :], 0), axis=2
    )
    shares = route_scores / jnp.sum(route_scores, axis=1, keepdims=True)
    coarse = lax.reduce_precision(shares, 8, 7)
    table = jnp.concatenate([slot_of.astype(jnp.float32), coarse, shares - coarse], axis=1)
    table = table.astype(jnp.bfloat16).T.reshape(-1, tokens.shape[1])
    table = jnp.pad(table, ((0, -table.shape[0] % 8), (0, 0)))
    chip = lax.axis_index("req")
    chip_slots = jnp.arange(slots_dev, dtype=jnp.int32)
    slot_ids = jnp.concatenate(
        [
            (chip * cores + seq_index) * slots_dev + chip_slots,
            (chip * cores + 1 - seq_index) * slots_dev + chip_slots,
        ]
    ).astype(jnp.int32)

    row_index = jnp.arange(row_count, dtype=jnp.int32)
    cosine, sine = rope_tables(
        length
        + jnp.concatenate(
            [seq_index * row_count + row_index, (1 - seq_index) * row_count + row_index]
        )
    )
    queries, appended, other_span = project(
        tokens, other_tokens, attn_gain, cosine, sine, w_qkv, [k_other, v_other]
    )
    later_up, later_down, _ = lax.optimization_barrier((expert_up, expert_down, appended))
    up_other, down_other = swap(later_up), swap(later_down)
    half = row_count // 2
    filled, lines = [], []
    for index in range(2):
        attended, stream, expert_in = attend(
            cache_len,
            queries,
            (k_cache, k_other, v_cache, v_other),
            (appended, other_span),
            w_out,
            tokens,
            ffn_gain,
            index * half,
            half,
            [] if index else [table],
            filled,
            [up_other, down_other] if index else [],
        )
        filled = [attended, stream]
        sent = expert_in
        if index:
            sent, _ = lax.optimization_barrier((sent, lines[0][1:]))
        lines.append(gather_line(sent, shift, sizes))
    first, second = lines
    planes = gather_planes(stack_rows(first, [expert_in]), shift, sizes, second[1:])
    stacked = stack_rows(second, [plane[0] for plane in planes[1:]])
    halves = [planes, gather_planes(stacked, shift, sizes, [])]
    cuts = (5 * row_count // 8, row_count - 5 * row_count // 8)
    own, others, held = [], [], None
    for index in range(sizes["b"]):
        pick, back, share = plan_routes(
            slot_ids, halves[0][index], half, row_count, capacity, top_count
        )
        held = run_experts(
            [[planes[index][j] for planes in halves] for j in range(sizes["a"])],
            pick,
            share,
            (expert_up, up_other),
            (expert_down, down_other),
            (half, row_count - half),
            [held] if index else [],
        )
        mixed = mix_rows(held, back, sizes["a"], cuts, [v for line in own for v in line[1:]])
        chunks = [[piece[i] for piece in mixed] for i in range(len(cuts))]
        if index == 0:
            chunks, _ = lax.optimization_barrier((chunks, halves[1][1:]))
            own = [leave_along_a(plane, shift) for plane in chunks]
        else:
            others.append(chunks)
    others = [[planes[i] for planes in others] for i in range(len(cuts))]
    own, _ = lax.optimization_barrier((own, held))
    expert_mix = scatter_chunks(own, others, shift, sizes)
    return (attended, stream, expert_mix, appended)


def solution(mesh):
    return jax.shard_map(
        shards,
        mesh=mesh,
        in_specs=(
            P(("req", "seq"), None),
            P(),
            P(),
            P(),
            P("req", "seq", None),
            P("req", "seq", None),
            P("req"),
            P(),
            P(("req", "seq"), None),
            P(("req", "seq"), None),
            P(("req", "seq"), None),
            P(("req", "seq"), None, None),
            P(("req", "seq"), None, None),
        ),
        out_specs=(
            P(("req", "seq"), None),
            P(("req", "seq"), None),
            P(("req", "seq"), None),
            P(("req", "seq"), None),
        ),
        check_vma=False,
    )
```

```python
import functools
import math

import jax
import jax.numpy as jnp
from jax import lax
from jax.experimental import pallas as pl
from jax.experimental.pallas import tpu as pltpu
from jax.sharding import PartitionSpec as P

HEADS = 24
KV_HEADS = 8
HEAD = 64
GROUP = HEADS // KV_HEADS
LANES = 128
PAIR = 2 * GROUP * HEAD

epsilon = 1e-06
residual_scale = 0.22
score_scale = 0.015625
rope_base = 10000.0
neg_big = -1e30

BOTH = ("req", "seq")


def vmem_spec():
    return pl.BlockSpec(memory_space=pltpu.VMEM)


def params(mebibytes):
    return pltpu.CompilerParams(vmem_limit_bytes=mebibytes * 2**20)


def qkv_kernel(own_ref, other_ref, gain_ref, cos_ref, sin_ref, w_ref, *refs):
    q_ref, kv_ref, kvo_ref, normed = refs[-4:]
    step = pl.program_id(0)
    rows = own_ref.shape[0]
    width = w_ref.shape[1]

    @pl.when(step == 0)
    def _():
        for index, ref in enumerate((own_ref, other_ref)):
            wide = ref[...].astype(jnp.float32)
            mean_square = jnp.mean(wide * wide, axis=-1, keepdims=True)
            normed[index * rows : (index + 1) * rows] = (
                wide * lax.rsqrt(mean_square + epsilon) * gain_ref[...][None, :]
            ).astype(jnp.bfloat16)

    def rotated(x, row_slice):
        lane = lax.broadcasted_iota(jnp.int32, x.shape, 1)
        low = (lane & (HEAD - 1)) < HEAD // 2
        swapped = jnp.where(
            low, pltpu.roll(x, width - HEAD // 2, 1), pltpu.roll(x, HEAD // 2, 1)
        )
        times = width // LANES
        cosine = jnp.concatenate([cos_ref[row_slice]] * times, axis=1)
        sine = jnp.concatenate([sin_ref[row_slice]] * times, axis=1)
        return x * cosine + swapped * sine

    @pl.when(step < 3)
    def _():
        x = jnp.dot(normed[:rows], w_ref[...], preferred_element_type=jnp.float32)
        q_ref[...] = (rotated(x, slice(0, rows)) * score_scale).astype(jnp.bfloat16)

    @pl.when(step == 3)
    def _():
        x = jnp.dot(normed[...], w_ref[...], preferred_element_type=jnp.float32)
        x = rotated(x, slice(0, 2 * rows)).astype(jnp.bfloat16)
        kv_ref[...] = x[:rows]
        kvo_ref[...] = x[rows:]

    @pl.when(step == 4)
    def _():
        x = jnp.dot(normed[...], w_ref[...], preferred_element_type=jnp.float32)
        x = x.astype(jnp.bfloat16)
        kv_ref[...] = x[:rows]
        kvo_ref[...] = x[rows:]


def project(own, other, gain, cosine, sine, w_qkv, after):
    rows, width = own.shape
    tile = KV_HEADS * HEAD
    return pl.pallas_call(
        qkv_kernel,
        grid=(5,),
        in_specs=[vmem_spec()] * 5
        + [pl.BlockSpec((width, tile), lambda i: (0, i))]
        + [pl.BlockSpec(memory_space=pl.ANY)] * len(after),
        out_specs=[
            pl.BlockSpec((rows, tile), lambda i: (0, jnp.minimum(i, 2))),
            pl.BlockSpec((rows, tile), lambda i: (0, jnp.maximum(i - 3, 0))),
            pl.BlockSpec((rows, tile), lambda i: (0, jnp.maximum(i - 3, 0))),
        ],
        out_shape=[
            jax.ShapeDtypeStruct((rows, HEADS * HEAD), jnp.bfloat16),
            jax.ShapeDtypeStruct((rows, 2 * tile), jnp.bfloat16),
            jax.ShapeDtypeStruct((rows, 2 * tile), jnp.bfloat16),
        ],
        scratch_shapes=[pltpu.VMEM((2 * rows, width), jnp.bfloat16)],
        compiler_params=params(58),
        cost_estimate=pl.CostEstimate(
            flops=2 * rows * width * 3584, bytes_accessed=9_500_000, transcendentals=0
        ),
        name="project_rows",
    )(own, other, gain, cosine, sine, w_qkv, *after)


def attend_kernel(first_row, riders, extra, place_ref, q_ref, kc_ref, kco_ref, vc_ref, vco_ref, ks_ref, kso_ref, vs_ref, vso_ref, w_out_ref, tokens_ref, gain_ref, *refs):
    attended_ref, stream_ref, expert_in_ref, keys, values, wide_q, total = refs[riders + extra :]
    step = pl.program_id(0)
    rows = q_ref.shape[0]
    cached = kc_ref.shape[1]
    span = ks_ref.shape[0]
    seq_index = lax.axis_index("seq")
    length = place_ref[0]

    @pl.when(step == 0)
    def _():
        position = lax.broadcasted_iota(jnp.int32, (cached, LANES), 0)
        for index, half in enumerate((seq_index, 1 - seq_index)):
            visible = position + half * cached < length
            keys[index * cached : (index + 1) * cached, LANES:] = jnp.where(
                visible, 0.0, neg_big
            ).astype(jnp.bfloat16)
        key = lax.broadcasted_iota(jnp.int32, (span, LANES), 0)
        row = lax.broadcasted_iota(jnp.int32, (span, LANES), 1)
        keys[2 * cached : 2 * cached + span, LANES:] = jnp.where(key <= row, 0.0, neg_big).astype(
            jnp.bfloat16
        )
        keys[2 * cached + span :, LANES:] = jnp.where(
            jnp.zeros((span, LANES), jnp.int32) < seq_index, 0.0, neg_big
        ).astype(jnp.bfloat16)
        values[:, LANES:] = jnp.ones((values.shape[0], LANES), jnp.bfloat16)
        row = lax.broadcasted_iota(jnp.int32, (rows, LANES), 0) + first_row
        lane = lax.broadcasted_iota(jnp.int32, (rows, LANES), 1)
        chosen = jnp.where(row == lane, 1.0, 0.0).astype(jnp.bfloat16)
        for head in range(2 * GROUP):
            wide_q[head * rows : (head + 1) * rows, LANES:] = chosen

    for ref, parts in ((keys, (kc_ref, kco_ref)), (values, (vc_ref, vco_ref))):
        for index, part in enumerate(parts):
            ref[index * cached : (index + 1) * cached, :LANES] = part[0]
    for ref, parts in ((keys, (ks_ref, kso_ref)), (values, (vs_ref, vso_ref))):
        for index, part in enumerate(parts):
            start = 2 * cached + index * span
            ref[start : start + span, :LANES] = part[...]

    low = lax.broadcasted_iota(jnp.int32, (rows, LANES), 1) < HEAD
    tiles = [q_ref[:, i * LANES : (i + 1) * LANES].astype(jnp.float32) for i in range(3)]
    parts = [
        jnp.where(low, tiles[0], 0.0),
        jnp.where(low, pltpu.roll(tiles[0], HEAD, 1), 0.0),
        jnp.where(low, tiles[1], 0.0),
        jnp.where(low, 0.0, tiles[1]),
        jnp.where(low, 0.0, pltpu.roll(tiles[2], HEAD, 1)),
        jnp.where(low, 0.0, tiles[2]),
    ]
    for head, part in enumerate(parts):
        wide_q[head * rows : (head + 1) * rows, :LANES] = part.astype(jnp.bfloat16)

    heads = []
    batch = 2 * GROUP * rows
    for first in range(0, 2 * GROUP * rows, batch):
        scores = lax.dot_general(
            wide_q[first : first + batch],
            keys[...],
            (((1,), (1,)), ((), ())),
            preferred_element_type=jnp.float32,
        )
        best = jnp.max(scores, axis=-1, keepdims=True)
        weights = jnp.exp(scores - best).astype(jnp.bfloat16)
        sums = jnp.dot(weights, values[...], preferred_element_type=jnp.float32)
        mean = sums[:, :LANES] / sums[:, LANES:]
        heads += [mean[i : i + rows] for i in range(0, batch, rows)]
    merged = jnp.concatenate(
        [
            jnp.where(low, heads[0], pltpu.roll(heads[1], HEAD, 1)),
            jnp.where(low, heads[2], heads[3]),
            jnp.where(low, pltpu.roll(heads[4], HEAD, 1), heads[5]),
        ],
        axis=1,
    ).astype(jnp.bfloat16)
    attended_ref[...] = merged
    product = jnp.dot(merged, w_out_ref[...], preferred_element_type=jnp.float32)

    @pl.when(step == 0)
    def _():
        total[...] = product

    @pl.when(step > 0)
    def _():
        total[...] += product

    @pl.when(step == pl.num_programs(0) - 1)
    def _():
        stream = (tokens_ref[...].astype(jnp.float32) + residual_scale * total[...]).astype(
            jnp.bfloat16
        )
        stream_ref[...] = stream
        wide = stream.astype(jnp.float32)
        mean_square = jnp.mean(wide * wide, axis=-1, keepdims=True)
        sent = (wide * lax.rsqrt(mean_square + epsilon) * gain_ref[...][None, :]).astype(
            jnp.bfloat16
        )
        expert_in_ref[...] = jnp.concatenate([sent, *[r[...] for r in refs[:riders]]], axis=0)


def attend(place, queries, caches, spans, w_out, tokens, gain, first_row, rows, riders, filled, after):
    k_cache, k_other, v_cache, v_other = caches
    own_span, other_span = spans
    cached = k_cache.shape[1]
    span, width = tokens.shape
    pairs = KV_HEADS // 2
    part = first_row // rows
    key_count = 2 * cached + 2 * span
    cache_spec = pl.BlockSpec((1, cached, LANES), lambda j: (0, 0, j))
    key_spec = pl.BlockSpec((span, LANES), lambda j: (0, j))
    value_spec = pl.BlockSpec((span, LANES), lambda j: (0, pairs + j))
    extra = [*filled, *after]
    sent = rows + sum(r.shape[0] for r in riders)
    return pl.pallas_call(
        functools.partial(attend_kernel, first_row, len(riders), len(extra)),
        grid=(pairs,),
        in_specs=[
            pl.BlockSpec(memory_space=pltpu.SMEM),
            pl.BlockSpec((rows, PAIR), lambda j: (part, j)),
            cache_spec,
            cache_spec,
            cache_spec,
            cache_spec,
            key_spec,
            key_spec,
            value_spec,
            value_spec,
            pl.BlockSpec((PAIR, width), lambda j: (j, 0)),
            pl.BlockSpec((rows, width), lambda j: (part, 0)),
            vmem_spec(),
        ]
        + [vmem_spec()] * len(riders)
        + [pl.BlockSpec(memory_space=pl.ANY)] * len(extra),
        out_specs=[
            pl.BlockSpec((rows, PAIR), lambda j: (part, j)),
            pl.BlockSpec((rows, width), lambda j: (part, 0)),
            pl.BlockSpec((sent, width), lambda j: (0, 0)),
        ],
        out_shape=[
            jax.ShapeDtypeStruct((span, HEADS * HEAD), jnp.bfloat16),
            jax.ShapeDtypeStruct((span, width), jnp.bfloat16),
            jax.ShapeDtypeStruct((sent, width), jnp.bfloat16),
        ],
        input_output_aliases={13 + len(riders) + i: i for i in range(len(filled))},
        scratch_shapes=[
            pltpu.VMEM((key_count, 2 * LANES), jnp.bfloat16),
            pltpu.VMEM((key_count, 2 * LANES), jnp.bfloat16),
            pltpu.VMEM((2 * GROUP * rows, 2 * LANES), jnp.bfloat16),
            pltpu.VMEM((rows, width), jnp.float32),
        ],
        compiler_params=params(58),
        cost_estimate=pl.CostEstimate(
            flops=16 * HEADS * rows * key_count * LANES,
            bytes_accessed=10_000_000,
            transcendentals=HEADS * rows * key_count,
        ),
        name="attend_rows",
    )(
        place,
        queries,
        k_cache,
        k_other,
        v_cache,
        v_other,
        own_span,
        other_span,
        own_span,
        other_span,
        w_out,
        tokens,
        gain,
        *riders,
        *extra,
    )


def plan_kernel(pieces, first, capacity, top, slot_ref, *refs):
    pick_ref, back_ref, share_ref = refs[pieces:]
    slots = slot_ref.shape[0]
    sources, _, tokens = pick_ref.shape
    deep = sources // pieces
    earlier = jnp.where(
        lax.broadcasted_iota(jnp.int32, (tokens, tokens), 0)
        < lax.broadcasted_iota(jnp.int32, (tokens, tokens), 1),
        1.0,
        0.0,
    ).astype(jnp.bfloat16)
    place = lax.broadcasted_iota(jnp.int32, (capacity, tokens), 0).astype(jnp.float32)
    hot_rows, share_lines = [], []
    for source in range(sources):
        packed = refs[source // deep][source % deep][first:].astype(jnp.float32)
        across = packed.shape[1] // tokens
        lines = [
            packed[i // across : i // across + 1, i % across * tokens : (i % across + 1) * tokens]
            for i in range(3 * top)
        ]
        ids = jnp.concatenate(lines[:top], axis=0)
        shares = jnp.concatenate(lines[top : 2 * top], axis=0)
        shares += jnp.concatenate(lines[2 * top :], axis=0)
        for slot in range(slots):
            match = ids == slot_ref[slot].astype(jnp.float32)
            hot_rows.append(jnp.max(jnp.where(match, 1.0, 0.0), axis=0, keepdims=True))
            share_lines.append(jnp.sum(jnp.where(match, shares, 0.0), axis=0, keepdims=True))
    hot = jnp.concatenate(hot_rows, axis=0)
    rank = jnp.dot(hot.astype(jnp.bfloat16), earlier, preferred_element_type=jnp.float32)
    rank = jnp.where(hot > 0.0, rank, -1.0)
    for source in range(sources):
        picks = []
        for slot in range(slots):
            line = source * slots + slot
            chosen = jnp.where(place == rank[line : line + 1], 1.0, 0.0)
            share_ref[slot, source * capacity : (source + 1) * capacity] = jnp.sum(
                chosen * share_lines[line], axis=1, keepdims=True
            )
            picks.append(chosen)
        picked = jnp.concatenate(picks, axis=0)
        pick_ref[source] = picked.astype(jnp.bfloat16)
        back_ref[source] = jnp.transpose(picked).astype(jnp.bfloat16)


def plan_routes(slot_ids, pieces, first, tokens, capacity, top):
    slots = slot_ids.shape[0]
    sources = sum(p.shape[0] for p in pieces)
    return pl.pallas_call(
        functools.partial(plan_kernel, len(pieces), first, capacity, top),
        in_specs=[pl.BlockSpec(memory_space=pltpu.SMEM)] + [vmem_spec()] * len(pieces),
        out_specs=[vmem_spec()] * 3,
        out_shape=[
            jax.ShapeDtypeStruct((sources, slots * capacity, tokens), jnp.bfloat16),
            jax.ShapeDtypeStruct((sources, tokens, slots * capacity), jnp.bfloat16),
            jax.ShapeDtypeStruct((slots, sources * capacity, 1), jnp.float32),
        ],
        compiler_params=params(24),
        cost_estimate=pl.CostEstimate(
            flops=1_000_000_000, bytes_accessed=2_000_000, transcendentals=0
        ),
        name="plan_routes",
    )(slot_ids, *pieces)


def expert_kernel(pieces, in_cuts, extra, *refs):
    halves = len(in_cuts)
    row_refs = refs[: pieces * halves]
    pick_ref, share_ref, up_ref, up_other_ref, down_ref, down_other_ref = refs[
        pieces * halves : pieces * halves + 6
    ]
    out_ref, held = refs[-2:]
    step = pl.program_id(0)
    slots = held.shape[0]
    own_slots = slots // 2
    sources = pick_ref.shape[0]
    deep = sources // pieces
    capacity = held.shape[1] // sources
    hidden = down_ref.shape[1]

    @pl.when(step == 0)
    def _():
        for source in range(sources):
            piece = source // deep
            rows = jnp.concatenate(
                [
                    row_refs[piece * halves + index][source % deep, :count]
                    for index, count in enumerate(in_cuts)
                ],
                axis=0,
            )
            rows = jnp.dot(
                pick_ref[source], rows, preferred_element_type=jnp.float32
            ).astype(jnp.bfloat16)
            for slot in range(slots):
                held[slot, source * capacity : (source + 1) * capacity] = rows[
                    slot * capacity : (slot + 1) * capacity
                ]

    def run(up, down):
        gate_up = jnp.dot(held[step], up[0], preferred_element_type=jnp.float32)
        active = (
            jax.nn.silu(gate_up[:, :hidden]) * gate_up[:, hidden:] * share_ref[step]
        ).astype(jnp.bfloat16)
        out_ref[step] = jnp.dot(active, down[0], preferred_element_type=jnp.float32).astype(
            jnp.bfloat16
        )

    @pl.when(step < own_slots)
    def _():
        run(up_ref, down_ref)

    @pl.when(step >= own_slots)
    def _():
        run(up_other_ref, down_other_ref)


def run_experts(rows, pick, share, ups, downs, in_cuts, after):
    pieces, halves = len(rows), len(rows[0])
    width = rows[0][0].shape[2]
    own_slots, _, double = ups[0].shape
    hidden = double // 2
    slots = 2 * own_slots
    places = share.shape[1]

    def own(j):
        return (jnp.minimum(j, own_slots - 1), 0, 0)

    def other(j):
        return (jnp.maximum(j - own_slots, 0), 0, 0)

    return pl.pallas_call(
        functools.partial(expert_kernel, pieces, tuple(in_cuts), len(after)),
        grid=(slots,),
        in_specs=[vmem_spec()] * (pieces * halves + 2)
        + [
            pl.BlockSpec((1, width, double), own),
            pl.BlockSpec((1, width, double), other),
            pl.BlockSpec((1, hidden, width), own),
            pl.BlockSpec((1, hidden, width), other),
        ]
        + [pl.BlockSpec(memory_space=pl.ANY)] * len(after),
        out_specs=vmem_spec(),
        out_shape=jax.ShapeDtypeStruct((slots, places, width), jnp.bfloat16),
        scratch_shapes=[pltpu.VMEM((slots, places, width), jnp.bfloat16)],
        compiler_params=params(44),
        cost_estimate=pl.CostEstimate(
            flops=10 * slots * places * width * hidden,
            bytes_accessed=26_000_000,
            transcendentals=slots * places * hidden,
        ),
        name="run_experts",
    )(*[r for piece in rows for r in piece], pick, share, ups[0], ups[1], downs[0], downs[1], *after)


def mix_kernel(pieces, out_cuts, held_ref, back_ref, *refs):
    count = len(out_cuts)
    out_refs = refs[-pieces * count :]
    slots, places, _ = held_ref.shape
    sources = back_ref.shape[0]
    deep = sources // pieces
    capacity = places // sources
    for source in range(sources):
        rows = jnp.concatenate(
            [
                held_ref[slot, source * capacity : (source + 1) * capacity]
                for slot in range(slots)
            ],
            axis=0,
        )
        mixed = jnp.dot(back_ref[source], rows, preferred_element_type=jnp.float32)
        start = 0
        for index, cut in enumerate(out_cuts):
            ref = out_refs[source // deep * count + index]
            ref[source % deep] = mixed[start : start + cut].astype(jnp.bfloat16)
            start += cut


def mix_rows(held, back, pieces, out_cuts, after):
    width = held.shape[2]
    deep = back.shape[0] // pieces
    flat = pl.pallas_call(
        functools.partial(mix_kernel, pieces, tuple(out_cuts)),
        in_specs=[vmem_spec()] * 2 + [pl.BlockSpec(memory_space=pl.ANY)] * len(after),
        out_specs=[vmem_spec()] * (pieces * len(out_cuts)),
        out_shape=[jax.ShapeDtypeStruct((deep, c, width), jnp.bfloat16) for c in out_cuts]
        * pieces,
        compiler_params=params(24),
        cost_estimate=pl.CostEstimate(
            flops=2_000_000_000, bytes_accessed=6_000_000, transcendentals=0
        ),
        name="mix_rows",
    )(held, back, *after)
    count = len(out_cuts)
    return [flat[i * count : (i + 1) * count] for i in range(pieces)]


def stack_kernel(count, *refs):
    out_ref = refs[-1]
    for index in range(count):
        out_ref[index] = refs[index][...]


def stack_rows(parts, after):
    return pl.pallas_call(
        functools.partial(stack_kernel, len(parts)),
        in_specs=[vmem_spec()] * len(parts) + [pl.BlockSpec(memory_space=pl.ANY)] * len(after),
        out_specs=vmem_spec(),
        out_shape=jax.ShapeDtypeStruct((len(parts), *parts[0].shape), parts[0].dtype),
        compiler_params=params(16),
        name="stack_rows",
    )(*parts, *after)


def chip_shape(chips):
    depth = 4 if chips % 4 == 0 else 1
    plane = chips // depth
    side = math.isqrt(plane)
    while plane % side:
        side -= 1
    return depth, plane // side, side


def make_shift(chips, cores):
    depth, tall, wide = chip_shape(chips)
    swap = tall == wide
    sizes = {"z": depth, "a": tall, "b": wide}

    def pairs(role, offset):
        out = []
        for z in range(depth):
            for y in range(tall):
                for x in range(wide):
                    for core in range(cores):
                        axis = role
                        if swap and core % 2 == 1:
                            axis = {"z": "z", "a": "b", "b": "a"}[role]
                        to_z, to_y, to_x = z, y, x
                        if axis == "z":
                            to_z = z ^ offset
                        elif axis == "a":
                            to_y = (y + offset) % tall
                        else:
                            to_x = (x + offset) % wide
                        source = ((z * tall + y) * wide + x) * cores + core
                        target = ((to_z * tall + to_y) * wide + to_x) * cores + core
                        out.append((source, target))
        return out

    def shift(value, role, offset):
        if role != "z":
            offset %= sizes[role]
        return lax.ppermute(value, BOTH, pairs(role, offset))

    return shift, sizes


def gather_line(value, shift, sizes):
    return [value] + [shift(value, "z", k) for k in range(1, sizes["z"])]


def scatter_line(line, shift, sizes):
    step = 1
    while step < sizes["z"]:
        kept = [k for k in range(0, sizes["z"], step) if not k & step]
        if len(kept) == 1:
            arrived = [shift(add_all(line[step]), "z", step)]
        else:
            arrived = shift(jnp.stack([add_all(line[k | step]) for k in kept]), "z", step)
        for place, k in enumerate(kept):
            line[k] = line[k] + [arrived[place]]
        step *= 2
    return line[0]


def gather_planes(line, shift, sizes, before):
    plane = [line] + [shift(line, "a", j) for j in range(1, sizes["a"])]
    forwarded = plane[1:]
    if before:
        forwarded, _ = lax.optimization_barrier((forwarded, before))
    return [plane] + [
        [shift(v, "b", k) for v in [line, *forwarded]] for k in range(1, sizes["b"])
    ]


def add_all(terms):
    total = terms[0].astype(jnp.float32)
    for term in terms[1:]:
        total = total + term.astype(jnp.float32)
    return total.astype(terms[0].dtype)


def leave_along_a(plane, shift):
    return [plane[0]] + [shift(v, "a", -j) for j, v in enumerate(plane) if j]


def scatter_plane(terms, shift, sizes):
    return scatter_line({i: [t[i] for t in terms] for i in range(sizes["z"])}, shift, sizes)


def scatter_chunks(own, others, shift, sizes):
    sums, before, early = [], [], []
    for index, (terms, sending) in enumerate(zip(own, others)):
        if before:
            sending, _ = lax.optimization_barrier((sending, before))
        planes = [leave_along_a(plane, shift) for plane in sending]
        if index == len(own) - 1:
            for k, part in enumerate(planes):
                total = add_all(part)
                if early:
                    total, _ = lax.optimization_barrier((total, early))
                terms = terms + [shift(total, "b", -k - 1)]
            found = scatter_plane(terms, shift, sizes)
        else:
            found = scatter_plane(terms, shift, sizes)
            before = [v for part in planes for v in part[1:]]
            early = found[-1:]
            for k, part in enumerate(planes):
                total = add_all(scatter_plane(part, shift, sizes))
                found = found + [shift(total, "b", -k - 1)]
        sums.append(add_all(found))
    total = jnp.zeros((sum(v.shape[0] for v in sums), sums[0].shape[1]), sums[0].dtype)
    first = 0
    for value in sums:
        total = lax.dynamic_update_slice(total, value, (first, 0))
        first += value.shape[0]
    return total


def rope_tables(positions):
    half = HEAD // 2
    frequency = rope_base ** (-jnp.arange(half, dtype=jnp.float32) / half)
    angles = positions.astype(jnp.float32)[:, None] * frequency[None, :]
    cosine, sine = jnp.cos(angles), jnp.sin(angles)
    return (
        jnp.concatenate([cosine] * 4, axis=1),
        jnp.concatenate([-sine, sine, -sine, sine], axis=1),
    )


def shards(
    tokens,
    attn_gain,
    w_qkv,
    w_out,
    k_cache,
    v_cache,
    cache_len,
    ffn_gain,
    routes,
    route_scores,
    replica_slot,
    expert_up,
    expert_down,
):
    row_count, top_count = routes.shape
    chips, cores = lax.axis_size("req"), lax.axis_size("seq")
    seq_index = lax.axis_index("seq")
    length = cache_len[0]
    slots_dev = expert_up.shape[0]
    slot_total = chips * cores * slots_dev
    capacity = 2 * ((row_count * top_count + slot_total - 1) // slot_total)
    shift, sizes = make_shift(chips, cores)

    def swap(value):
        return lax.ppermute(value, "seq", [(0, 1), (1, 0)])

    other_tokens = swap(tokens)
    k_other, v_other = swap(k_cache), swap(v_cache)
    experts = jnp.arange(replica_slot.shape[1], dtype=jnp.int32)
    slot_of = jnp.sum(
        jnp.where(routes[:, :, None] == experts, replica_slot[:, None, :], 0), axis=2
    )
    shares = route_scores / jnp.sum(route_scores, axis=1, keepdims=True)
    coarse = lax.reduce_precision(shares, 8, 7)
    table = jnp.concatenate([slot_of.astype(jnp.float32), coarse, shares - coarse], axis=1)
    table = table.astype(jnp.bfloat16).T.reshape(-1, tokens.shape[1])
    table = jnp.pad(table, ((0, -table.shape[0] % 8), (0, 0)))
    chip = lax.axis_index("req")
    chip_slots = jnp.arange(slots_dev, dtype=jnp.int32)
    slot_ids = jnp.concatenate(
        [
            (chip * cores + seq_index) * slots_dev + chip_slots,
            (chip * cores + 1 - seq_index) * slots_dev + chip_slots,
        ]
    ).astype(jnp.int32)

    row_index = jnp.arange(row_count, dtype=jnp.int32)
    cosine, sine = rope_tables(
        length
        + jnp.concatenate(
            [seq_index * row_count + row_index, (1 - seq_index) * row_count + row_index]
        )
    )
    queries, appended, other_span = project(
        tokens, other_tokens, attn_gain, cosine, sine, w_qkv, [k_other, v_other]
    )
    later_up, later_down, _ = lax.optimization_barrier((expert_up, expert_down, appended))
    up_other, down_other = swap(later_up), swap(later_down)
    half = row_count // 2
    filled, lines = [], []
    for index in range(2):
        attended, stream, expert_in = attend(
            cache_len,
            queries,
            (k_cache, k_other, v_cache, v_other),
            (appended, other_span),
            w_out,
            tokens,
            ffn_gain,
            index * half,
            half,
            [] if index else [table],
            filled,
            [up_other, down_other] if index else [],
        )
        filled = [attended, stream]
        sent = expert_in
        if index:
            sent, _ = lax.optimization_barrier((sent, lines[0][1:]))
        lines.append(gather_line(sent, shift, sizes))
    first, second = lines
    planes = gather_planes(stack_rows(first, [expert_in]), shift, sizes, second[1:])
    stacked = stack_rows(second, [plane[0] for plane in planes[1:]])
    halves = [planes, gather_planes(stacked, shift, sizes, [])]
    cuts = (5 * row_count // 8, row_count - 5 * row_count // 8)
    own, others, held = [], [], None
    for index in range(sizes["b"]):
        pick, back, share = plan_routes(
            slot_ids, halves[0][index], half, row_count, capacity, top_count
        )
        held = run_experts(
            [[planes[index][j] for planes in halves] for j in range(sizes["a"])],
            pick,
            share,
            (expert_up, up_other),
            (expert_down, down_other),
            (half, row_count - half),
            [held] if index else [],
        )
        mixed = mix_rows(held, back, sizes["a"], cuts, [v for line in own[:1] for v in line[1:]])
        chunks = [[piece[i] for piece in mixed] for i in range(len(cuts))]
        if index == 0:
            chunks, _ = lax.optimization_barrier((chunks, halves[1][1:]))
            own = [leave_along_a(plane, shift) for plane in chunks]
        else:
            others.append(chunks)
    others = [[planes[i] for planes in others] for i in range(len(cuts))]
    own, _ = lax.optimization_barrier((own, others))
    expert_mix = scatter_chunks(own, others, shift, sizes)
    return (attended, stream, expert_mix, appended)


def solution(mesh):
    return jax.shard_map(
        shards,
        mesh=mesh,
        in_specs=(
            P(("req", "seq"), None),
            P(),
            P(),
            P(),
            P("req", "seq", None),
            P("req", "seq", None),
            P("req"),
            P(),
            P(("req", "seq"), None),
            P(("req", "seq"), None),
            P(("req", "seq"), None),
            P(("req", "seq"), None, None),
            P(("req", "seq"), None, None),
        ),
        out_specs=(
            P(("req", "seq"), None),
            P(("req", "seq"), None),
            P(("req", "seq"), None),
            P(("req", "seq"), None),
        ),
        check_vma=False,
    )
```
